32 devices in a mesh: cuts: 2 (over x), brick: 16 (over z, y, core).
Axes of the slice: x: 2, y: 2, z: 4, core: 2. Of those that a mesh axis runs over, the one named last changes fastest.
Arguments:
- eigen_vectors: float32 [64, 2, 3, 64, 512], P(None, None, None, ('cuts', 'brick')), parts along dimension 3, may hold values from -6 to 6
- link_field: float32 [3, 2, 3, 3, 64, 512], P(None, None, None, None, ('cuts', 'brick')), parts along dimension 4, may hold values from -3 to 3
- block_slot: int32 [63], replicated, may hold values from 0 to 63, as said below
Outputs:
- elementals: float32 [128, 32, 128], P(('cuts', 'brick')), parts along dimension 0
The draws below stay inside these ranges and needn't reach their ends.
There are 2 independent parts, one for each index of `cuts`. The reference program is written for one: setup_inputs(seed, part) draws one part's arguments, and reference() takes and returns one part's arrays. A program takes and returns all parts, laid end to end along the dimension named above; an argument that names none is the same for every part. Nothing has to cross between parts.
Inputs may be any that keep to these rules, and one draw needn't show every extreme that they name: block_slot names distinct slots; slot s belongs to device s // 4 of the brick axis; in every draw some device has all 4 of its slots named.
All inputs are finite; a program needn't handle non-finite values.
Results may differ from the reference program's by a relative error of at most 0.0044.
Values sent between devices are 32-bit elements; how exact they have to be, the bound alone decides.
No kernel may reach another device: no remote copies, remote signals or barrier semaphores. Data moves between devices by JAX's collectives and lax.ppermute only.
A program may use at most 64 MiB of HBM per device.

```python
import math
import jax
import jax.numpy as jnp
import numpy as np
from jax import lax

NV = 64
PB = 32
CAP = 4
LX = 8
LY = 64
LZ = 32
NBLK = 63
SLOTS = 64


def draw_block_slot(key, part):
    key_owner, key_score, key_order = jax.random.split(key, 3)
    slot_ids = jnp.arange(SLOTS, dtype=jnp.int32)
    full_owner = jax.random.randint(key_owner, (), 0, SLOTS // CAP)
    slot_score = jax.random.permutation(key_score, SLOTS).astype(jnp.int32)
    slot_score = jnp.where(slot_ids // CAP == full_owner, slot_ids % CAP - CAP, slot_score)
    slot_order = jnp.argsort(slot_score, stable=True)[:NBLK]
    return jax.random.permutation(key_order, slot_order).astype(jnp.int32)


def block_scale(own_key, shape, cuts, low, high):
    level, own = 1.0, jax.random.fold_in(own_key, 6)
    for axis_at, shards_of in cuts:
        draws = jnp.exp(jax.random.uniform(jax.random.fold_in(own, axis_at), (shards_of,), jnp.float32, low / len(cuts), high / len(cuts)))
        level = level * jnp.repeat(draws, shape[axis_at] // shards_of).reshape([-1 if axis == axis_at else 1 for axis in range(len(shape))])
    return level


def centred(rng, shape, spread, limit, cuts=(), kind=jnp.bfloat16):
    array = jax.random.normal(rng, shape, jnp.float32) * spread
    if len(cuts) > 0:
        array = block_scale(rng, shape, cuts, -0.22, 0.18) * array
    return jnp.clip(array, min=-limit, max=limit).astype(kind)


def setup_inputs(seed: int = 0, part: int = 0) -> dict:
    splits = jax.random.split(jax.random.key(seed), 4)
    own_keys = jax.random.split(jax.random.fold_in(splits[3], part), 4)
    eigen_vectors = centred(own_keys[0], (NV, 2, 3, LZ, LX * LY), 1.0, 6.0, ((3, 16),), jnp.float32)
    link_field = centred(own_keys[1], (3, 2, 3, 3, LZ, LX * LY), 0.5, 3.0, ((4, 16),), jnp.float32)
    block_slot = draw_block_slot(jax.random.fold_in(splits[3], 71), part)
    return dict(eigen_vectors=eigen_vectors, link_field=link_field, block_slot=block_slot)


def periodic(lattice_field, rim_depth, along):
    plane_count = lattice_field.shape[along]
    lower = lax.slice_in_dim(lattice_field, plane_count - rim_depth, plane_count, axis=along)
    upper = lax.slice_in_dim(lattice_field, 0, rim_depth, axis=along)
    return jnp.concatenate([lower, lattice_field, upper], axis=along)

def shift_columns(lattice_field, forward):
    column = jnp.arange(lattice_field.shape[-1]) % LX
    if forward:
        return jnp.where(column == LX - 1, jnp.roll(lattice_field, LX - 1, axis=-1), jnp.roll(lattice_field, -1, axis=-1))
    return jnp.where(column == 0, jnp.roll(lattice_field, -(LX - 1), axis=-1), jnp.roll(lattice_field, 1, axis=-1))

def link_times(link_set, lattice_field):
    real_rows = []
    imag_rows = []
    for out_row in range(3):
        real_part = link_set[0, out_row, 0] * lattice_field[:, 0, 0] - link_set[1, out_row, 0] * lattice_field[:, 1, 0]
        imag_part = link_set[0, out_row, 0] * lattice_field[:, 1, 0] + link_set[1, out_row, 0] * lattice_field[:, 0, 0]
        for in_row in (1, 2):
            real_part = real_part + link_set[0, out_row, in_row] * lattice_field[:, 0, in_row] - link_set[1, out_row, in_row] * lattice_field[:, 1, in_row]
            imag_part = imag_part + link_set[0, out_row, in_row] * lattice_field[:, 1, in_row] + link_set[1, out_row, in_row] * lattice_field[:, 0, in_row]
        real_rows.append(real_part)
        imag_rows.append(imag_part)
    return jnp.stack([jnp.stack(real_rows, 1), jnp.stack(imag_rows, 1)], 1)

def adjoint_times(link_set, lattice_field):
    real_rows = []
    imag_rows = []
    for out_row in range(3):
        real_part = link_set[0, 0, out_row] * lattice_field[:, 0, 0] + link_set[1, 0, out_row] * lattice_field[:, 1, 0]
        imag_part = link_set[0, 0, out_row] * lattice_field[:, 1, 0] - link_set[1, 0, out_row] * lattice_field[:, 0, 0]
        for in_row in (1, 2):
            real_part = real_part + link_set[0, in_row, out_row] * lattice_field[:, 0, in_row] + link_set[1, in_row, out_row] * lattice_field[:, 1, in_row]
            imag_part = imag_part + link_set[0, in_row, out_row] * lattice_field[:, 1, in_row] - link_set[1, in_row, out_row] * lattice_field[:, 0, in_row]
        real_rows.append(real_part)
        imag_rows.append(imag_part)
    return jnp.stack([jnp.stack(real_rows, 1), jnp.stack(imag_rows, 1)], 1)

def apply_hops(lattice_field, link_field):
    inner_field = lattice_field[:, :, :, 1:-1]
    inner_links = link_field[:, :, :, :, 1:-1]
    hop_total = link_times(inner_links[0], shift_columns(inner_field, True))
    hop_total = hop_total + shift_columns(adjoint_times(inner_links[0], inner_field), False)
    hop_total = hop_total + link_times(inner_links[1], jnp.roll(inner_field, -LX, axis=4))
    hop_total = hop_total + jnp.roll(adjoint_times(inner_links[1], inner_field), LX, axis=4)
    hop_total = hop_total + link_times(link_field[2][:, :, :, 1:-1], lattice_field[:, :, :, 2:])
    hop_total = hop_total + adjoint_times(link_field[2][:, :, :, :-2], lattice_field[:, :, :, :-2])
    return hop_total * (1.0 / 6.0)

def diquark_block(left_rows, right_rows):
    real_rows = []
    imag_rows = []
    for colour in range(3):
        first_colour = (colour + 1) % 3
        second_colour = (colour + 2) % 3
        real_part = left_rows[:, 0, first_colour] * right_rows[:, 0, second_colour] - left_rows[:, 1, first_colour] * right_rows[:, 1, second_colour] - (left_rows[:, 0, second_colour] * right_rows[:, 0, first_colour] - left_rows[:, 1, second_colour] * right_rows[:, 1, first_colour])
        imag_part = left_rows[:, 0, first_colour] * right_rows[:, 1, second_colour] + left_rows[:, 1, first_colour] * right_rows[:, 0, second_colour] - (left_rows[:, 0, second_colour] * right_rows[:, 1, first_colour] + left_rows[:, 1, second_colour] * right_rows[:, 0, first_colour])
        real_rows.append(real_part)
        imag_rows.append(imag_part)
    return jnp.stack([jnp.stack(real_rows, 1), jnp.stack(imag_rows, 1)], 1)

def elemental_block(quarks, vectors_low):
    pair_count = quarks.shape[0]
    vector_count = vectors_low.shape[0]
    left_mat = quarks.astype(jnp.float32).reshape(pair_count * 2, -1)
    right_mat = vectors_low.astype(jnp.float32).reshape(vector_count * 2, -1)
    products = lax.dot_general(left_mat, right_mat, (((1,), (1,)), ((), ())), precision=lax.Precision.HIGHEST, preferred_element_type=jnp.float32)
    products = products.reshape(pair_count, 2, vector_count, 2)
    real_part = products[:, 0, :, 0] - products[:, 1, :, 1]
    imag_part = products[:, 0, :, 1] + products[:, 1, :, 0]
    return jnp.stack([real_part, imag_part], 1).reshape(pair_count, 2 * vector_count)

def reference(eigen_vectors, link_field, block_slot):
    link_wide = periodic(link_field, 1, 4)
    first_step = apply_hops(periodic(eigen_vectors, 1, 3), link_wide)
    filtered = 2.0 * apply_hops(periodic(first_step, 1, 3), link_wide) - eigen_vectors
    vectors_low = filtered.astype(jnp.bfloat16)
    first_index, second_index = np.triu_indices(NV, 1)
    first_table = jnp.asarray(first_index.reshape(NBLK, PB).astype(np.int32))
    second_table = jnp.asarray(second_index.reshape(NBLK, PB).astype(np.int32))

    def one_block(pair_rows):
        quarks = diquark_block(jnp.take(filtered, pair_rows[0], axis=0), jnp.take(filtered, pair_rows[1], axis=0)).astype(jnp.bfloat16)
        return elemental_block(quarks, vectors_low)
    blocks = lax.map(one_block, (first_table, second_table))
    factor = 1.0 / math.sqrt(3.0 * LX * LY * LZ)
    elemental = blocks * factor
    return jnp.zeros((SLOTS, PB, 2 * NV), jnp.float32).at[block_slot].set(elemental)
```

```python
import functools
import math

import jax
import jax.numpy as jnp
import numpy as np
from jax import lax
from jax.experimental import pallas as pl
from jax.experimental.pallas import tpu as pltpu
from jax.sharding import PartitionSpec as P

PB = 32
CAP = 4
LX = 8
LANES = 128
ROWS = 8
VMEM = pl.BlockSpec(memory_space=pltpu.VMEM)
SMEM = pl.BlockSpec(memory_space=pltpu.SMEM)


def params(limit_mib):
    return pltpu.CompilerParams(vmem_limit_bytes=limit_mib * 1024 * 1024)


def cost(flops, bytes_accessed):
    return pl.CostEstimate(
        flops=int(flops), bytes_accessed=int(bytes_accessed), transcendentals=0
    )


def tile_rows(array):
    planes, sites = array.shape[-2:]
    tiles = sites // LANES
    lead = math.prod(array.shape[:-2])
    array = array.reshape(lead, planes, tiles, LANES).transpose(0, 2, 1, 3)
    return array.reshape(lead * tiles * planes, LANES)


def times(link, field, total):
    total = list(total)
    for out_row in range(3):
        for in_row in range(3):
            real, imag = link(0, out_row, in_row), link(1, out_row, in_row)
            f_real, f_imag = field[in_row], field[3 + in_row]
            total[out_row] = total[out_row] + real * f_real - imag * f_imag
            total[3 + out_row] = total[3 + out_row] + real * f_imag + imag * f_real
    return total


def adjoint(link, field, total):
    total = list(total)
    for out_row in range(3):
        for in_row in range(3):
            real, imag = link(0, in_row, out_row), link(1, in_row, out_row)
            f_real, f_imag = field[in_row], field[3 + in_row]
            total[out_row] = total[out_row] + real * f_real + imag * f_imag
            total[3 + out_row] = total[3 + out_row] + real * f_imag - imag * f_real
    return total


def split_kernel(tiles, per_chunk, x_ref, *out_refs):
    vectors = out_refs[0].shape[1]
    chunks = tiles // per_chunk
    for part in range(6):
        for tile in range(tiles):
            for plane in range(2):
                rows = pl.ds((part * tiles + tile) * 2 + plane, vectors, stride=6 * tiles * 2)
                at = (tile % per_chunk) * LANES
                out_refs[plane * chunks + tile // per_chunk][part, :, at : at + LANES] = x_ref[
                    rows, :
                ]


def local_kernel(tiles, per_chunk, link_ref, *refs):
    chunks = tiles // per_chunk
    fields, totals = refs[: 2 * chunks], refs[2 * chunks :]
    vectors = fields[0].shape[1]
    lane = lax.broadcasted_iota(jnp.int32, (ROWS, LANES), 1)
    column = lane % LX
    first_column, last_column = column == 0, column == LX - 1
    below, above = lane < LX, lane >= LANES - LX
    zeros = [jnp.zeros((ROWS, LANES), jnp.float32)] * 6

    def step(group, carry):
        rows = pl.ds(pl.multiple_of(group * ROWS, ROWS), ROWS)

        def get(plane, tile):
            at = (tile % per_chunk) * LANES
            ref = fields[plane * chunks + tile // per_chunk]
            return [ref[part, rows, at : at + LANES] for part in range(6)]

        def link_of(direction, plane, tile):
            def link(part, row, column_at):
                index = ((direction * 2 + part) * 3 + row) * 3 + column_at
                index = (index * tiles + tile) * 2 + plane
                return link_ref[index : index + 1, :]

            return link

        for plane in range(2):
            sums = []
            rolled_in = []
            rolled_out = []
            for tile in range(tiles):
                field = get(plane, tile)
                ahead = [
                    jnp.where(
                        last_column, pltpu.roll(f, LX - 1, 1), pltpu.roll(f, LANES - 1, 1)
                    )
                    for f in field
                ]
                behind = adjoint(link_of(0, plane, tile), field, zeros)
                total = [
                    jnp.where(
                        first_column, pltpu.roll(f, LANES - LX + 1, 1), pltpu.roll(f, 1, 1)
                    )
                    for f in behind
                ]
                total = times(link_of(0, plane, tile), ahead, total)
                if plane == 0:
                    total = times(link_of(2, 0, tile), get(1, tile), total)
                else:
                    total = adjoint(link_of(2, 0, tile), get(0, tile), total)
                sums.append(total)
                rolled_in.append([pltpu.roll(f, LANES - LX, 1) for f in field])
                rolled_out.append(
                    [
                        pltpu.roll(f, LX, 1)
                        for f in adjoint(link_of(1, plane, tile), field, zeros)
                    ]
                )
            for tile in range(tiles):
                after, before = (tile + 1) % tiles, (tile - 1) % tiles
                ahead = [
                    jnp.where(above, b, a) for a, b in zip(rolled_in[tile], rolled_in[after])
                ]
                total = times(link_of(1, plane, tile), ahead, sums[tile])
                at = (tile % per_chunk) * LANES
                out = totals[plane * chunks + tile // per_chunk]
                for part in range(6):
                    back = jnp.where(below, rolled_out[before][part], rolled_out[tile][part])
                    out[part, rows, at : at + LANES] = total[part] + back
        return carry

    lax.fori_loop(0, vectors // ROWS, step, 0)


def outer_hops(tiles, first_tile, link_ref, low_ref, lower, upper, part_sums, rows, at, tile):
    def up(part, row, column_at):
        index = ((2 * 2 + part) * 3 + row) * 3 + column_at
        index = (index * tiles + first_tile + tile) * 2 + 1
        return link_ref[index : index + 1, :]

    def down(part, row, column_at):
        index = (part * 3 + row) * 3 + column_at
        index = index * tiles + first_tile + tile
        return low_ref[index : index + 1, :]

    def get(ref):
        return [ref[part, rows, at : at + LANES] for part in range(6)]

    return (
        adjoint(down, get(lower), get(part_sums[0])),
        times(up, get(upper), get(part_sums[1])),
    )


def edge_kernel(
    tiles, first_tile, link_ref, low_ref, lower, upper, sum_0, sum_1, out_0, out_1
):
    vectors, width = lower.shape[1:]

    def step(group, carry):
        rows = pl.ds(pl.multiple_of(group * ROWS, ROWS), ROWS)
        for tile in range(width // LANES):
            at = tile * LANES
            found = outer_hops(
                tiles, first_tile, link_ref, low_ref, lower, upper, (sum_0, sum_1), rows, at, tile
            )
            for plane, out in enumerate((out_0, out_1)):
                for part in range(6):
                    out[part, rows, at : at + LANES] = found[plane][part] * (1.0 / 6.0)
        return carry

    lax.fori_loop(0, vectors // ROWS, step, 0)


def pair_tiles(vectors):
    groups = vectors // ROWS
    return [(left, right) for right in range(groups) for left in range(right + 1)]


def chunk_sums(
    tiles, first_tile, link_ref, low_ref, lower, upper, sum_0, sum_1, own_0, own_1, field, low,
    quarks, store,
):
    vectors, width = lower.shape[1:]

    def filter_step(group, carry):
        rows = pl.ds(pl.multiple_of(group * ROWS, ROWS), ROWS)
        for tile in range(width // LANES):
            at = tile * LANES
            found = outer_hops(
                tiles, first_tile, link_ref, low_ref, lower, upper, (sum_0, sum_1), rows, at, tile
            )
            for plane, own in enumerate((own_0, own_1)):
                for part in range(6):
                    field[plane * 6 + part, rows, at : at + LANES] = (
                        found[plane][part] * (2.0 / 6.0) - own[part, rows, at : at + LANES]
                    )
        return carry

    lax.fori_loop(0, vectors // ROWS, filter_step, 0)

    for plane in range(2):
        for colour in range(3):
            real = field[plane * 6 + colour].astype(jnp.bfloat16)
            imag = field[plane * 6 + 3 + colour].astype(jnp.bfloat16)
            for part, (top, bottom) in enumerate(((real, imag), (-imag, real))):
                at = (part * 3 + colour) * width
                low[plane, :vectors, at : at + width] = top
                low[plane, vectors:, at : at + width] = bottom

    combos = pair_tiles(vectors)
    groups = vectors // ROWS
    block = ROWS * ROWS

    def plane_step(plane, carry):
        for right in range(groups):
            base = right * (right + 1) // 2

            def left_step(left, inner):
                start = pl.multiple_of((base + left) * block, block)
                for tile in range(width // LANES):
                    at = tile * LANES

                    def load(part, rows):
                        return field[plane * 6 + part, rows, at : at + LANES]

                    right_rows = pl.ds(right * ROWS, ROWS)
                    left_rows = pl.ds(pl.multiple_of(left * ROWS, ROWS), ROWS)
                    b = [load(part, right_rows) for part in range(6)]
                    group = [
                        field.at[plane * 6 + part, left_rows, at : at + LANES]
                        for part in range(6)
                    ]
                    made = [[] for _ in range(6)]
                    for row in range(ROWS):
                        a = [ref[row : row + 1, :] for ref in group]
                        for colour in range(3):
                            x, y = (colour + 1) % 3, (colour + 2) % 3
                            real = (a[x] * b[y] - a[3 + x] * b[3 + y]) - (
                                a[y] * b[x] - a[3 + y] * b[3 + x]
                            )
                            imag = (a[x] * b[3 + y] + a[3 + x] * b[y]) - (
                                a[y] * b[3 + x] + a[3 + y] * b[x]
                            )
                            made[colour].append(real)
                            made[3 + colour].append(imag)
                    for part in range(6):
                        quarks[pl.ds(start, block), part * width + at : part * width + at + LANES] = (
                            jnp.concatenate(made[part], 0).astype(jnp.bfloat16)
                        )
                return inner

            lax.fori_loop(0, right + 1, left_step, 0)
        store(
            plane,
            lax.dot_general(
                quarks[...],
                low[plane],
                (((1,), (1,)), ((), ())),
                preferred_element_type=jnp.float32,
            ),
        )
        return carry

    lax.fori_loop(0, 2, plane_step, 0)


def first_chunk_kernel(tiles, link_ref, low_ref, *refs):
    ins, out, scratch = refs[:6], refs[6], refs[7:]

    def store(plane, value):
        @pl.when(plane == 0)
        def _():
            out[...] = value

        @pl.when(plane > 0)
        def _():
            out[...] += value

    chunk_sums(tiles, 0, link_ref, low_ref, *ins, *scratch, store)


def last_chunk_kernel(
    tiles, first_tile, factor, place_ref, slot_ref, link_ref, low_ref, *refs
):
    ins, before, keep, send, sums, scratch = (
        refs[:6], refs[6], refs[7], refs[8], refs[9], refs[10:-1],
    )
    ordered = refs[-1]

    def store(plane, value):
        @pl.when(plane == 0)
        def _():
            sums[...] = before[...] + value

        @pl.when(plane > 0)
        def _():
            sums[...] += value

    chunk_sums(tiles, first_tile, link_ref, low_ref, *ins, *scratch, store)
    vectors = ins[0].shape[1]
    for number, (left, right) in enumerate(pair_tiles(vectors)):
        for row in range(ROWS):
            first = left * ROWS + row
            skip = max(0, first + 1 - right * ROWS)
            if skip >= ROWS:
                continue
            second = right * ROWS + skip
            pair = first * vectors - first * (first + 1) // 2 + second - first - 1
            at = (number * ROWS + row) * ROWS
            ordered[pair : pair + ROWS - skip, :] = sums[at + skip : at + ROWS, :] * factor
    keep[...] = jnp.zeros_like(keep)
    send[...] = jnp.zeros_like(send)
    chips = keep.shape[0]
    my_chip, my_core = place_ref[0], place_ref[1]

    def place(block, carry):
        slot = slot_ref[block]
        owner = slot // CAP
        away = lax.rem(owner // 2 - my_chip + chips, chips)
        value = ordered[pl.ds(pl.multiple_of(block * PB, PB), PB), :]

        @pl.when(owner % 2 == my_core)
        def _():
            keep[away, slot % CAP] = value

        @pl.when(owner % 2 != my_core)
        def _():
            send[away, slot % CAP] = value

        return carry

    lax.fori_loop(0, slot_ref.shape[0], place, 0)


def combine_kernel(keep, received, *outs):
    for away, out in enumerate(outs):
        out[...] = keep[away] + received[away]


def total_kernel(*refs):
    total = refs[0][...]
    for ref in refs[1:-1]:
        total = total + ref[...]
    refs[-1][...] = total


def on_device(eigen_vectors, link_field, block_slot):
    count = lax.axis_size("brick")
    vectors, _, _, planes, sites = eigen_vectors.shape
    tiles = sites // LANES
    chunks = 2
    per_chunk = tiles // chunks
    width = per_chunk * LANES
    piece = jax.ShapeDtypeStruct((6, vectors, width), jnp.float32)
    piece_bytes = 6 * vectors * width * 4
    pair_rows = len(pair_tiles(vectors)) * ROWS * ROWS
    upward = [(i, (i + 1) % count) for i in range(count)]
    downward = [((i + 1) % count, i) for i in range(count)]

    links = tile_rows(link_field)
    low_links = lax.ppermute(link_field[2, :, :, :, planes - 1], "brick", upward)
    low_links = low_links.reshape(18 * tiles, LANES)

    own = pl.pallas_call(
        functools.partial(split_kernel, tiles, per_chunk),
        out_shape=[piece] * (2 * chunks),
        in_specs=[VMEM],
        out_specs=[VMEM] * (2 * chunks),
        compiler_params=params(32),
        name="split",
    )(tile_rows(eigen_vectors))

    def exchange(fields):
        lower = [lax.ppermute(fields[chunks + c], "brick", upward) for c in range(chunks)]
        upper = [lax.ppermute(fields[c], "brick", downward) for c in range(chunks)]
        return lower, upper

    def local_hops(fields):
        return pl.pallas_call(
            functools.partial(local_kernel, tiles, per_chunk),
            out_shape=[piece] * (2 * chunks),
            in_specs=[VMEM] * (1 + 2 * chunks),
            out_specs=[VMEM] * (2 * chunks),
            compiler_params=params(48),
            cost_estimate=cost(5e9, 4 * chunks * piece_bytes),
            name="local",
        )(links, *fields)

    lower, upper = exchange(own)
    sums = local_hops(own)
    first = [None] * (2 * chunks)
    for c in range(chunks):
        first[c], first[chunks + c] = pl.pallas_call(
            functools.partial(edge_kernel, tiles, c * per_chunk),
            out_shape=[piece] * 2,
            in_specs=[VMEM] * 6,
            out_specs=[VMEM] * 2,
            compiler_params=params(32),
            name="edge",
        )(links, low_links, lower[c], upper[c], sums[c], sums[chunks + c])

    lower, upper = exchange(first)
    sums = local_hops(first)
    scratch = [
        pltpu.VMEM((12, vectors, width), jnp.float32),
        pltpu.VMEM((2, 2 * vectors, 6 * width), jnp.bfloat16),
        pltpu.VMEM((pair_rows, 6 * width), jnp.bfloat16),
    ]
    partial_sums = jax.ShapeDtypeStruct((pair_rows, 2 * vectors), jnp.float32)
    before = pl.pallas_call(
        functools.partial(first_chunk_kernel, tiles),
        out_shape=partial_sums,
        in_specs=[VMEM] * 8,
        out_specs=VMEM,
        scratch_shapes=scratch,
        compiler_params=params(48),
        cost_estimate=cost(8e9, 6 * piece_bytes),
        name="pairs",
    )(links, low_links, lower[0], upper[0], sums[0], sums[chunks], own[0], own[chunks])
    factor = 1.0 / math.sqrt(3.0 * sites * planes * count)
    me = lax.axis_index("brick")
    chips = count // 2
    place = jnp.stack([me // 2, me % 2]).astype(jnp.int32)
    half = jax.ShapeDtypeStruct((chips, CAP, PB, 2 * vectors), jnp.float32)
    blocks = vectors * (vectors - 1) // 2
    c = chunks - 1
    keep, send = pl.pallas_call(
        functools.partial(last_chunk_kernel, tiles, c * per_chunk, factor),
        out_shape=[half] * 2,
        in_specs=[SMEM] * 2 + [VMEM] * 9,
        out_specs=[VMEM] * 2,
        scratch_shapes=[pltpu.VMEM((pair_rows, 2 * vectors), jnp.float32)]
        + scratch
        + [pltpu.VMEM((blocks, 2 * vectors), jnp.float32)],
        compiler_params=params(48),
        cost_estimate=cost(8e9, 6 * piece_bytes),
        name="last_pairs",
    )(
        place, block_slot, links, low_links, lower[c], upper[c], sums[c], sums[chunks + c],
        own[c], own[chunks + c], before,
    )
    received = lax.ppermute(send, "brick", [(i, i ^ 1) for i in range(count)])
    share = jax.ShapeDtypeStruct((CAP, PB, 2 * vectors), jnp.float32)
    shares = pl.pallas_call(
        combine_kernel,
        out_shape=[share] * chips,
        in_specs=[VMEM] * 2,
        out_specs=[VMEM] * chips,
        compiler_params=params(32),
        name="combine",
    )(keep, received)
    arrived = [shares[0]] + [
        lax.ppermute(
            shares[away],
            "brick",
            [(i, ((i // 2 + away) % chips) * 2 + i % 2) for i in range(count)],
        )
        for away in range(1, chips)
    ]
    return pl.pallas_call(
        total_kernel,
        out_shape=share,
        in_specs=[VMEM] * chips,
        out_specs=VMEM,
        compiler_params=params(32),
        name="total",
    )(*arrived)


def solution(mesh):
    return jax.shard_map(
        on_device,
        mesh=mesh,
        in_specs=(
            P(None, None, None, ("cuts", "brick"), None),
            P(None, None, None, None, ("cuts", "brick"), None),
            P(),
        ),
        out_specs=P(("cuts", "brick"), None, None),
        check_vma=False,
    )
```

```python
import functools
import math

import jax
import jax.numpy as jnp
import numpy as np
from jax import lax
from jax.experimental import pallas as pl
from jax.experimental.pallas import tpu as pltpu
from jax.sharding import PartitionSpec as P

PB = 32
CAP = 4
LX = 8
LANES = 128
ROWS = 8
VMEM = pl.BlockSpec(memory_space=pltpu.VMEM)
SMEM = pl.BlockSpec(memory_space=pltpu.SMEM)


def params(limit_mib):
    return pltpu.CompilerParams(vmem_limit_bytes=limit_mib * 1024 * 1024)


def cost(flops, bytes_accessed):
    return pl.CostEstimate(
        flops=int(flops), bytes_accessed=int(bytes_accessed), transcendentals=0
    )


def tile_rows(array):
    planes, sites = array.shape[-2:]
    tiles = sites // LANES
    lead = math.prod(array.shape[:-2])
    array = array.reshape(lead, planes, tiles, LANES).transpose(0, 2, 1, 3)
    return array.reshape(lead * tiles * planes, LANES)


def times(link, field, total):
    total = list(total)
    for out_row in range(3):
        for in_row in range(3):
            real, imag = link(0, out_row, in_row), link(1, out_row, in_row)
            f_real, f_imag = field[in_row], field[3 + in_row]
            total[out_row] = total[out_row] + real * f_real - imag * f_imag
            total[3 + out_row] = total[3 + out_row] + real * f_imag + imag * f_real
    return total


def adjoint(link, field, total):
    total = list(total)
    for out_row in range(3):
        for in_row in range(3):
            real, imag = link(0, in_row, out_row), link(1, in_row, out_row)
            f_real, f_imag = field[in_row], field[3 + in_row]
            total[out_row] = total[out_row] + real * f_real + imag * f_imag
            total[3 + out_row] = total[3 + out_row] + real * f_imag - imag * f_real
    return total


def split_kernel(tiles, per_chunk, x_ref, *out_refs):
    vectors = out_refs[0].shape[1]
    chunks = tiles // per_chunk
    for part in range(6):
        for tile in range(tiles):
            for plane in range(2):
                rows = pl.ds((part * tiles + tile) * 2 + plane, vectors, stride=6 * tiles * 2)
                at = (tile % per_chunk) * LANES
                out_refs[plane * chunks + tile // per_chunk][part, :, at : at + LANES] = x_ref[
                    rows, :
                ]


def local_kernel(tiles, per_chunk, link_ref, *refs):
    chunks = tiles // per_chunk
    fields, totals = refs[: 2 * chunks], refs[2 * chunks :]
    vectors = fields[0].shape[1]
    lane = lax.broadcasted_iota(jnp.int32, (ROWS, LANES), 1)
    column = lane % LX
    first_column, last_column = column == 0, column == LX - 1
    below, above = lane < LX, lane >= LANES - LX
    zeros = [jnp.zeros((ROWS, LANES), jnp.float32)] * 6

    def step(group, carry):
        rows = pl.ds(pl.multiple_of(group * ROWS, ROWS), ROWS)

        def get(plane, tile):
            at = (tile % per_chunk) * LANES
            ref = fields[plane * chunks + tile // per_chunk]
            return [ref[part, rows, at : at + LANES] for part in range(6)]

        def link_of(direction, plane, tile):
            def link(part, row, column_at):
                index = ((direction * 2 + part) * 3 + row) * 3 + column_at
                index = (index * tiles + tile) * 2 + plane
                return link_ref[index : index + 1, :]

            return link

        for plane in range(2):
            sums = []
            rolled_in = []
            rolled_out = []
            for tile in range(tiles):
                field = get(plane, tile)
                ahead = [
                    jnp.where(
                        last_column, pltpu.roll(f, LX - 1, 1), pltpu.roll(f, LANES - 1, 1)
                    )
                    for f in field
                ]
                behind = adjoint(link_of(0, plane, tile), field, zeros)
                total = [
                    jnp.where(
                        first_column, pltpu.roll(f, LANES - LX + 1, 1), pltpu.roll(f, 1, 1)
                    )
                    for f in behind
                ]
                total = times(link_of(0, plane, tile), ahead, total)
                if plane == 0:
                    total = times(link_of(2, 0, tile), get(1, tile), total)
                else:
                    total = adjoint(link_of(2, 0, tile), get(0, tile), total)
                sums.append(total)
                rolled_in.append([pltpu.roll(f, LANES - LX, 1) for f in field])
                rolled_out.append(
                    [
                        pltpu.roll(f, LX, 1)
                        for f in adjoint(link_of(1, plane, tile), field, zeros)
                    ]
                )
            for tile in range(tiles):
                after, before = (tile + 1) % tiles, (tile - 1) % tiles
                ahead = [
                    jnp.where(above, b, a) for a, b in zip(rolled_in[tile], rolled_in[after])
                ]
                total = times(link_of(1, plane, tile), ahead, sums[tile])
                at = (tile % per_chunk) * LANES
                out = totals[plane * chunks + tile // per_chunk]
                for part in range(6):
                    back = jnp.where(below, rolled_out[before][part], rolled_out[tile][part])
                    out[part, rows, at : at + LANES] = total[part] + back
        return carry

    lax.fori_loop(0, vectors // ROWS, step, 0)


def outer_hops(tiles, first_tile, link_ref, low_ref, lower, upper, part_sums, rows, at, tile):
    def up(part, row, column_at):
        index = ((2 * 2 + part) * 3 + row) * 3 + column_at
        index = (index * tiles + first_tile + tile) * 2 + 1
        return link_ref[index : index + 1, :]

    def down(part, row, column_at):
        index = (part * 3 + row) * 3 + column_at
        index = index * tiles + first_tile + tile
        return low_ref[index : index + 1, :]

    def get(ref):
        return [ref[part, rows, at : at + LANES] for part in range(6)]

    return (
        adjoint(down, get(lower), get(part_sums[0])),
        times(up, get(upper), get(part_sums[1])),
    )


def edge_kernel(
    tiles, first_tile, link_ref, low_ref, lower, upper, sum_0, sum_1, out_0, out_1
):
    vectors, width = lower.shape[1:]

    def step(group, carry):
        rows = pl.ds(pl.multiple_of(group * ROWS, ROWS), ROWS)
        for tile in range(width // LANES):
            at = tile * LANES
            found = outer_hops(
                tiles, first_tile, link_ref, low_ref, lower, upper, (sum_0, sum_1), rows, at, tile
            )
            for plane, out in enumerate((out_0, out_1)):
                for part in range(6):
                    out[part, rows, at : at + LANES] = found[plane][part] * (1.0 / 6.0)
        return carry

    lax.fori_loop(0, vectors // ROWS, step, 0)


def pair_tiles(vectors):
    half = vectors // ROWS // 2
    return [
        (base + left, base + right)
        for base in (0, half)
        for right in range(half)
        for left in range(right + 1)
    ]


def chunk_sums(
    tiles, first_tile, link_ref, low_ref, lower, upper, sum_0, sum_1, own_0, own_1, field, low,
    quarks, store,
):
    vectors, width = lower.shape[1:]

    def filter_step(group, carry):
        rows = pl.ds(pl.multiple_of(group * ROWS, ROWS), ROWS)
        for tile in range(width // LANES):
            at = tile * LANES
            found = outer_hops(
                tiles, first_tile, link_ref, low_ref, lower, upper, (sum_0, sum_1), rows, at, tile
            )
            for plane, own in enumerate((own_0, own_1)):
                for part in range(6):
                    field[plane * 6 + part, rows, at : at + LANES] = (
                        found[plane][part] * (2.0 / 6.0) - own[part, rows, at : at + LANES]
                    )
        return carry

    lax.fori_loop(0, vectors // ROWS, filter_step, 0)

    for plane in range(2):
        for colour in range(3):
            real = field[plane * 6 + colour].astype(jnp.bfloat16)
            imag = field[plane * 6 + 3 + colour].astype(jnp.bfloat16)
            for part, (top, bottom) in enumerate(((real, imag), (-imag, real))):
                at = (part * 3 + colour) * width
                low[plane, :vectors, at : at + width] = top
                low[plane, vectors:, at : at + width] = bottom

    combos = pair_tiles(vectors)
    block = ROWS * ROWS
    steps = 4
    step_combos = len(combos) // steps
    step_rows = step_combos * block

    def form(plane, number):
        left, right = combos[number]
        for tile in range(width // LANES):
            at = tile * LANES
            lanes = slice(at, at + LANES)
            b = [
                field[plane * 6 + part, right * ROWS : (right + 1) * ROWS, lanes]
                for part in range(6)
            ]
            for row in range(0, ROWS, 2):
                made = [[] for _ in range(6)]
                for index in (left * ROWS + row, left * ROWS + row + 1):
                    a = [field[plane * 6 + part, index : index + 1, lanes] for part in range(6)]
                    for colour in range(3):
                        x, y = (colour + 1) % 3, (colour + 2) % 3
                        made[colour].append(
                            (a[x] * b[y] - a[3 + x] * b[3 + y])
                            - (a[y] * b[x] - a[3 + y] * b[3 + x])
                        )
                        made[3 + colour].append(
                            (a[x] * b[3 + y] + a[3 + x] * b[y])
                            - (a[y] * b[3 + x] + a[3 + y] * b[x])
                        )
                start = number * block + row * ROWS
                for part in range(6):
                    quarks[
                        start : start + 2 * ROWS, part * width + at : part * width + at + LANES
                    ] = jnp.concatenate(made[part], 0).astype(jnp.bfloat16)

    def plane_step(plane, carry):
        def form_step(step):
            for number in range(step * step_combos, (step + 1) * step_combos):
                form(plane, number)

        form_step(0)
        for step in range(steps):
            if step + 1 < steps:
                form_step(step + 1)
            rows = slice(step * step_rows, (step + 1) * step_rows)
            store(
                plane,
                rows,
                lax.dot_general(
                    quarks[rows, :],
                    low[plane],
                    (((1,), (1,)), ((), ())),
                    preferred_element_type=jnp.float32,
                ),
            )
        return carry

    lax.fori_loop(0, 2, plane_step, 0)


def first_chunk_kernel(tiles, link_ref, low_ref, *refs):
    ins, out, scratch = refs[:6], refs[6], refs[7:]
    out[...] = jnp.zeros_like(out)

    def store(plane, rows, value):
        out[rows, :] += value

    chunk_sums(tiles, 0, link_ref, low_ref, *ins, *scratch, store)


def arrange(sums, grid, crossed, ordered, factor):
    half = grid.shape[0] // 2
    side = math.isqrt(half)
    vectors = 2 * side
    block = ROWS * ROWS
    for number, (left, right) in enumerate(pair_tiles(vectors)):
        for row in range(ROWS):
            start = number * block + row * ROWS
            at = (left * ROWS + row) * side + right * ROWS % side
            grid[at : at + ROWS, :] = sums[start : start + ROWS, :] * factor
            if left != right:
                at = (right * ROWS + row) * side + left * ROWS % side
                grid[at : at + ROWS, :] = (
                    sums[pl.ds(number * block + row, ROWS, stride=ROWS), :] * -factor
                )
    lane = lax.broadcasted_iota(jnp.int32, (side, 2 * vectors), 1)
    own_half = lane % vectors < side
    per = 2 * vectors // side
    for start in range(0, half, 2 * vectors):
        turned = grid[half + start : half + start + 2 * vectors, :].T
        real, imag = turned[:side], turned[vectors : vectors + side]
        for index in range(per):
            second = start // side + index
            turn = (side - index * side) % (2 * vectors)
            value = jnp.where(
                lane < vectors,
                pltpu.roll(real, turn, 1) if turn else real,
                pltpu.roll(imag, (turn + vectors) % (2 * vectors), 1)
                if (turn + vectors) % (2 * vectors)
                else imag,
            )
            crossed[pl.ds(second, side, stride=side), :] = value
    for start in range(0, half, 2 * vectors):
        turned = grid[start : start + 2 * vectors, :].T
        real, imag = turned[side:vectors], turned[vectors + side :]
        for index in range(per):
            first = start // side + index
            turn = (-index * side) % (2 * vectors)
            value = jnp.where(
                lane < vectors,
                pltpu.roll(real, turn, 1) if turn else real,
                pltpu.roll(imag, (turn + vectors) % (2 * vectors), 1)
                if (turn + vectors) % (2 * vectors)
                else imag,
            )
            value = jnp.where(own_half, -value, crossed[first * side : (first + 1) * side, :])
            pair = first * vectors - first * (first + 1) // 2 + side - first - 1
            ordered[pair : pair + side, :] = value
    for first in range(vectors):
        skip = first % side + 1
        if skip < side:
            pair = first * vectors - first * (first + 1) // 2
            ordered[pair : pair + side - skip, :] = grid[
                first * side + skip : (first + 1) * side, :
            ]


def last_chunk_kernel(
    tiles, first_tile, factor, place_ref, slot_ref, link_ref, low_ref, *refs
):
    ins, before, keep, send, sums, scratch = (
        refs[:6], refs[6], refs[7], refs[8], refs[9], refs[10:-3],
    )
    grid, crossed, ordered = refs[-3:]
    sums[...] = before[...]

    def store(plane, rows, value):
        sums[rows, :] += value

    chunk_sums(tiles, first_tile, link_ref, low_ref, *ins, *scratch, store)
    arrange(sums, grid, crossed, ordered, factor)
    keep[...] = jnp.zeros_like(keep)
    send[...] = jnp.zeros_like(send)
    chips = keep.shape[0]
    my_chip, my_core = place_ref[0], place_ref[1]

    def place(block, carry):
        slot = slot_ref[block]
        owner = slot // CAP
        away = lax.rem(owner // 2 - my_chip + chips, chips)
        value = ordered[pl.ds(pl.multiple_of(block * PB, PB), PB), :]

        @pl.when(owner % 2 == my_core)
        def _():
            keep[away, slot % CAP] = value

        @pl.when(owner % 2 != my_core)
        def _():
            send[away, slot % CAP] = value

        return carry

    lax.fori_loop(0, slot_ref.shape[0], place, 0)


def combine_kernel(keep, received, *outs):
    for away, out in enumerate(outs):
        out[...] = keep[away] + received[away]


def total_kernel(*refs):
    total = refs[0][...]
    for ref in refs[1:-1]:
        total = total + ref[...]
    refs[-1][...] = total


def on_device(eigen_vectors, link_field, block_slot):
    count = lax.axis_size("brick")
    vectors, _, _, planes, sites = eigen_vectors.shape
    tiles = sites // LANES
    chunks = 2
    per_chunk = tiles // chunks
    width = per_chunk * LANES
    piece = jax.ShapeDtypeStruct((6, vectors, width), jnp.float32)
    piece_bytes = 6 * vectors * width * 4
    pair_rows = len(pair_tiles(vectors)) * ROWS * ROWS
    upward = [(i, (i + 1) % count) for i in range(count)]
    downward = [((i + 1) % count, i) for i in range(count)]

    links = tile_rows(link_field)
    low_links = lax.ppermute(link_field[2, :, :, :, planes - 1], "brick", upward)
    low_links = low_links.reshape(18 * tiles, LANES)

    own = pl.pallas_call(
        functools.partial(split_kernel, tiles, per_chunk),
        out_shape=[piece] * (2 * chunks),
        in_specs=[VMEM],
        out_specs=[VMEM] * (2 * chunks),
        compiler_params=params(32),
        name="split",
    )(tile_rows(eigen_vectors))

    def exchange(fields):
        lower = [lax.ppermute(fields[chunks + c], "brick", upward) for c in range(chunks)]
        upper = [lax.ppermute(fields[c], "brick", downward) for c in range(chunks)]
        return lower, upper

    def local_hops(fields):
        return pl.pallas_call(
            functools.partial(local_kernel, tiles, per_chunk),
            out_shape=[piece] * (2 * chunks),
            in_specs=[VMEM] * (1 + 2 * chunks),
            out_specs=[VMEM] * (2 * chunks),
            compiler_params=params(48),
            cost_estimate=cost(5e9, 4 * chunks * piece_bytes),
            name="local",
        )(links, *fields)

    lower, upper = exchange(own)
    sums = local_hops(own)
    first = [None] * (2 * chunks)
    for c in range(chunks):
        first[c], first[chunks + c] = pl.pallas_call(
            functools.partial(edge_kernel, tiles, c * per_chunk),
            out_shape=[piece] * 2,
            in_specs=[VMEM] * 6,
            out_specs=[VMEM] * 2,
            compiler_params=params(32),
            name="edge",
        )(links, low_links, lower[c], upper[c], sums[c], sums[chunks + c])

    lower, upper = exchange(first)
    sums = local_hops(first)
    scratch = [
        pltpu.VMEM((12, vectors, width), jnp.float32),
        pltpu.VMEM((2, 2 * vectors, 6 * width), jnp.bfloat16),
        pltpu.VMEM((pair_rows, 6 * width), jnp.bfloat16),
    ]
    partial_sums = jax.ShapeDtypeStruct((pair_rows, 2 * vectors), jnp.float32)
    before = pl.pallas_call(
        functools.partial(first_chunk_kernel, tiles),
        out_shape=partial_sums,
        in_specs=[VMEM] * 8,
        out_specs=VMEM,
        scratch_shapes=scratch,
        compiler_params=params(48),
        cost_estimate=cost(8e9, 6 * piece_bytes),
        name="pairs",
    )(links, low_links, lower[0], upper[0], sums[0], sums[chunks], own[0], own[chunks])
    factor = 1.0 / math.sqrt(3.0 * sites * planes * count)
    me = lax.axis_index("brick")
    chips = count // 2
    place = jnp.stack([me // 2, me % 2]).astype(jnp.int32)
    half = jax.ShapeDtypeStruct((chips, CAP, PB, 2 * vectors), jnp.float32)
    blocks = vectors * (vectors - 1) // 2
    c = chunks - 1
    keep, send = pl.pallas_call(
        functools.partial(last_chunk_kernel, tiles, c * per_chunk, factor),
        out_shape=[half] * 2,
        in_specs=[SMEM] * 2 + [VMEM] * 9,
        out_specs=[VMEM] * 2,
        scratch_shapes=[pltpu.VMEM((pair_rows, 2 * vectors), jnp.float32)]
        + scratch
        + [
            pltpu.VMEM((vectors * vectors // 2, 2 * vectors), jnp.float32),
            pltpu.VMEM((vectors * vectors // 4, 2 * vectors), jnp.float32),
            pltpu.VMEM((blocks, 2 * vectors), jnp.float32),
        ],
        compiler_params=params(48),
        cost_estimate=cost(8e9, 6 * piece_bytes),
        name="last_pairs",
    )(
        place, block_slot, links, low_links, lower[c], upper[c], sums[c], sums[chunks + c],
        own[c], own[chunks + c], before,
    )
    received = lax.ppermute(send, "brick", [(i, i ^ 1) for i in range(count)])
    share = jax.ShapeDtypeStruct((CAP, PB, 2 * vectors), jnp.float32)
    shares = pl.pallas_call(
        combine_kernel,
        out_shape=[share] * chips,
        in_specs=[VMEM] * 2,
        out_specs=[VMEM] * chips,
        compiler_params=params(32),
        name="combine",
    )(keep, received)
    arrived = [shares[0]] + [
        lax.ppermute(
            shares[away],
            "brick",
            [(i, ((i // 2 + away) % chips) * 2 + i % 2) for i in range(count)],
        )
        for away in range(1, chips)
    ]
    return pl.pallas_call(
        total_kernel,
        out_shape=share,
        in_specs=[VMEM] * chips,
        out_specs=VMEM,
        compiler_params=params(32),
        name="total",
    )(*arrived)


def solution(mesh):
    return jax.shard_map(
        on_device,
        mesh=mesh,
        in_specs=(
            P(None, None, None, ("cuts", "brick"), None),
            P(None, None, None, None, ("cuts", "brick"), None),
            P(),
        ),
        out_specs=P(("cuts", "brick"), None, None),
        check_vma=False,
    )
```

```python
import functools
import math

import jax
import jax.numpy as jnp
import numpy as np
from jax import lax
from jax.experimental import pallas as pl
from jax.experimental.pallas import tpu as pltpu
from jax.sharding import PartitionSpec as P

PB = 32
CAP = 4
LX = 8
LANES = 128
ROWS = 8
VMEM = pl.BlockSpec(memory_space=pltpu.VMEM)
SMEM = pl.BlockSpec(memory_space=pltpu.SMEM)


def params(limit_mib):
    return pltpu.CompilerParams(vmem_limit_bytes=limit_mib * 1024 * 1024)


def cost(flops, bytes_accessed):
    return pl.CostEstimate(
        flops=int(flops), bytes_accessed=int(bytes_accessed), transcendentals=0
    )


def tile_rows(array):
    planes, sites = array.shape[-2:]
    tiles = sites // LANES
    lead = math.prod(array.shape[:-2])
    array = array.reshape(lead, planes, tiles, LANES).transpose(0, 2, 1, 3)
    return array.reshape(lead * tiles * planes, LANES)


def times(link, field, total):
    total = list(total)
    for out_row in range(3):
        for in_row in range(3):
            real, imag = link(0, out_row, in_row), link(1, out_row, in_row)
            f_real, f_imag = field[in_row], field[3 + in_row]
            total[out_row] = total[out_row] + real * f_real - imag * f_imag
            total[3 + out_row] = total[3 + out_row] + real * f_imag + imag * f_real
    return total


def adjoint(link, field, total):
    total = list(total)
    for out_row in range(3):
        for in_row in range(3):
            real, imag = link(0, in_row, out_row), link(1, in_row, out_row)
            f_real, f_imag = field[in_row], field[3 + in_row]
            total[out_row] = total[out_row] + real * f_real + imag * f_imag
            total[3 + out_row] = total[3 + out_row] + real * f_imag - imag * f_real
    return total


def link_row(part, row, column):
    return (part * 3 + row) * 3 + column


def split_kernel(tiles, chunk_tiles, place_ref, x_ref, link_ref, *refs):
    outer, (inner, plane_links, cross_links, top_links) = refs[: len(chunk_tiles)], refs[len(chunk_tiles) :]
    vectors = inner.shape[1]
    lower_core = place_ref[1] == 0
    for chunk, (first_tile, count) in enumerate(chunk_tiles):
        for part in range(6):
            for tile in range(first_tile, first_tile + count):
                start = (part * tiles + tile) * 2
                plane_0, plane_1 = (
                    x_ref[pl.ds(start + plane, vectors, stride=6 * tiles * 2), :]
                    for plane in range(2)
                )
                at = (tile - first_tile) * LANES
                outer[chunk][part, :, at : at + LANES] = jnp.where(lower_core, plane_0, plane_1)
                at = tile * LANES
                inner[part, :, at : at + LANES] = jnp.where(lower_core, plane_1, plane_0)
    for index in range(36 * tiles):
        plane_0, plane_1 = (link_ref[index * 2 + plane : index * 2 + plane + 1, :] for plane in range(2))
        plane_links[index : index + 1, :] = jnp.where(lower_core, plane_1, plane_0)
        index += 36 * tiles
        plane_links[index : index + 1, :] = jnp.where(lower_core, plane_0, plane_1)
    for part in range(2):
        for row in range(3):
            for column in range(3):
                for tile in range(tiles):
                    straight = ((36 + link_row(part, row, column)) * tiles + tile) * 2
                    turned = ((36 + link_row(part, column, row)) * tiles + tile) * 2
                    index = link_row(part, row, column) * tiles + tile
                    sign = -1.0 if part else 1.0
                    cross_links[index : index + 1, :] = jnp.where(
                        lower_core,
                        link_ref[straight : straight + 1, :],
                        sign * link_ref[turned : turned + 1, :],
                    )
                    top_links[index : index + 1, :] = link_ref[straight + 1 : straight + 2, :]


def z_link(top_links, low_links, tiles, tile, use_low):
    found = {}
    for part in range(2):
        for row in range(3):
            for column in range(3):
                straight = link_row(part, row, column) * tiles + tile
                turned = link_row(part, column, row) * tiles + tile
                sign = -1.0 if part else 1.0
                found[part, row, column] = jnp.where(
                    use_low,
                    sign * low_links[turned : turned + 1, :],
                    top_links[straight : straight + 1, :],
                )
    return lambda *index: found[index]


def local_kernel(tiles, chunk_tiles, filtering, place_ref, *refs):
    plane_links, cross_links, top_links, low_links, inner, partner = refs[:6]
    outer = refs[6 : 6 + len(chunk_tiles)]
    refs = refs[6 + len(chunk_tiles) :]
    own = None
    if filtering:
        own, refs = refs[0], refs[1:]
    inner_out, outer_out = refs
    vectors = inner.shape[1]
    use_low = place_ref[1] == 1
    lane = lax.broadcasted_iota(jnp.int32, (ROWS, LANES), 1)
    column = lane % LX
    first_column, last_column = column == 0, column == LX - 1
    below, above = lane < LX, lane >= LANES - LX
    zeros = [jnp.zeros((ROWS, LANES), jnp.float32)] * 6

    def step(group, carry):
        rows = pl.ds(pl.multiple_of(group * ROWS, ROWS), ROWS)

        def get(plane, tile):
            if plane == 0:
                ref, at = inner, tile * LANES
            else:
                for chunk, (first_tile, count) in enumerate(chunk_tiles):
                    if first_tile <= tile < first_tile + count:
                        ref, at = outer[chunk], (tile - first_tile) * LANES
            return [ref[part, rows, at : at + LANES] for part in range(6)]

        def link_of(direction, plane, tile):
            def link(part, row, column_at):
                index = plane * 36 + direction * 18 + link_row(part, row, column_at)
                index = index * tiles + tile
                return plane_links[index : index + 1, :]

            return link

        def cross_of(tile):
            def link(part, row, column_at):
                index = link_row(part, row, column_at) * tiles + tile
                return cross_links[index : index + 1, :]

            return link

        for plane in range(2):
            sums = []
            rolled_in = []
            rolled_out = []
            for tile in range(tiles):
                field = get(plane, tile)
                ahead = [
                    jnp.where(
                        last_column, pltpu.roll(f, LX - 1, 1), pltpu.roll(f, LANES - 1, 1)
                    )
                    for f in field
                ]
                behind = adjoint(link_of(0, plane, tile), field, zeros)
                total = [
                    jnp.where(
                        first_column, pltpu.roll(f, LANES - LX + 1, 1), pltpu.roll(f, 1, 1)
                    )
                    for f in behind
                ]
                total = times(link_of(0, plane, tile), ahead, total)
                if plane == 0:
                    total = adjoint(cross_of(tile), get(1, tile), total)
                    beyond = [
                        partner[part, rows, tile * LANES : (tile + 1) * LANES] for part in range(6)
                    ]
                    link = z_link(top_links, low_links, tiles, tile, use_low)
                    total = times(link, beyond, total)
                else:
                    total = times(cross_of(tile), get(0, tile), total)
                sums.append(total)
                rolled_in.append([pltpu.roll(f, LANES - LX, 1) for f in field])
                rolled_out.append(
                    [
                        pltpu.roll(f, LX, 1)
                        for f in adjoint(link_of(1, plane, tile), field, zeros)
                    ]
                )
            for tile in range(tiles):
                after, before = (tile + 1) % tiles, (tile - 1) % tiles
                ahead = [
                    jnp.where(above, b, a) for a, b in zip(rolled_in[tile], rolled_in[after])
                ]
                total = times(link_of(1, plane, tile), ahead, sums[tile])
                lanes = slice(tile * LANES, (tile + 1) * LANES)
                for part in range(6):
                    back = jnp.where(below, rolled_out[before][part], rolled_out[tile][part])
                    value = total[part] + back
                    if plane == 1:
                        outer_out[part, rows, lanes] = value
                    elif filtering:
                        inner_out[part, rows, lanes] = (
                            value * (2.0 / 6.0) - own[part, rows, lanes]
                        )
                    else:
                        inner_out[part, rows, lanes] = value * (1.0 / 6.0)
        return carry

    lax.fori_loop(0, vectors // ROWS, step, 0)


def finish_outer(tiles, chunk, place_ref, top_links, low_links, far, sums, out, finish):
    first_tile, count = chunk
    vectors = far.shape[1]
    use_low = place_ref[1] == 0
    for tile in range(count):
        link = z_link(top_links, low_links, tiles, first_tile + tile, use_low)
        lanes = slice(tile * LANES, (tile + 1) * LANES)
        at = (first_tile + tile) * LANES

        def step(group, carry):
            rows = pl.ds(pl.multiple_of(group * ROWS, ROWS), ROWS)
            field = [far[part, rows, lanes] for part in range(6)]
            total = [sums[part, rows, at : at + LANES] for part in range(6)]
            total = times(link, field, total)
            for part in range(6):
                out[part, rows, lanes] = finish(total[part], (part, rows, lanes))
            return carry

        lax.fori_loop(0, vectors // ROWS, step, 0, unroll=2)


def edge_kernel(tiles, chunk, place_ref, top_links, low_links, far, sums, out):
    finish_outer(
        tiles, chunk, place_ref, top_links, low_links, far, sums, out,
        lambda total, index: total * (1.0 / 6.0),
    )


def pair_tiles(vectors):
    half = vectors // ROWS // 2
    return [
        (base + left, base + right)
        for base in (0, half)
        for right in range(half)
        for left in range(right + 1)
    ]


def add_pairs(field, low, quarks, sums):
    vectors, width = field.shape[1:]
    for colour in range(3):
        real = field[colour].astype(jnp.bfloat16)
        imag = field[3 + colour].astype(jnp.bfloat16)
        for part, (top, bottom) in enumerate(((real, imag), (-imag, real))):
            at = (part * 3 + colour) * width
            low[:vectors, at : at + width] = top
            low[vectors:, at : at + width] = bottom

    combos = pair_tiles(vectors)
    block = ROWS * ROWS
    steps = 4
    step_combos = len(combos) // steps
    step_rows = step_combos * block

    def form(number):
        left, right = combos[number]
        for tile in range(width // LANES):
            at = tile * LANES
            lanes = slice(at, at + LANES)
            b = [
                field[part, right * ROWS : (right + 1) * ROWS, lanes]
                for part in range(6)
            ]
            for row in range(0, ROWS, 2):
                made = [[] for _ in range(6)]
                for index in (left * ROWS + row, left * ROWS + row + 1):
                    a = [field[part, index : index + 1, lanes] for part in range(6)]
                    for colour in range(3):
                        x, y = (colour + 1) % 3, (colour + 2) % 3
                        made[colour].append(
                            (a[x] * b[y] - a[3 + x] * b[3 + y])
                            - (a[y] * b[x] - a[3 + y] * b[3 + x])
                        )
                        made[3 + colour].append(
                            (a[x] * b[3 + y] + a[3 + x] * b[y])
                            - (a[y] * b[3 + x] + a[3 + y] * b[x])
                        )
                start = number * block + row * ROWS
                for part in range(6):
                    quarks[
                        start : start + 2 * ROWS, part * width + at : part * width + at + LANES
                    ] = jnp.concatenate(made[part], 0).astype(jnp.bfloat16)

    def form_step(step):
        for number in range(step * step_combos, (step + 1) * step_combos):
            form(number)

    form_step(0)
    for step in range(steps):
        if step + 1 < steps:
            form_step(step + 1)
        rows = slice(step * step_rows, (step + 1) * step_rows)
        sums[rows, :] += lax.dot_general(
            quarks[rows, :],
            low[...],
            (((1,), (1,)), ((), ())),
            preferred_element_type=jnp.float32,
        )


def inner_pairs_kernel(field, sums, low, quarks):
    sums[...] = jnp.zeros_like(sums)
    width = low.shape[1] // 6
    for start in range(0, field.shape[2], width):
        add_pairs(field.at[:, :, start : start + width], low, quarks, sums)


def outer_pairs_kernel(
    tiles, chunk, place_ref, top_links, low_links, far, partial, own, before, sums, field, low, quarks
):
    finish_outer(
        tiles, chunk, place_ref, top_links, low_links, far, partial, field,
        lambda total, index: total * (2.0 / 6.0) - own[index],
    )
    sums[...] = before[...]
    add_pairs(field, low, quarks, sums)


def arrange(sums, grid, crossed, ordered, factor):
    half = grid.shape[0] // 2
    side = math.isqrt(half)
    vectors = 2 * side
    block = ROWS * ROWS
    for number, (left, right) in enumerate(pair_tiles(vectors)):
        for row in range(ROWS):
            start = number * block + row * ROWS
            at = (left * ROWS + row) * side + right * ROWS % side
            grid[at : at + ROWS, :] = sums[start : start + ROWS, :] * factor
            if left != right:
                at = (right * ROWS + row) * side + left * ROWS % side
                grid[at : at + ROWS, :] = (
                    sums[pl.ds(number * block + row, ROWS, stride=ROWS), :] * -factor
                )
    lane = lax.broadcasted_iota(jnp.int32, (side, 2 * vectors), 1)
    own_half = lane % vectors < side
    per = 2 * vectors // side
    for start in range(0, half, 2 * vectors):
        turned = grid[half + start : half + start + 2 * vectors, :].T
        real, imag = turned[:side], turned[vectors : vectors + side]
        for index in range(per):
            second = start // side + index
            turn = (side - index * side) % (2 * vectors)
            value = jnp.where(
                lane < vectors,
                pltpu.roll(real, turn, 1) if turn else real,
                pltpu.roll(imag, (turn + vectors) % (2 * vectors), 1)
                if (turn + vectors) % (2 * vectors)
                else imag,
            )
            crossed[pl.ds(second, side, stride=side), :] = value
    for start in range(0, half, 2 * vectors):
        turned = grid[start : start + 2 * vectors, :].T
        real, imag = turned[side:vectors], turned[vectors + side :]
        for index in range(per):
            first = start // side + index
            turn = (-index * side) % (2 * vectors)
            value = jnp.where(
                lane < vectors,
                pltpu.roll(real, turn, 1) if turn else real,
                pltpu.roll(imag, (turn + vectors) % (2 * vectors), 1)
                if (turn + vectors) % (2 * vectors)
                else imag,
            )
            value = jnp.where(own_half, -value, crossed[first * side : (first + 1) * side, :])
            pair = first * vectors - first * (first + 1) // 2 + side - first - 1
            ordered[pair : pair + side, :] = value
    for first in range(vectors):
        skip = first % side + 1
        if skip < side:
            pair = first * vectors - first * (first + 1) // 2
            ordered[pair : pair + side - skip, :] = grid[
                first * side + skip : (first + 1) * side, :
            ]


def last_pairs_kernel(
    tiles, chunk, factor, slot_ref, place_ref, top_links, low_links, far, partial, own, before,
    keep, send, sums, field, low, quarks, grid, crossed, ordered,
):
    outer_pairs_kernel(
        tiles, chunk, place_ref, top_links, low_links, far, partial, own, before, sums, field, low,
        quarks,
    )
    arrange(sums, grid, crossed, ordered, factor)
    keep[...] = jnp.zeros_like(keep)
    send[...] = jnp.zeros_like(send)
    chips = keep.shape[0]
    my_chip, my_core = place_ref[0], place_ref[1]

    def place(block, carry):
        slot = slot_ref[block]
        owner = slot // CAP
        away = lax.rem(owner // 2 - my_chip + chips, chips)
        value = ordered[pl.ds(pl.multiple_of(block * PB, PB), PB), :]

        @pl.when(owner % 2 == my_core)
        def _():
            keep[away, slot % CAP] = value

        @pl.when(owner % 2 != my_core)
        def _():
            send[away, slot % CAP] = value

        return carry

    lax.fori_loop(0, slot_ref.shape[0], place, 0)


def combine_kernel(keep, received, *outs):
    for away, out in enumerate(outs):
        out[...] = keep[away] + received[away]


def total_kernel(*refs):
    total = refs[0][...]
    for ref in refs[1:-1]:
        total = total + ref[...]
    refs[-1][...] = total


def on_device(eigen_vectors, link_field, block_slot):
    count = lax.axis_size("brick")
    vectors, sites = eigen_vectors.shape[0], eigen_vectors.shape[-1]
    planes = eigen_vectors.shape[-2]
    tiles = sites // LANES
    half_tiles = tiles // 2
    chunk_tiles = ((0, half_tiles), (half_tiles, tiles - half_tiles))

    def plane_of(width):
        return jax.ShapeDtypeStruct((6, vectors, width), jnp.float32)

    plane = plane_of(sites)
    pieces = [plane_of(size * LANES) for _, size in chunk_tiles]
    plane_bytes = 6 * vectors * sites * 4
    pair_rows = len(pair_tiles(vectors)) * ROWS * ROWS
    up = [(i, (i + 1) % count) for i in range(count)]
    on_chip = [(i, i ^ 1) for i in range(count)]
    off_chip = [(i, (i + 2 * (i % 2) - 1) % count) for i in range(count)]
    me = lax.axis_index("brick")
    place = jnp.stack([me // 2, me % 2]).astype(jnp.int32)
    z_links = jax.ShapeDtypeStruct((18 * tiles, LANES), jnp.float32)

    *outer, inner, plane_links, cross_links, top_links = pl.pallas_call(
        functools.partial(split_kernel, tiles, chunk_tiles),
        out_shape=pieces
        + [plane, jax.ShapeDtypeStruct((72 * tiles, LANES), jnp.float32), z_links, z_links],
        in_specs=[SMEM] + [VMEM] * 2,
        out_specs=[VMEM] * (len(pieces) + 4),
        compiler_params=params(32),
        name="split",
    )(place, tile_rows(eigen_vectors), tile_rows(link_field))

    def off(fields):
        return [lax.ppermute(field, "brick", off_chip) for field in fields]

    def local_hops(inner, partner, outer, own=()):
        return pl.pallas_call(
            functools.partial(local_kernel, tiles, chunk_tiles, len(own) > 0),
            out_shape=[plane] * 2,
            in_specs=[SMEM] + [VMEM] * (6 + len(pieces) + len(own)),
            out_specs=[VMEM] * 2,
            compiler_params=params(48),
            cost_estimate=cost(5e9, 5 * plane_bytes),
            name="local",
        )(place, plane_links, cross_links, top_links, low_links, inner, partner, *outer, *own)

    far = off(outer)
    low_links = lax.ppermute(top_links, "brick", up)
    partner = lax.ppermute(inner, "brick", on_chip)
    first_inner, sums = local_hops(inner, partner, outer)
    partner = lax.ppermute(first_inner, "brick", on_chip)
    first_outer = []
    for chunk, piece, field in zip(chunk_tiles, pieces, far):
        first_outer.append(
            pl.pallas_call(
                functools.partial(edge_kernel, tiles, chunk),
                out_shape=piece,
                in_specs=[SMEM] + [VMEM] * 4,
                out_specs=VMEM,
                compiler_params=params(32),
                name="edge",
            )(place, top_links, low_links, field, sums)
        )
    far = off(first_outer)
    filtered_inner, sums = local_hops(first_inner, partner, first_outer, (inner,))

    def scratch(width):
        return [
            pltpu.VMEM((2 * vectors, 6 * width), jnp.bfloat16),
            pltpu.VMEM((pair_rows, 6 * width), jnp.bfloat16),
        ]

    partial_sums = jax.ShapeDtypeStruct((pair_rows, 2 * vectors), jnp.float32)
    before = pl.pallas_call(
        inner_pairs_kernel,
        out_shape=partial_sums,
        in_specs=[VMEM],
        out_specs=VMEM,
        scratch_shapes=scratch(2 * LANES),
        compiler_params=params(48),
        cost_estimate=cost(8e9, 6 * plane_bytes),
        name="inner_pairs",
    )(filtered_inner)
    for chunk, piece, field, own in zip(chunk_tiles[:-1], pieces, far, outer):
        before = pl.pallas_call(
            functools.partial(outer_pairs_kernel, tiles, chunk),
            out_shape=partial_sums,
            in_specs=[SMEM] + [VMEM] * 6,
            out_specs=VMEM,
            scratch_shapes=[pltpu.VMEM(piece.shape, jnp.float32)] + scratch(piece.shape[2]),
            compiler_params=params(48),
            cost_estimate=cost(4e9, 3 * plane_bytes),
            name="outer_pairs",
        )(place, top_links, low_links, field, sums, own, before)
    factor = 1.0 / math.sqrt(3.0 * sites * planes * count)
    chips = count // 2
    half = jax.ShapeDtypeStruct((chips, CAP, PB, 2 * vectors), jnp.float32)
    blocks = vectors * (vectors - 1) // 2
    keep, send = pl.pallas_call(
        functools.partial(last_pairs_kernel, tiles, chunk_tiles[-1], factor),
        out_shape=[half] * 2,
        in_specs=[SMEM] * 2 + [VMEM] * 6,
        out_specs=[VMEM] * 2,
        scratch_shapes=[
            pltpu.VMEM(partial_sums.shape, jnp.float32),
            pltpu.VMEM(pieces[-1].shape, jnp.float32),
        ]
        + scratch(pieces[-1].shape[2])
        + [
            pltpu.VMEM((vectors * vectors // 2, 2 * vectors), jnp.float32),
            pltpu.VMEM((vectors * vectors // 4, 2 * vectors), jnp.float32),
            pltpu.VMEM((blocks, 2 * vectors), jnp.float32),
        ],
        compiler_params=params(48),
        cost_estimate=cost(4e9, 3 * plane_bytes),
        name="last_pairs",
    )(block_slot, place, top_links, low_links, far[-1], sums, outer[-1], before)
    received = lax.ppermute(send, "brick", on_chip)
    share = jax.ShapeDtypeStruct((CAP, PB, 2 * vectors), jnp.float32)
    shares = pl.pallas_call(
        combine_kernel,
        out_shape=[share] * chips,
        in_specs=[VMEM] * 2,
        out_specs=[VMEM] * chips,
        compiler_params=params(32),
        name="combine",
    )(keep, received)
    arrived = [shares[0]] + [
        lax.ppermute(
            shares[away],
            "brick",
            [(i, ((i // 2 + away) % chips) * 2 + i % 2) for i in range(count)],
        )
        for away in range(1, chips)
    ]
    return pl.pallas_call(
        total_kernel,
        out_shape=share,
        in_specs=[VMEM] * chips,
        out_specs=VMEM,
        compiler_params=params(32),
        name="total",
    )(*arrived)


def solution(mesh):
    return jax.shard_map(
        on_device,
        mesh=mesh,
        in_specs=(
            P(None, None, None, ("cuts", "brick"), None),
            P(None, None, None, None, ("cuts", "brick"), None),
            P(),
        ),
        out_specs=P(("cuts", "brick"), None, None),
        check_vma=False,
    )
```

```python
import functools
import math

import jax
import jax.numpy as jnp
import numpy as np
from jax import lax
from jax.experimental import pallas as pl
from jax.experimental.pallas import tpu as pltpu
from jax.sharding import PartitionSpec as P

PB = 32
CAP = 4
LX = 8
LANES = 128
ROWS = 8
VMEM = pl.BlockSpec(memory_space=pltpu.VMEM)
SMEM = pl.BlockSpec(memory_space=pltpu.SMEM)


def params(limit_mib):
    return pltpu.CompilerParams(vmem_limit_bytes=limit_mib * 1024 * 1024)


def cost(flops, bytes_accessed):
    return pl.CostEstimate(
        flops=int(flops), bytes_accessed=int(bytes_accessed), transcendentals=0
    )


def tile_rows(array):
    planes, sites = array.shape[-2:]
    tiles = sites // LANES
    lead = math.prod(array.shape[:-2])
    array = array.reshape(lead, planes, tiles, LANES).transpose(0, 2, 1, 3)
    return array.reshape(lead * tiles * planes, LANES)


def times(link, field, total):
    total = list(total)
    for out_row in range(3):
        for in_row in range(3):
            real, imag = link(0, out_row, in_row), link(1, out_row, in_row)
            f_real, f_imag = field[in_row], field[3 + in_row]
            total[out_row] = total[out_row] + real * f_real - imag * f_imag
            total[3 + out_row] = total[3 + out_row] + real * f_imag + imag * f_real
    return total


def adjoint(link, field, total):
    total = list(total)
    for out_row in range(3):
        for in_row in range(3):
            real, imag = link(0, in_row, out_row), link(1, in_row, out_row)
            f_real, f_imag = field[in_row], field[3 + in_row]
            total[out_row] = total[out_row] + real * f_real + imag * f_imag
            total[3 + out_row] = total[3 + out_row] + real * f_imag - imag * f_real
    return total


def link_row(part, row, column):
    return (part * 3 + row) * 3 + column


def split_kernel(tiles, chunk_tiles, place_ref, x_ref, link_ref, *refs):
    outer, (inner, plane_links, cross_links, top_links) = refs[: len(chunk_tiles)], refs[len(chunk_tiles) :]
    vectors = inner.shape[1]
    lower_core = place_ref[1] == 0
    for chunk, (first_tile, count) in enumerate(chunk_tiles):
        for part in range(6):
            for tile in range(first_tile, first_tile + count):
                start = (part * tiles + tile) * 2
                plane_0, plane_1 = (
                    x_ref[pl.ds(start + plane, vectors, stride=6 * tiles * 2), :]
                    for plane in range(2)
                )
                at = (tile - first_tile) * LANES
                outer[chunk][part, :, at : at + LANES] = jnp.where(lower_core, plane_0, plane_1)
                at = tile * LANES
                inner[part, :, at : at + LANES] = jnp.where(lower_core, plane_1, plane_0)
    for index in range(36 * tiles):
        plane_0, plane_1 = (link_ref[index * 2 + plane : index * 2 + plane + 1, :] for plane in range(2))
        plane_links[index : index + 1, :] = jnp.where(lower_core, plane_1, plane_0)
        index += 36 * tiles
        plane_links[index : index + 1, :] = jnp.where(lower_core, plane_0, plane_1)
    for part in range(2):
        for row in range(3):
            for column in range(3):
                for tile in range(tiles):
                    straight = ((36 + link_row(part, row, column)) * tiles + tile) * 2
                    turned = ((36 + link_row(part, column, row)) * tiles + tile) * 2
                    index = link_row(part, row, column) * tiles + tile
                    sign = -1.0 if part else 1.0
                    cross_links[index : index + 1, :] = jnp.where(
                        lower_core,
                        link_ref[straight : straight + 1, :],
                        sign * link_ref[turned : turned + 1, :],
                    )
                    top_links[index : index + 1, :] = link_ref[straight + 1 : straight + 2, :]


def z_link(top_links, low_links, tiles, tile, use_low):
    found = {}
    for part in range(2):
        for row in range(3):
            for column in range(3):
                straight = link_row(part, row, column) * tiles + tile
                turned = link_row(part, column, row) * tiles + tile
                sign = -1.0 if part else 1.0
                found[part, row, column] = jnp.where(
                    use_low,
                    sign * low_links[turned : turned + 1, :],
                    top_links[straight : straight + 1, :],
                )
    return lambda *index: found[index]


def local_kernel(tiles, chunk_tiles, plane_links, cross_links, inner, *refs):
    outer, (inner_out, outer_out) = refs[: len(chunk_tiles)], refs[len(chunk_tiles) :]
    vectors = inner.shape[1]
    lane = lax.broadcasted_iota(jnp.int32, (ROWS, LANES), 1)
    column = lane % LX
    first_column, last_column = column == 0, column == LX - 1
    below, above = lane < LX, lane >= LANES - LX
    zeros = [jnp.zeros((ROWS, LANES), jnp.float32)] * 6

    def step(group, carry):
        rows = pl.ds(pl.multiple_of(group * ROWS, ROWS), ROWS)

        def get(plane, tile):
            if plane == 0:
                ref, at = inner, tile * LANES
            else:
                for chunk, (first_tile, count) in enumerate(chunk_tiles):
                    if first_tile <= tile < first_tile + count:
                        ref, at = outer[chunk], (tile - first_tile) * LANES
            return [ref[part, rows, at : at + LANES] for part in range(6)]

        def link_of(direction, plane, tile):
            def link(part, row, column_at):
                index = plane * 36 + direction * 18 + link_row(part, row, column_at)
                index = index * tiles + tile
                return plane_links[index : index + 1, :]

            return link

        def cross_of(tile):
            def link(part, row, column_at):
                index = link_row(part, row, column_at) * tiles + tile
                return cross_links[index : index + 1, :]

            return link

        for plane in range(2):
            sums = []
            rolled_in = []
            rolled_out = []
            for tile in range(tiles):
                field = get(plane, tile)
                ahead = [
                    jnp.where(
                        last_column, pltpu.roll(f, LX - 1, 1), pltpu.roll(f, LANES - 1, 1)
                    )
                    for f in field
                ]
                behind = adjoint(link_of(0, plane, tile), field, zeros)
                total = [
                    jnp.where(
                        first_column, pltpu.roll(f, LANES - LX + 1, 1), pltpu.roll(f, 1, 1)
                    )
                    for f in behind
                ]
                total = times(link_of(0, plane, tile), ahead, total)
                if plane == 0:
                    total = adjoint(cross_of(tile), get(1, tile), total)
                else:
                    total = times(cross_of(tile), get(0, tile), total)
                sums.append(total)
                rolled_in.append([pltpu.roll(f, LANES - LX, 1) for f in field])
                rolled_out.append(
                    [
                        pltpu.roll(f, LX, 1)
                        for f in adjoint(link_of(1, plane, tile), field, zeros)
                    ]
                )
            for tile in range(tiles):
                after, before = (tile + 1) % tiles, (tile - 1) % tiles
                ahead = [
                    jnp.where(above, b, a) for a, b in zip(rolled_in[tile], rolled_in[after])
                ]
                total = times(link_of(1, plane, tile), ahead, sums[tile])
                lanes = slice(tile * LANES, (tile + 1) * LANES)
                for part in range(6):
                    back = jnp.where(below, rolled_out[before][part], rolled_out[tile][part])
                    out = outer_out if plane else inner_out
                    out[part, rows, lanes] = total[part] + back
        return carry

    lax.fori_loop(0, vectors // ROWS, step, 0)


def finish_hop(tiles, chunk, use_low, top_links, low_links, beyond, sums, out, finish):
    first_tile, count = chunk
    vectors = beyond.shape[1]
    for tile in range(count):
        link = z_link(top_links, low_links, tiles, first_tile + tile, use_low)
        lanes = slice(tile * LANES, (tile + 1) * LANES)
        at = (first_tile + tile) * LANES

        def step(group, carry):
            rows = pl.ds(pl.multiple_of(group * ROWS, ROWS), ROWS)
            field = [beyond[part, rows, lanes] for part in range(6)]
            total = [sums[part, rows, at : at + LANES] for part in range(6)]
            total = times(link, field, total)
            for part in range(6):
                out[part, rows, lanes] = finish(total[part], (part, rows, lanes))
            return carry

        lax.fori_loop(0, vectors // ROWS, step, 0, unroll=2)


def edge_kernel(tiles, chunk, low_core, place_ref, top_links, low_links, beyond, sums, *refs):
    finish_hop(
        tiles, chunk, place_ref[1] == low_core, top_links, low_links, beyond, sums, refs[-1],
        lambda total, index: total * (1.0 / 6.0),
    )


def pair_tiles(vectors):
    half = vectors // ROWS // 2
    return [
        (base + left, base + right)
        for base in (0, half)
        for right in range(half)
        for left in range(right + 1)
    ]


def add_pairs(field, low, quarks, sums):
    vectors, width = field.shape[1:]
    for colour in range(3):
        real = field[colour].astype(jnp.bfloat16)
        imag = field[3 + colour].astype(jnp.bfloat16)
        for part, (top, bottom) in enumerate(((real, imag), (-imag, real))):
            at = (part * 3 + colour) * width
            low[:vectors, at : at + width] = top
            low[vectors:, at : at + width] = bottom

    combos = pair_tiles(vectors)
    block = ROWS * ROWS
    steps = 4
    step_combos = len(combos) // steps
    step_rows = step_combos * block

    def form(number):
        left, right = combos[number]
        for tile in range(width // LANES):
            at = tile * LANES
            lanes = slice(at, at + LANES)
            b = [
                field[part, right * ROWS : (right + 1) * ROWS, lanes]
                for part in range(6)
            ]
            for row in range(0, ROWS, 2):
                made = [[] for _ in range(6)]
                for index in (left * ROWS + row, left * ROWS + row + 1):
                    a = [field[part, index : index + 1, lanes] for part in range(6)]
                    for colour in range(3):
                        x, y = (colour + 1) % 3, (colour + 2) % 3
                        made[colour].append(
                            (a[x] * b[y] - a[3 + x] * b[3 + y])
                            - (a[y] * b[x] - a[3 + y] * b[3 + x])
                        )
                        made[3 + colour].append(
                            (a[x] * b[3 + y] + a[3 + x] * b[y])
                            - (a[y] * b[3 + x] + a[3 + y] * b[x])
                        )
                start = number * block + row * ROWS
                for part in range(6):
                    quarks[
                        start : start + 2 * ROWS, part * width + at : part * width + at + LANES
                    ] = jnp.concatenate(made[part], 0).astype(jnp.bfloat16)

    def form_step(step):
        for number in range(step * step_combos, (step + 1) * step_combos):
            form(number)

    form_step(0)
    for step in range(steps):
        if step + 1 < steps:
            form_step(step + 1)
        rows = slice(step * step_rows, (step + 1) * step_rows)
        sums[rows, :] += lax.dot_general(
            quarks[rows, :],
            low[...],
            (((1,), (1,)), ((), ())),
            preferred_element_type=jnp.float32,
        )


def inner_pairs_kernel(
    tiles, place_ref, top_links, low_links, partner, partial, own, sums, field, low, quarks
):
    finish_hop(
        tiles, (0, tiles), place_ref[1] == 1, top_links, low_links, partner, partial, field,
        lambda total, index: total * (2.0 / 6.0) - own[index],
    )
    sums[...] = jnp.zeros_like(sums)
    width = low.shape[1] // 6
    for start in range(0, field.shape[2], width):
        add_pairs(field.at[:, :, start : start + width], low, quarks, sums)


def outer_pairs_kernel(
    tiles, chunk, place_ref, top_links, low_links, far, partial, own, before, sums, field, low, quarks
):
    finish_hop(
        tiles, chunk, place_ref[1] == 0, top_links, low_links, far, partial, field,
        lambda total, index: total * (2.0 / 6.0) - own[index],
    )
    sums[...] = before[...]
    add_pairs(field, low, quarks, sums)


def arrange(sums, grid, crossed, ordered, factor):
    half = grid.shape[0] // 2
    side = math.isqrt(half)
    vectors = 2 * side
    block = ROWS * ROWS
    for number, (left, right) in enumerate(pair_tiles(vectors)):
        for row in range(ROWS):
            start = number * block + row * ROWS
            at = (left * ROWS + row) * side + right * ROWS % side
            grid[at : at + ROWS, :] = sums[start : start + ROWS, :] * factor
            if left != right:
                at = (right * ROWS + row) * side + left * ROWS % side
                grid[at : at + ROWS, :] = (
                    sums[pl.ds(number * block + row, ROWS, stride=ROWS), :] * -factor
                )
    lane = lax.broadcasted_iota(jnp.int32, (side, 2 * vectors), 1)
    own_half = lane % vectors < side
    per = 2 * vectors // side
    for start in range(0, half, 2 * vectors):
        turned = grid[half + start : half + start + 2 * vectors, :].T
        real, imag = turned[:side], turned[vectors : vectors + side]
        for index in range(per):
            second = start // side + index
            turn = (side - index * side) % (2 * vectors)
            value = jnp.where(
                lane < vectors,
                pltpu.roll(real, turn, 1) if turn else real,
                pltpu.roll(imag, (turn + vectors) % (2 * vectors), 1)
                if (turn + vectors) % (2 * vectors)
                else imag,
            )
            crossed[pl.ds(second, side, stride=side), :] = value
    for start in range(0, half, 2 * vectors):
        turned = grid[start : start + 2 * vectors, :].T
        real, imag = turned[side:vectors], turned[vectors + side :]
        for index in range(per):
            first = start // side + index
            turn = (-index * side) % (2 * vectors)
            value = jnp.where(
                lane < vectors,
                pltpu.roll(real, turn, 1) if turn else real,
                pltpu.roll(imag, (turn + vectors) % (2 * vectors), 1)
                if (turn + vectors) % (2 * vectors)
                else imag,
            )
            value = jnp.where(own_half, -value, crossed[first * side : (first + 1) * side, :])
            pair = first * vectors - first * (first + 1) // 2 + side - first - 1
            ordered[pair : pair + side, :] = value
    for first in range(vectors):
        skip = first % side + 1
        if skip < side:
            pair = first * vectors - first * (first + 1) // 2
            ordered[pair : pair + side - skip, :] = grid[
                first * side + skip : (first + 1) * side, :
            ]


def last_pairs_kernel(
    tiles, chunk, factor, slot_ref, place_ref, top_links, low_links, far, partial, own, before,
    keep, send, sums, field, low, quarks, grid, crossed, ordered,
):
    outer_pairs_kernel(
        tiles, chunk, place_ref, top_links, low_links, far, partial, own, before, sums, field, low,
        quarks,
    )
    arrange(sums, grid, crossed, ordered, factor)
    keep[...] = jnp.zeros_like(keep)
    send[...] = jnp.zeros_like(send)
    chips = keep.shape[0]
    my_chip, my_core = place_ref[0], place_ref[1]

    def place(block, carry):
        slot = slot_ref[block]
        owner = slot // CAP
        away = lax.rem(owner // 2 - my_chip + chips, chips)
        value = ordered[pl.ds(pl.multiple_of(block * PB, PB), PB), :]

        @pl.when(owner % 2 == my_core)
        def _():
            keep[away, slot % CAP] = value

        @pl.when(owner % 2 != my_core)
        def _():
            send[away, slot % CAP] = value

        return carry

    lax.fori_loop(0, slot_ref.shape[0], place, 0)


def combine_kernel(keep, received, *outs):
    for away, out in enumerate(outs):
        out[...] = keep[away] + received[away]


def total_kernel(*refs):
    total = refs[0][...]
    for ref in refs[1:-1]:
        total = total + ref[...]
    refs[-1][...] = total


def on_device(eigen_vectors, link_field, block_slot):
    count = lax.axis_size("brick")
    vectors, sites = eigen_vectors.shape[0], eigen_vectors.shape[-1]
    planes = eigen_vectors.shape[-2]
    tiles = sites // LANES
    half_tiles = tiles // 2
    chunk_tiles = ((0, half_tiles), (half_tiles, tiles - half_tiles))

    def plane_of(width):
        return jax.ShapeDtypeStruct((6, vectors, width), jnp.float32)

    plane = plane_of(sites)
    pieces = [plane_of(size * LANES) for _, size in chunk_tiles]
    plane_bytes = 6 * vectors * sites * 4
    pair_rows = len(pair_tiles(vectors)) * ROWS * ROWS
    up = [(i, (i + 1) % count) for i in range(count)]
    on_chip = [(i, i ^ 1) for i in range(count)]
    off_chip = [(i, (i + 2 * (i % 2) - 1) % count) for i in range(count)]
    me = lax.axis_index("brick")
    place = jnp.stack([me // 2, me % 2]).astype(jnp.int32)
    z_links = jax.ShapeDtypeStruct((18 * tiles, LANES), jnp.float32)

    *outer, inner, plane_links, cross_links, top_links = pl.pallas_call(
        functools.partial(split_kernel, tiles, chunk_tiles),
        out_shape=pieces
        + [plane, jax.ShapeDtypeStruct((72 * tiles, LANES), jnp.float32), z_links, z_links],
        in_specs=[SMEM] + [VMEM] * 2,
        out_specs=[VMEM] * (len(pieces) + 4),
        compiler_params=params(32),
        name="split",
    )(place, tile_rows(eigen_vectors), tile_rows(link_field))

    def off(fields):
        return [lax.ppermute(field, "brick", off_chip) for field in fields]

    def local_hops(inner, outer):
        return pl.pallas_call(
            functools.partial(local_kernel, tiles, chunk_tiles),
            out_shape=[plane] * 2,
            in_specs=[VMEM] * (3 + len(pieces)),
            out_specs=[VMEM] * 2,
            compiler_params=params(48),
            cost_estimate=cost(5e9, 4 * plane_bytes),
            name="local",
        )(plane_links, cross_links, inner, *outer)

    def edge(chunk, low_core, shape, *args):
        return pl.pallas_call(
            functools.partial(edge_kernel, tiles, chunk, low_core),
            out_shape=shape,
            in_specs=[SMEM] + [VMEM] * (2 + len(args)),
            out_specs=VMEM,
            compiler_params=params(32),
            name="edge",
        )(place, top_links, low_links, *args)

    far = off(outer)
    low_links = lax.ppermute(top_links, "brick", up)
    partner = lax.ppermute(inner, "brick", on_chip)
    inner_sums, outer_sums = local_hops(inner, outer)
    first_inner = edge((0, tiles), 1, plane, partner, inner_sums)
    partner = lax.ppermute(first_inner, "brick", on_chip)
    token = sum(field[0, :ROWS, :LANES] for field in far)
    token = lax.ppermute(token, "brick", on_chip)
    first_outer = [
        edge(chunk, 0, piece, field, outer_sums, token)
        for chunk, piece, field in zip(chunk_tiles, pieces, far)
    ]
    far = off(first_outer)
    inner_sums, sums = local_hops(first_inner, first_outer)

    def scratch(width):
        return [
            pltpu.VMEM((2 * vectors, 6 * width), jnp.bfloat16),
            pltpu.VMEM((pair_rows, 6 * width), jnp.bfloat16),
        ]

    partial_sums = jax.ShapeDtypeStruct((pair_rows, 2 * vectors), jnp.float32)
    before = pl.pallas_call(
        functools.partial(inner_pairs_kernel, tiles),
        out_shape=partial_sums,
        in_specs=[SMEM] + [VMEM] * 5,
        out_specs=VMEM,
        scratch_shapes=[pltpu.VMEM(plane.shape, jnp.float32)] + scratch(2 * LANES),
        compiler_params=params(48),
        cost_estimate=cost(8e9, 6 * plane_bytes),
        name="inner_pairs",
    )(place, top_links, low_links, partner, inner_sums, inner)
    for chunk, piece, field, own in zip(chunk_tiles[:-1], pieces, far, outer):
        before = pl.pallas_call(
            functools.partial(outer_pairs_kernel, tiles, chunk),
            out_shape=partial_sums,
            in_specs=[SMEM] + [VMEM] * 6,
            out_specs=VMEM,
            scratch_shapes=[pltpu.VMEM(piece.shape, jnp.float32)] + scratch(piece.shape[2]),
            compiler_params=params(48),
            cost_estimate=cost(4e9, 3 * plane_bytes),
            name="outer_pairs",
        )(place, top_links, low_links, field, sums, own, before)
    factor = 1.0 / math.sqrt(3.0 * sites * planes * count)
    chips = count // 2
    half = jax.ShapeDtypeStruct((chips, CAP, PB, 2 * vectors), jnp.float32)
    blocks = vectors * (vectors - 1) // 2
    keep, send = pl.pallas_call(
        functools.partial(last_pairs_kernel, tiles, chunk_tiles[-1], factor),
        out_shape=[half] * 2,
        in_specs=[SMEM] * 2 + [VMEM] * 6,
        out_specs=[VMEM] * 2,
        scratch_shapes=[
            pltpu.VMEM(partial_sums.shape, jnp.float32),
            pltpu.VMEM(pieces[-1].shape, jnp.float32),
        ]
        + scratch(pieces[-1].shape[2])
        + [
            pltpu.VMEM((vectors * vectors // 2, 2 * vectors), jnp.float32),
            pltpu.VMEM((vectors * vectors // 4, 2 * vectors), jnp.float32),
            pltpu.VMEM((blocks, 2 * vectors), jnp.float32),
        ],
        compiler_params=params(48),
        cost_estimate=cost(4e9, 3 * plane_bytes),
        name="last_pairs",
    )(block_slot, place, top_links, low_links, far[-1], sums, outer[-1], before)
    received = lax.ppermute(send, "brick", on_chip)
    share = jax.ShapeDtypeStruct((CAP, PB, 2 * vectors), jnp.float32)
    shares = pl.pallas_call(
        combine_kernel,
        out_shape=[share] * chips,
        in_specs=[VMEM] * 2,
        out_specs=[VMEM] * chips,
        compiler_params=params(32),
        name="combine",
    )(keep, received)
    arrived = [shares[0]] + [
        lax.ppermute(
            shares[away],
            "brick",
            [(i, ((i // 2 + away) % chips) * 2 + i % 2) for i in range(count)],
        )
        for away in range(1, chips)
    ]
    return pl.pallas_call(
        total_kernel,
        out_shape=share,
        in_specs=[VMEM] * chips,
        out_specs=VMEM,
        compiler_params=params(32),
        name="total",
    )(*arrived)


def solution(mesh):
    return jax.shard_map(
        on_device,
        mesh=mesh,
        in_specs=(
            P(None, None, None, ("cuts", "brick"), None),
            P(None, None, None, None, ("cuts", "brick"), None),
            P(),
        ),
        out_specs=P(("cuts", "brick"), None, None),
        check_vma=False,
    )
```

```python
import functools
import math

import jax
import jax.numpy as jnp
import numpy as np
from jax import lax
from jax.experimental import pallas as pl
from jax.experimental.pallas import tpu as pltpu
from jax.sharding import PartitionSpec as P

PB = 32
CAP = 4
LX = 8
LANES = 128
ROWS = 8
VMEM = pl.BlockSpec(memory_space=pltpu.VMEM)
SMEM = pl.BlockSpec(memory_space=pltpu.SMEM)


def params(limit_mib):
    return pltpu.CompilerParams(vmem_limit_bytes=limit_mib * 1024 * 1024)


def cost(flops, bytes_accessed):
    return pl.CostEstimate(
        flops=int(flops), bytes_accessed=int(bytes_accessed), transcendentals=0
    )


def tile_rows(array):
    planes, sites = array.shape[-2:]
    tiles = sites // LANES
    lead = math.prod(array.shape[:-2])
    array = array.reshape(lead, planes, tiles, LANES).transpose(0, 2, 1, 3)
    return array.reshape(lead * tiles * planes, LANES)


def times(link, field, total):
    total = list(total)
    for out_row in range(3):
        for in_row in range(3):
            real, imag = link(0, out_row, in_row), link(1, out_row, in_row)
            f_real, f_imag = field[in_row], field[3 + in_row]
            total[out_row] = total[out_row] + real * f_real - imag * f_imag
            total[3 + out_row] = total[3 + out_row] + real * f_imag + imag * f_real
    return total


def adjoint(link, field, total):
    total = list(total)
    for out_row in range(3):
        for in_row in range(3):
            real, imag = link(0, in_row, out_row), link(1, in_row, out_row)
            f_real, f_imag = field[in_row], field[3 + in_row]
            total[out_row] = total[out_row] + real * f_real + imag * f_imag
            total[3 + out_row] = total[3 + out_row] + real * f_imag - imag * f_real
    return total


def link_row(part, row, column):
    return (part * 3 + row) * 3 + column


def split_kernel(tiles, chunk_tiles, place_ref, x_ref, *refs):
    outer, inner = refs[:-1], refs[-1]
    vectors = inner.shape[1]
    lower_core = place_ref[1] == 0
    for chunk, (first_tile, count) in enumerate(chunk_tiles):
        for part in range(6):
            for tile in range(first_tile, first_tile + count):
                start = (part * tiles + tile) * 2
                plane_0, plane_1 = (
                    x_ref[pl.ds(start + plane, vectors, stride=6 * tiles * 2), :]
                    for plane in range(2)
                )
                at = (tile - first_tile) * LANES
                outer[chunk][part, :, at : at + LANES] = jnp.where(lower_core, plane_0, plane_1)
                at = tile * LANES
                inner[part, :, at : at + LANES] = jnp.where(lower_core, plane_1, plane_0)


def link_kernel(tiles, place_ref, link_ref, plane_links, cross_links, top_links):
    lower_core = place_ref[1] == 0
    for index in range(36 * tiles):
        plane_0, plane_1 = (
            link_ref[index * 2 + plane : index * 2 + plane + 1, :] for plane in range(2)
        )
        plane_links[index : index + 1, :] = jnp.where(lower_core, plane_1, plane_0)
        index += 36 * tiles
        plane_links[index : index + 1, :] = jnp.where(lower_core, plane_0, plane_1)
    for part in range(2):
        for row in range(3):
            for column in range(3):
                for tile in range(tiles):
                    straight = ((36 + link_row(part, row, column)) * tiles + tile) * 2
                    turned = ((36 + link_row(part, column, row)) * tiles + tile) * 2
                    index = link_row(part, row, column) * tiles + tile
                    sign = -1.0 if part else 1.0
                    cross_links[index : index + 1, :] = jnp.where(
                        lower_core,
                        link_ref[straight : straight + 1, :],
                        sign * link_ref[turned : turned + 1, :],
                    )
                    top_links[index : index + 1, :] = link_ref[straight + 1 : straight + 2, :]


def z_link(top_links, low_links, tiles, tile, use_low):
    found = {}
    for part in range(2):
        for row in range(3):
            for column in range(3):
                straight = link_row(part, row, column) * tiles + tile
                turned = link_row(part, column, row) * tiles + tile
                sign = -1.0 if part else 1.0
                found[part, row, column] = jnp.where(
                    use_low,
                    sign * low_links[turned : turned + 1, :],
                    top_links[straight : straight + 1, :],
                )
    return lambda *index: found[index]


def local_kernel(tiles, chunk_tiles, plane_links, cross_links, inner, *refs):
    outer, (inner_out, outer_out) = refs[: len(chunk_tiles)], refs[len(chunk_tiles) :]
    vectors = inner.shape[1]
    lane = lax.broadcasted_iota(jnp.int32, (ROWS, LANES), 1)
    column = lane % LX
    first_column, last_column = column == 0, column == LX - 1
    below, above = lane < LX, lane >= LANES - LX
    zeros = [jnp.zeros((ROWS, LANES), jnp.float32)] * 6

    def step(group, carry):
        rows = pl.ds(pl.multiple_of(group * ROWS, ROWS), ROWS)

        def get(plane, tile):
            if plane == 0:
                ref, at = inner, tile * LANES
            else:
                for chunk, (first_tile, count) in enumerate(chunk_tiles):
                    if first_tile <= tile < first_tile + count:
                        ref, at = outer[chunk], (tile - first_tile) * LANES
            return [ref[part, rows, at : at + LANES] for part in range(6)]

        def link_of(direction, plane, tile):
            def link(part, row, column_at):
                index = plane * 36 + direction * 18 + link_row(part, row, column_at)
                index = index * tiles + tile
                return plane_links[index : index + 1, :]

            return link

        def cross_of(tile):
            def link(part, row, column_at):
                index = link_row(part, row, column_at) * tiles + tile
                return cross_links[index : index + 1, :]

            return link

        for plane in range(2):
            sums = []
            rolled_in = []
            rolled_out = []
            for tile in range(tiles):
                field = get(plane, tile)
                ahead = [
                    jnp.where(
                        last_column, pltpu.roll(f, LX - 1, 1), pltpu.roll(f, LANES - 1, 1)
                    )
                    for f in field
                ]
                behind = adjoint(link_of(0, plane, tile), field, zeros)
                total = [
                    jnp.where(
                        first_column, pltpu.roll(f, LANES - LX + 1, 1), pltpu.roll(f, 1, 1)
                    )
                    for f in behind
                ]
                total = times(link_of(0, plane, tile), ahead, total)
                if plane == 0:
                    total = adjoint(cross_of(tile), get(1, tile), total)
                else:
                    total = times(cross_of(tile), get(0, tile), total)
                sums.append(total)
                rolled_in.append([pltpu.roll(f, LANES - LX, 1) for f in field])
                rolled_out.append(
                    [
                        pltpu.roll(f, LX, 1)
                        for f in adjoint(link_of(1, plane, tile), field, zeros)
                    ]
                )
            for tile in range(tiles):
                after, before = (tile + 1) % tiles, (tile - 1) % tiles
                ahead = [
                    jnp.where(above, b, a) for a, b in zip(rolled_in[tile], rolled_in[after])
                ]
                total = times(link_of(1, plane, tile), ahead, sums[tile])
                lanes = slice(tile * LANES, (tile + 1) * LANES)
                for part in range(6):
                    back = jnp.where(below, rolled_out[before][part], rolled_out[tile][part])
                    out = outer_out if plane else inner_out
                    out[part, rows, lanes] = total[part] + back
        return carry

    lax.fori_loop(0, vectors // ROWS, step, 0)


def finish_hop(tiles, chunk, use_low, top_links, low_links, beyond, sums, out, finish):
    first_tile, count = chunk
    vectors = beyond.shape[1]
    for tile in range(count):
        link = z_link(top_links, low_links, tiles, first_tile + tile, use_low)
        lanes = slice(tile * LANES, (tile + 1) * LANES)
        at = (first_tile + tile) * LANES

        def step(group, carry):
            rows = pl.ds(pl.multiple_of(group * ROWS, ROWS), ROWS)
            field = [beyond[part, rows, lanes] for part in range(6)]
            total = [sums[part, rows, at : at + LANES] for part in range(6)]
            total = times(link, field, total)
            for part in range(6):
                out[part, rows, lanes] = finish(total[part], (part, rows, lanes))
            return carry

        lax.fori_loop(0, vectors // ROWS, step, 0, unroll=2)


def edge_kernel(tiles, chunk, low_core, place_ref, top_links, low_links, beyond, sums, *refs):
    finish_hop(
        tiles, chunk, place_ref[1] == low_core, top_links, low_links, beyond, sums, refs[-1],
        lambda total, index: total * (1.0 / 6.0),
    )


def pair_tiles(vectors):
    half = vectors // ROWS // 2
    return [
        (base + left, base + right)
        for base in (0, half)
        for left in range(half)
        for right in range(left, half)
    ]


def add_pairs(field, low, quarks, sums):
    vectors, width = field.shape[1:]
    for colour in range(3):
        real = field[colour].astype(jnp.bfloat16)
        imag = field[3 + colour].astype(jnp.bfloat16)
        for part, (top, bottom) in enumerate(((real, imag), (-imag, real))):
            at = (part * 3 + colour) * width
            low[:vectors, at : at + width] = top
            low[vectors:, at : at + width] = bottom

    combos = pair_tiles(vectors)
    block = ROWS * ROWS
    lefts = sorted({left for left, _ in combos})
    half = len(lefts) // 2
    steps = [lefts[:1], lefts[1:half], lefts[half : half + 1], lefts[half + 1 :]]

    def form(left):
        numbers = [number for number, combo in enumerate(combos) if combo[0] == left]
        for tile in range(width // LANES):
            at = tile * LANES
            lanes = slice(at, at + LANES)
            rights = [
                [
                    field[part, right * ROWS : (right + 1) * ROWS, lanes]
                    for part in range(6)
                ]
                for right in (combos[number][1] for number in numbers)
            ]
            for row in range(0, ROWS, 2):
                pair = [
                    [field[part, index : index + 1, lanes] for part in range(6)]
                    for index in (left * ROWS + row, left * ROWS + row + 1)
                ]
                for number, b in zip(numbers, rights):
                    made = [[] for _ in range(6)]
                    for a in pair:
                        for colour in range(3):
                            x, y = (colour + 1) % 3, (colour + 2) % 3
                            made[colour].append(
                                (a[x] * b[y] - a[3 + x] * b[3 + y])
                                - (a[y] * b[x] - a[3 + y] * b[3 + x])
                            )
                            made[3 + colour].append(
                                (a[x] * b[3 + y] + a[3 + x] * b[y])
                                - (a[y] * b[3 + x] + a[3 + y] * b[x])
                            )
                    start = number * block + row * ROWS
                    for part in range(6):
                        quarks[
                            start : start + 2 * ROWS,
                            part * width + at : part * width + at + LANES,
                        ] = jnp.concatenate(made[part], 0).astype(jnp.bfloat16)

    def multiply(step):
        numbers = [number for number, combo in enumerate(combos) if combo[0] in step]
        rows = slice(numbers[0] * block, (numbers[-1] + 1) * block)
        sums[rows, :] += lax.dot_general(
            quarks[rows, :],
            low[...],
            (((1,), (1,)), ((), ())),
            preferred_element_type=jnp.float32,
        )

    for left in steps[0]:
        form(left)
    for now, later in zip(steps, steps[1:] + [[]]):
        for left in later:
            form(left)
        multiply(now)


def inner_pairs_kernel(
    tiles, place_ref, top_links, low_links, partner, partial, own, sums, field, low, quarks
):
    finish_hop(
        tiles, (0, tiles), place_ref[1] == 1, top_links, low_links, partner, partial, field,
        lambda total, index: total * (2.0 / 6.0) - own[index],
    )
    sums[...] = jnp.zeros_like(sums)
    width = low.shape[1] // 6
    for start in range(0, field.shape[2], width):
        add_pairs(field.at[:, :, start : start + width], low, quarks, sums)


def outer_pairs_kernel(
    tiles, chunk, place_ref, top_links, low_links, far, partial, own, before, sums, field, low, quarks
):
    finish_hop(
        tiles, chunk, place_ref[1] == 0, top_links, low_links, far, partial, field,
        lambda total, index: total * (2.0 / 6.0) - own[index],
    )
    sums[...] = before[...]
    add_pairs(field, low, quarks, sums)


def arrange(sums, grid, crossed, ordered, factor):
    half = grid.shape[0] // 2
    side = math.isqrt(half)
    vectors = 2 * side
    block = ROWS * ROWS
    for number, (left, right) in enumerate(pair_tiles(vectors)):
        for row in range(ROWS):
            start = number * block + row * ROWS
            at = (left * ROWS + row) * side + right * ROWS % side
            grid[at : at + ROWS, :] = sums[start : start + ROWS, :] * factor
            if left != right:
                at = (right * ROWS + row) * side + left * ROWS % side
                grid[at : at + ROWS, :] = (
                    sums[pl.ds(number * block + row, ROWS, stride=ROWS), :] * -factor
                )
    lane = lax.broadcasted_iota(jnp.int32, (side, 2 * vectors), 1)
    own_half = lane % vectors < side
    per = 2 * vectors // side
    for start in range(0, half, 2 * vectors):
        turned = grid[half + start : half + start + 2 * vectors, :].T
        real, imag = turned[:side], turned[vectors : vectors + side]
        for index in range(per):
            second = start // side + index
            turn = (side - index * side) % (2 * vectors)
            value = jnp.where(
                lane < vectors,
                pltpu.roll(real, turn, 1) if turn else real,
                pltpu.roll(imag, (turn + vectors) % (2 * vectors), 1)
                if (turn + vectors) % (2 * vectors)
                else imag,
            )
            crossed[pl.ds(second, side, stride=side), :] = value
    for start in range(0, half, 2 * vectors):
        turned = grid[start : start + 2 * vectors, :].T
        real, imag = turned[side:vectors], turned[vectors + side :]
        for index in range(per):
            first = start // side + index
            turn = (-index * side) % (2 * vectors)
            value = jnp.where(
                lane < vectors,
                pltpu.roll(real, turn, 1) if turn else real,
                pltpu.roll(imag, (turn + vectors) % (2 * vectors), 1)
                if (turn + vectors) % (2 * vectors)
                else imag,
            )
            value = jnp.where(own_half, -value, crossed[first * side : (first + 1) * side, :])
            pair = first * vectors - first * (first + 1) // 2 + side - first - 1
            ordered[pair : pair + side, :] = value
    for first in range(vectors):
        skip = first % side + 1
        if skip < side:
            pair = first * vectors - first * (first + 1) // 2
            ordered[pair : pair + side - skip, :] = grid[
                first * side + skip : (first + 1) * side, :
            ]


def last_pairs_kernel(
    tiles, chunk, factor, slot_ref, place_ref, top_links, low_links, far, partial, own, before,
    keep, send, sums, field, low, quarks, grid, crossed, ordered,
):
    outer_pairs_kernel(
        tiles, chunk, place_ref, top_links, low_links, far, partial, own, before, sums, field, low,
        quarks,
    )
    arrange(sums, grid, crossed, ordered, factor)
    keep[...] = jnp.zeros_like(keep)
    send[...] = jnp.zeros_like(send)
    my_core = place_ref[1]

    def place(block, carry):
        slot = slot_ref[block]
        owner = slot // CAP
        chip = owner // 2
        value = ordered[pl.ds(pl.multiple_of(block * PB, PB), PB), :]

        @pl.when(owner % 2 == my_core)
        def _():
            keep[chip, slot % CAP] = value

        @pl.when(owner % 2 != my_core)
        def _():
            send[chip, slot % CAP] = value

        return carry

    lax.fori_loop(0, slot_ref.shape[0], place, 0)


def combine_kernel(keep, received, out):
    out[...] = keep[...] + received[...]


def total_kernel(arrived, out):
    total = arrived[0]
    for chip in range(1, arrived.shape[0]):
        total = total + arrived[chip]
    out[...] = total


def on_device(eigen_vectors, link_field, block_slot):
    count = lax.axis_size("brick")
    vectors, sites = eigen_vectors.shape[0], eigen_vectors.shape[-1]
    planes = eigen_vectors.shape[-2]
    tiles = sites // LANES
    half_tiles = tiles // 2
    chunk_tiles = ((0, half_tiles), (half_tiles, tiles - half_tiles))

    def plane_of(width):
        return jax.ShapeDtypeStruct((6, vectors, width), jnp.float32)

    plane = plane_of(sites)
    pieces = [plane_of(size * LANES) for _, size in chunk_tiles]
    plane_bytes = 6 * vectors * sites * 4
    pair_rows = len(pair_tiles(vectors)) * ROWS * ROWS
    up = [(i, (i + 1) % count) for i in range(count)]
    on_chip = [(i, i ^ 1) for i in range(count)]
    off_chip = [(i, (i + 2 * (i % 2) - 1) % count) for i in range(count)]
    me = lax.axis_index("brick")
    place = jnp.stack([me // 2, me % 2]).astype(jnp.int32)
    z_links = jax.ShapeDtypeStruct((18 * tiles, LANES), jnp.float32)

    plane_links, cross_links, top_links = pl.pallas_call(
        functools.partial(link_kernel, tiles),
        out_shape=[jax.ShapeDtypeStruct((72 * tiles, LANES), jnp.float32), z_links, z_links],
        in_specs=[SMEM, VMEM],
        out_specs=[VMEM] * 3,
        compiler_params=params(32),
        name="links",
    )(place, tile_rows(link_field))
    *outer, inner = pl.pallas_call(
        functools.partial(split_kernel, tiles, chunk_tiles),
        out_shape=pieces + [plane],
        in_specs=[SMEM, VMEM],
        out_specs=[VMEM] * (len(pieces) + 1),
        compiler_params=params(32),
        name="split",
    )(place, tile_rows(eigen_vectors))

    def off(fields):
        return [lax.ppermute(field, "brick", off_chip) for field in fields]

    def local_hops(inner, outer):
        return pl.pallas_call(
            functools.partial(local_kernel, tiles, chunk_tiles),
            out_shape=[plane] * 2,
            in_specs=[VMEM] * (3 + len(pieces)),
            out_specs=[VMEM] * 2,
            compiler_params=params(48),
            cost_estimate=cost(5e9, 4 * plane_bytes),
            name="local",
        )(plane_links, cross_links, inner, *outer)

    def edge(chunk, low_core, shape, *args):
        return pl.pallas_call(
            functools.partial(edge_kernel, tiles, chunk, low_core),
            out_shape=shape,
            in_specs=[SMEM] + [VMEM] * (2 + len(args)),
            out_specs=VMEM,
            compiler_params=params(32),
            name="edge",
        )(place, top_links, low_links, *args)

    far = off(outer)
    low_links = lax.ppermute(top_links, "brick", up)
    partner = lax.ppermute(inner, "brick", on_chip)
    inner_sums, outer_sums = local_hops(inner, outer)
    first_inner = edge((0, tiles), 1, plane, partner, inner_sums)
    partner = lax.ppermute(first_inner, "brick", on_chip)
    token = sum(field[0, :ROWS, :LANES] for field in far)
    token = lax.ppermute(token, "brick", on_chip)
    first_outer = [
        edge(chunk, 0, piece, field, outer_sums, token)
        for chunk, piece, field in zip(chunk_tiles, pieces, far)
    ]
    far = off(first_outer)
    inner_sums, sums = local_hops(first_inner, first_outer)

    def scratch(width):
        return [
            pltpu.VMEM((2 * vectors, 6 * width), jnp.bfloat16),
            pltpu.VMEM((pair_rows, 6 * width), jnp.bfloat16),
        ]

    partial_sums = jax.ShapeDtypeStruct((pair_rows, 2 * vectors), jnp.float32)
    before = pl.pallas_call(
        functools.partial(inner_pairs_kernel, tiles),
        out_shape=partial_sums,
        in_specs=[SMEM] + [VMEM] * 5,
        out_specs=VMEM,
        scratch_shapes=[pltpu.VMEM(plane.shape, jnp.float32)] + scratch(2 * LANES),
        compiler_params=params(48),
        cost_estimate=cost(8e9, 6 * plane_bytes),
        name="inner_pairs",
    )(place, top_links, low_links, partner, inner_sums, inner)
    for chunk, piece, field, own in zip(chunk_tiles[:-1], pieces, far, outer):
        before = pl.pallas_call(
            functools.partial(outer_pairs_kernel, tiles, chunk),
            out_shape=partial_sums,
            in_specs=[SMEM] + [VMEM] * 6,
            out_specs=VMEM,
            scratch_shapes=[pltpu.VMEM(piece.shape, jnp.float32)] + scratch(piece.shape[2]),
            compiler_params=params(48),
            cost_estimate=cost(4e9, 3 * plane_bytes),
            name="outer_pairs",
        )(place, top_links, low_links, field, sums, own, before)
    factor = 1.0 / math.sqrt(3.0 * sites * planes * count)
    chips = count // 2
    half = jax.ShapeDtypeStruct((chips, CAP, PB, 2 * vectors), jnp.float32)
    blocks = vectors * (vectors - 1) // 2
    keep, send = pl.pallas_call(
        functools.partial(last_pairs_kernel, tiles, chunk_tiles[-1], factor),
        out_shape=[half] * 2,
        in_specs=[SMEM] * 2 + [VMEM] * 6,
        out_specs=[VMEM] * 2,
        scratch_shapes=[
            pltpu.VMEM(partial_sums.shape, jnp.float32),
            pltpu.VMEM(pieces[-1].shape, jnp.float32),
        ]
        + scratch(pieces[-1].shape[2])
        + [
            pltpu.VMEM((vectors * vectors // 2, 2 * vectors), jnp.float32),
            pltpu.VMEM((vectors * vectors // 4, 2 * vectors), jnp.float32),
            pltpu.VMEM((blocks, 2 * vectors), jnp.float32),
        ],
        compiler_params=params(48),
        cost_estimate=cost(4e9, 3 * plane_bytes),
        name="last_pairs",
    )(block_slot, place, top_links, low_links, far[-1], sums, outer[-1], before)
    received = lax.ppermute(send, "brick", on_chip)
    share = jax.ShapeDtypeStruct((CAP, PB, 2 * vectors), jnp.float32)
    shares = pl.pallas_call(
        combine_kernel,
        out_shape=half,
        in_specs=[VMEM] * 2,
        out_specs=VMEM,
        compiler_params=params(32),
        name="combine",
    )(keep, received)
    arrived = lax.all_to_all(
        shares,
        "brick",
        0,
        0,
        axis_index_groups=[list(range(core, count, 2)) for core in range(2)],
        tiled=True,
    )
    return pl.pallas_call(
        total_kernel,
        out_shape=share,
        in_specs=[VMEM],
        out_specs=VMEM,
        compiler_params=params(32),
        name="total",
    )(arrived)


def solution(mesh):
    return jax.shard_map(
        on_device,
        mesh=mesh,
        in_specs=(
            P(None, None, None, ("cuts", "brick"), None),
            P(None, None, None, None, ("cuts", "brick"), None),
            P(),
        ),
        out_specs=P(("cuts", "brick"), None, None),
        check_vma=False,
    )
```

```python
import functools
import math

import jax
import jax.numpy as jnp
import numpy as np
from jax import lax
from jax.experimental import pallas as pl
from jax.experimental.pallas import tpu as pltpu
from jax.sharding import PartitionSpec as P

PB = 32
CAP = 4
LX = 8
LANES = 128
ROWS = 8
VMEM = pl.BlockSpec(memory_space=pltpu.VMEM)
SMEM = pl.BlockSpec(memory_space=pltpu.SMEM)


def params(limit_mib):
    return pltpu.CompilerParams(vmem_limit_bytes=limit_mib * 1024 * 1024)


def cost(flops, bytes_accessed):
    return pl.CostEstimate(
        flops=int(flops), bytes_accessed=int(bytes_accessed), transcendentals=0
    )


def tile_rows(array):
    planes, sites = array.shape[-2:]
    tiles = sites // LANES
    lead = math.prod(array.shape[:-2])
    array = array.reshape(lead, planes, tiles, LANES).transpose(0, 2, 1, 3)
    return array.reshape(lead * tiles * planes, LANES)


def times(link, field, total):
    total = list(total)
    for out_row in range(3):
        for in_row in range(3):
            real, imag = link(0, out_row, in_row), link(1, out_row, in_row)
            f_real, f_imag = field[in_row], field[3 + in_row]
            total[out_row] = total[out_row] + real * f_real - imag * f_imag
            total[3 + out_row] = total[3 + out_row] + real * f_imag + imag * f_real
    return total


def adjoint(link, field, total):
    total = list(total)
    for out_row in range(3):
        for in_row in range(3):
            real, imag = link(0, in_row, out_row), link(1, in_row, out_row)
            f_real, f_imag = field[in_row], field[3 + in_row]
            total[out_row] = total[out_row] + real * f_real + imag * f_imag
            total[3 + out_row] = total[3 + out_row] + real * f_imag - imag * f_real
    return total


def link_row(part, row, column):
    return (part * 3 + row) * 3 + column


def plane_rows(x_ref, part, tile, tiles, vectors, lower_core, inner):
    start = (part * tiles + tile) * 2
    plane_0, plane_1 = (
        x_ref[pl.ds(start + plane, vectors, stride=6 * tiles * 2), :] for plane in range(2)
    )
    if inner:
        return jnp.where(lower_core, plane_1, plane_0)
    return jnp.where(lower_core, plane_0, plane_1)


def outer_kernel(tiles, chunk_tiles, place_ref, x_ref, *outer):
    lower_core = place_ref[1] == 0
    for (first_tile, count), out in zip(chunk_tiles, outer):
        for part in range(6):
            for tile in range(count):
                at = tile * LANES
                out[part, :, at : at + LANES] = plane_rows(
                    x_ref, part, first_tile + tile, tiles, out.shape[1], lower_core, False
                )


def inner_kernel(
    tiles, vectors, place_ref, x_ref, link_ref, after, inner, plane_links, cross_links, top_links
):
    del after
    lower_core = place_ref[1] == 0
    for part in range(6):
        for tile in range(tiles):
            inner[part, :vectors, tile * LANES : (tile + 1) * LANES] = plane_rows(
                x_ref, part, tile, tiles, vectors, lower_core, True
            )
    inner[:, vectors:, :] = jnp.zeros_like(inner[:, vectors:, :])
    for index in range(36 * tiles):
        plane_0, plane_1 = (
            link_ref[index * 2 + plane : index * 2 + plane + 1, :] for plane in range(2)
        )
        plane_links[index : index + 1, :] = jnp.where(lower_core, plane_1, plane_0)
        index += 36 * tiles
        plane_links[index : index + 1, :] = jnp.where(lower_core, plane_0, plane_1)
    for part in range(2):
        for row in range(3):
            for column in range(3):
                for tile in range(tiles):
                    straight = ((36 + link_row(part, row, column)) * tiles + tile) * 2
                    turned = ((36 + link_row(part, column, row)) * tiles + tile) * 2
                    number = link_row(part, row, column)
                    index = number * tiles + tile
                    sign = -1.0 if part else 1.0
                    cross_links[index : index + 1, :] = jnp.where(
                        lower_core,
                        link_ref[straight : straight + 1, :],
                        sign * link_ref[turned : turned + 1, :],
                    )
                    top = link_ref[straight + 1 : straight + 2, :]
                    top_links[index : index + 1, :] = top
                    inner[
                        number // 3,
                        vectors + number % 3 : vectors + number % 3 + 1,
                        tile * LANES : (tile + 1) * LANES,
                    ] = top


def z_link(tiles, tile, top_links, low_link, use_low):
    found = {}
    for part in range(2):
        for row in range(3):
            for column in range(3):
                straight = link_row(part, row, column) * tiles + tile
                sign = -1.0 if part else 1.0
                value = jnp.where(
                    use_low,
                    sign * low_link(part, column, row, tile),
                    top_links[straight : straight + 1, :],
                )
                found[part, row, column] = jnp.broadcast_to(value, (ROWS, LANES))
    return lambda *index: found[index]


def low_rows(low_links, tiles):
    def low_link(part, row, column, tile):
        index = link_row(part, row, column) * tiles + tile
        return low_links[index : index + 1, :]

    return low_link


def partner_rows(partner, vectors):
    def low_link(part, row, column, tile):
        number = link_row(part, row, column)
        at = vectors + number % 3
        return partner[number // 3, at : at + 1, tile * LANES : (tile + 1) * LANES]

    return low_link


def tile_of(chunk_tiles, refs, tile):
    for (first_tile, count), ref in zip(chunk_tiles, refs):
        if first_tile <= tile < first_tile + count:
            return ref, slice((tile - first_tile) * LANES, (tile - first_tile + 1) * LANES)


def cross_of(cross_links, tiles, tile):
    def link(part, row, column):
        index = link_row(part, row, column) * tiles + tile
        return cross_links[index : index + 1, :]

    return link


def plane_hops(tiles, plane, plane_links, get, extra, put):
    lane = lax.broadcasted_iota(jnp.int32, (ROWS, LANES), 1)
    column = lane % LX
    first_column, last_column = column == 0, column == LX - 1
    below, above = lane < LX, lane >= LANES - LX
    zeros = [jnp.zeros((ROWS, LANES), jnp.float32)] * 6

    def link_of(direction, tile):
        def link(part, row, column_at):
            index = plane * 36 + direction * 18 + link_row(part, row, column_at)
            index = index * tiles + tile
            return plane_links[index : index + 1, :]

        return link

    sums = []
    rolled_in = []
    rolled_out = []
    for tile in range(tiles):
        field = get(tile)
        ahead = [
            jnp.where(last_column, pltpu.roll(f, LX - 1, 1), pltpu.roll(f, LANES - 1, 1))
            for f in field
        ]
        total = [
            jnp.where(first_column, pltpu.roll(f, LANES - LX + 1, 1), pltpu.roll(f, 1, 1))
            for f in adjoint(link_of(0, tile), field, zeros)
        ]
        sums.append(extra(tile, times(link_of(0, tile), ahead, total)))
        rolled_in.append([pltpu.roll(f, LANES - LX, 1) for f in field])
        rolled_out.append(
            [pltpu.roll(f, LX, 1) for f in adjoint(link_of(1, tile), field, zeros)]
        )
    for tile in range(tiles):
        after, before = (tile + 1) % tiles, (tile - 1) % tiles
        ahead = [jnp.where(above, b, a) for a, b in zip(rolled_in[tile], rolled_in[after])]
        total = times(link_of(1, tile), ahead, sums[tile])
        put(
            tile,
            [
                t + jnp.where(below, b, o)
                for t, b, o in zip(total, rolled_out[before], rolled_out[tile])
            ],
        )


def groups_loop(vectors, step, unroll=1):
    def body(group, carry):
        step(pl.ds(pl.multiple_of(group * ROWS, ROWS), ROWS))
        return carry

    lax.fori_loop(0, vectors // ROWS, body, 0, unroll=unroll)


def local_kernel(tiles, chunk_tiles, planes, plane_links, cross_links, inner, *refs):
    outer, outs = refs[: len(chunk_tiles)], refs[-len(planes) :]

    def step(rows):
        def get(plane, tile):
            if plane == 0:
                ref, lanes = inner, slice(tile * LANES, (tile + 1) * LANES)
            else:
                ref, lanes = tile_of(chunk_tiles, outer, tile)
            return [ref[part, rows, lanes] for part in range(6)]

        for plane, out in zip(planes, outs):
            hop = times if plane else adjoint

            def put(tile, total):
                for part in range(6):
                    out[part, rows, tile * LANES : (tile + 1) * LANES] = total[part]

            plane_hops(
                tiles,
                plane,
                plane_links,
                lambda tile: get(plane, tile),
                lambda tile, total: hop(
                    cross_of(cross_links, tiles, tile), get(1 - plane, tile), total
                ),
                put,
            )

    groups_loop(outer[0].shape[1], step)


def inner_hop_kernel(tiles, plane_links, first, out):
    def step(rows):
        def put(tile, total):
            for part in range(6):
                out[part, rows, tile * LANES : (tile + 1) * LANES] = total[part]

        plane_hops(
            tiles,
            0,
            plane_links,
            lambda tile: [
                first[part, rows, tile * LANES : (tile + 1) * LANES] for part in range(6)
            ],
            lambda tile, total: total,
            put,
        )

    groups_loop(out.shape[1], step)


def finish_hop(tiles, chunk, use_low, top_links, low_link, beyond, sums, out, finish):
    first_tile, count = chunk
    for tile in range(count):
        link = z_link(tiles, first_tile + tile, top_links, low_link, use_low)
        lanes = slice(tile * LANES, (tile + 1) * LANES)
        at = (first_tile + tile) * LANES

        def step(rows):
            field = [beyond[part, rows, lanes] for part in range(6)]
            total = [sums[part, rows, at : at + LANES] for part in range(6)]
            total = times(link, field, total)
            for part in range(6):
                out[part, rows, lanes] = finish(total[part], (part, rows, lanes))

        groups_loop(out.shape[1], step, 2)


def inner_edge_kernel(tiles, place_ref, top_links, partner, sums, out):
    finish_hop(
        tiles, (0, tiles), place_ref[1] == 1, top_links, partner_rows(partner, out.shape[1]),
        partner, sums, out, lambda total, index: total * (1.0 / 6.0),
    )


def inner_rest_kernel(tiles, place_ref, top_links, linked, partner, sums, own, out):
    finish_hop(
        tiles, (0, tiles), place_ref[1] == 1, top_links, partner_rows(linked, out.shape[1]),
        partner, sums, out, lambda total, index: total * (2.0 / 6.0) - own[index],
    )


def edge_kernel(tiles, chunk, place_ref, top_links, low_links, beyond, sums, token, out):
    del token
    finish_hop(
        tiles, chunk, place_ref[1] == 0, top_links, low_rows(low_links, tiles), beyond, sums, out,
        lambda total, index: total * (1.0 / 6.0),
    )


def pair_tiles(vectors):
    half = vectors // ROWS // 2
    return [
        (base + left, base + right)
        for base in (0, half)
        for left in range(half)
        for right in range(left, half)
    ]


def add_pairs(field, low, quarks, sums):
    vectors, width = field.shape[1:]
    for colour in range(3):
        real = field[colour].astype(jnp.bfloat16)
        imag = field[3 + colour].astype(jnp.bfloat16)
        for part, (top, bottom) in enumerate(((real, imag), (-imag, real))):
            at = (part * 3 + colour) * width
            low[:vectors, at : at + width] = top
            low[vectors:, at : at + width] = bottom

    combos = pair_tiles(vectors)
    block = ROWS * ROWS
    lefts = sorted({left for left, _ in combos})
    half = len(lefts) // 2
    steps = [lefts[:1], lefts[1:half], lefts[half : half + 1], lefts[half + 1 :]]

    def form(left):
        numbers = [number for number, combo in enumerate(combos) if combo[0] == left]
        for tile in range(width // LANES):
            at = tile * LANES
            lanes = slice(at, at + LANES)
            rights = [
                [
                    field[part, right * ROWS : (right + 1) * ROWS, lanes]
                    for part in range(6)
                ]
                for right in (combos[number][1] for number in numbers)
            ]
            for row in range(0, ROWS, 2):
                pair = [
                    [field[part, index : index + 1, lanes] for part in range(6)]
                    for index in (left * ROWS + row, left * ROWS + row + 1)
                ]
                for number, b in zip(numbers, rights):
                    made = [[] for _ in range(6)]
                    for a in pair:
                        for colour in range(3):
                            x, y = (colour + 1) % 3, (colour + 2) % 3
                            made[colour].append(
                                (a[x] * b[y] - a[3 + x] * b[3 + y])
                                - (a[y] * b[x] - a[3 + y] * b[3 + x])
                            )
                            made[3 + colour].append(
                                (a[x] * b[3 + y] + a[3 + x] * b[y])
                                - (a[y] * b[3 + x] + a[3 + y] * b[x])
                            )
                    start = number * block + row * ROWS
                    for part in range(6):
                        quarks[
                            start : start + 2 * ROWS,
                            part * width + at : part * width + at + LANES,
                        ] = jnp.concatenate(made[part], 0).astype(jnp.bfloat16)

    def multiply(step):
        numbers = [number for number, combo in enumerate(combos) if combo[0] in step]
        rows = slice(numbers[0] * block, (numbers[-1] + 1) * block)
        sums[rows, :] += lax.dot_general(
            quarks[rows, :],
            low[...],
            (((1,), (1,)), ((), ())),
            preferred_element_type=jnp.float32,
        )

    for left in steps[0]:
        form(left)
    for now, later in zip(steps, steps[1:] + [[]]):
        for left in later:
            form(left)
        multiply(now)


def inner_pairs_kernel(tiles, chunk_tiles, cross_links, rest, *refs):
    outer, (sums, field, low, quarks) = refs[: len(chunk_tiles)], refs[len(chunk_tiles) :]
    for tile in range(tiles):
        ref, from_lanes = tile_of(chunk_tiles, outer, tile)
        lanes = slice(tile * LANES, (tile + 1) * LANES)
        link = cross_of(cross_links, tiles, tile)
        found = {
            (part, row, column): jnp.broadcast_to(link(part, row, column), (ROWS, LANES))
            for part in range(2)
            for row in range(3)
            for column in range(3)
        }

        def step(rows):
            source = [ref[part, rows, from_lanes] for part in range(6)]
            zeros = [jnp.zeros((ROWS, LANES), jnp.float32)] * 6
            total = adjoint(lambda *index: found[index], source, zeros)
            for part in range(6):
                field[part, rows, lanes] = rest[part, rows, lanes] + total[part] * (2.0 / 6.0)

        groups_loop(field.shape[1], step, 2)
    sums[...] = jnp.zeros_like(sums)
    width = low.shape[1] // 6
    for start in range(0, field.shape[2], width):
        add_pairs(field.at[:, :, start : start + width], low, quarks, sums)


def outer_pairs_kernel(
    tiles, chunk, place_ref, top_links, low_links, far, partial, own, before, sums, field, low, quarks
):
    finish_hop(
        tiles, chunk, place_ref[1] == 0, top_links, low_rows(low_links, tiles), far, partial, field,
        lambda total, index: total * (2.0 / 6.0) - own[index],
    )
    sums[...] = before[...]
    add_pairs(field, low, quarks, sums)


def arrange(sums, grid, crossed, ordered, factor):
    half = grid.shape[0] // 2
    side = math.isqrt(half)
    vectors = 2 * side
    block = ROWS * ROWS
    for number, (left, right) in enumerate(pair_tiles(vectors)):
        for row in range(ROWS):
            start = number * block + row * ROWS
            at = (left * ROWS + row) * side + right * ROWS % side
            grid[at : at + ROWS, :] = sums[start : start + ROWS, :] * factor
            if left != right:
                at = (right * ROWS + row) * side + left * ROWS % side
                grid[at : at + ROWS, :] = (
                    sums[pl.ds(number * block + row, ROWS, stride=ROWS), :] * -factor
                )
    lane = lax.broadcasted_iota(jnp.int32, (side, 2 * vectors), 1)
    own_half = lane % vectors < side
    per = 2 * vectors // side
    for start in range(0, half, 2 * vectors):
        turned = grid[half + start : half + start + 2 * vectors, :].T
        real, imag = turned[:side], turned[vectors : vectors + side]
        for index in range(per):
            second = start // side + index
            turn = (side - index * side) % (2 * vectors)
            value = jnp.where(
                lane < vectors,
                pltpu.roll(real, turn, 1) if turn else real,
                pltpu.roll(imag, (turn + vectors) % (2 * vectors), 1)
                if (turn + vectors) % (2 * vectors)
                else imag,
            )
            crossed[pl.ds(second, side, stride=side), :] = value
    for start in range(0, half, 2 * vectors):
        turned = grid[start : start + 2 * vectors, :].T
        real, imag = turned[side:vectors], turned[vectors + side :]
        for index in range(per):
            first = start // side + index
            turn = (-index * side) % (2 * vectors)
            value = jnp.where(
                lane < vectors,
                pltpu.roll(real, turn, 1) if turn else real,
                pltpu.roll(imag, (turn + vectors) % (2 * vectors), 1)
                if (turn + vectors) % (2 * vectors)
                else imag,
            )
            value = jnp.where(own_half, -value, crossed[first * side : (first + 1) * side, :])
            pair = first * vectors - first * (first + 1) // 2 + side - first - 1
            ordered[pair : pair + side, :] = value
    for first in range(vectors):
        skip = first % side + 1
        if skip < side:
            pair = first * vectors - first * (first + 1) // 2
            ordered[pair : pair + side - skip, :] = grid[
                first * side + skip : (first + 1) * side, :
            ]


def last_pairs_kernel(
    tiles, chunk, factor, slot_ref, place_ref, top_links, low_links, far, partial, own, before,
    keep, send, sums, field, low, quarks, grid, crossed, ordered,
):
    outer_pairs_kernel(
        tiles, chunk, place_ref, top_links, low_links, far, partial, own, before, sums, field, low,
        quarks,
    )
    arrange(sums, grid, crossed, ordered, factor)
    keep[...] = jnp.zeros_like(keep)
    send[...] = jnp.zeros_like(send)
    my_core = place_ref[1]

    def place(block, carry):
        slot = slot_ref[block]
        owner = slot // CAP
        chip = owner // 2
        value = ordered[pl.ds(pl.multiple_of(block * PB, PB), PB), :]

        @pl.when(owner % 2 == my_core)
        def _():
            keep[chip, slot % CAP] = value

        @pl.when(owner % 2 != my_core)
        def _():
            send[chip, slot % CAP] = value

        return carry

    lax.fori_loop(0, slot_ref.shape[0], place, 0)


def fold_kernel(parts, place_ref, *refs):
    ins, outs = refs[: -2 * len(parts)], refs[-2 * len(parts) :]
    for number, (rows, bit, position) in enumerate(parts):
        kept, received = ins[:2] if len(ins) == 2 else ins[2 * number : 2 * number + 2]
        stay, leave = outs[2 * number : 2 * number + 2]
        mine = lax.rem(lax.div(place_ref[0], 1 << bit), 2)
        for index in range(stay.shape[0]):
            low = index % (1 << position)
            base = (index - low) * 2 + low
            for out, value in ((stay, mine), (leave, 1 - mine)):
                at = base + value * (1 << position)
                out[index] = kept[at, :, rows, :] + received[at, :, rows, :]


def total_kernel(cut, *refs):
    out = refs[-1]
    for number, rows in enumerate(cut):
        out[:, rows, :] = refs[2 * number][0] + refs[2 * number + 1][0]


def on_device(eigen_vectors, link_field, block_slot):
    count = lax.axis_size("brick")
    vectors, sites = eigen_vectors.shape[0], eigen_vectors.shape[-1]
    planes = eigen_vectors.shape[-2]
    tiles = sites // LANES
    half_tiles = tiles // 2
    chunk_tiles = ((0, half_tiles), (half_tiles, tiles - half_tiles))

    def plane_of(width):
        return jax.ShapeDtypeStruct((6, vectors, width), jnp.float32)

    plane = plane_of(sites)
    pieces = [plane_of(size * LANES) for _, size in chunk_tiles]
    plane_bytes = 6 * vectors * sites * 4
    pair_rows = len(pair_tiles(vectors)) * ROWS * ROWS
    up = [(i, (i + 1) % count) for i in range(count)]
    on_chip = [(i, i ^ 1) for i in range(count)]
    off_chip = [(i, (i + 2 * (i % 2) - 1) % count) for i in range(count)]
    me = lax.axis_index("brick")
    place = jnp.stack([me // 2, me % 2]).astype(jnp.int32)
    z_links = jax.ShapeDtypeStruct((18 * tiles, LANES), jnp.float32)

    def call(kernel, shapes, name, smem, *args, limit=32, flops=0, scratch=()):
        many = isinstance(shapes, list)
        return pl.pallas_call(
            kernel,
            out_shape=shapes,
            in_specs=[SMEM] * smem + [VMEM] * (len(args) - smem),
            out_specs=[VMEM] * len(shapes) if many else VMEM,
            scratch_shapes=list(scratch),
            compiler_params=params(limit),
            cost_estimate=cost(flops, 2 * plane_bytes) if flops else None,
            name=name,
        )(*args)

    rows = tile_rows(eigen_vectors)
    outer = call(
        functools.partial(outer_kernel, tiles, chunk_tiles), pieces, "outer", 1, place, rows
    )
    with_links = jax.ShapeDtypeStruct((6, vectors + ROWS, sites), jnp.float32)
    inner, plane_links, cross_links, top_links = call(
        functools.partial(inner_kernel, tiles, vectors),
        [with_links, jax.ShapeDtypeStruct((72 * tiles, LANES), jnp.float32), z_links, z_links],
        "inner", 1, place, rows, tile_rows(link_field), outer[-1],
    )

    def off(fields):
        return [lax.ppermute(field, "brick", off_chip) for field in fields]

    far = off(outer)
    linked = lax.ppermute(inner, "brick", on_chip)
    low_links = lax.ppermute(top_links, "brick", up)
    inner_sums, outer_sums = call(
        functools.partial(local_kernel, tiles, chunk_tiles, (0, 1)), [plane] * 2, "local", 0,
        plane_links, cross_links, inner, *outer, limit=48, flops=4e9,
    )
    first_inner = call(
        functools.partial(inner_edge_kernel, tiles), plane, "inner_edge", 1,
        place, top_links, linked, inner_sums,
    )
    partner = lax.ppermute(first_inner, "brick", on_chip)
    inner_sums = call(
        functools.partial(inner_hop_kernel, tiles), plane, "inner_hop", 0,
        plane_links, first_inner, flops=2e9,
    )
    rest = call(
        functools.partial(inner_rest_kernel, tiles), plane, "inner_rest", 1,
        place, top_links, linked, partner, inner_sums, inner, flops=1e9,
    )
    token = sum(field[0, :ROWS, :LANES] for field in [rest, *far])
    token = lax.ppermute(token, "brick", [(i, i ^ 1) for i in range(count) if i % 4 in (1, 2)])
    first_outer = [
        call(
            functools.partial(edge_kernel, tiles, chunk), piece, "edge", 1,
            place, top_links, low_links, field, outer_sums, token,
        )
        for chunk, piece, field in zip(chunk_tiles, pieces, far)
    ]
    far = off(first_outer)
    def scratch(width):
        return [
            pltpu.VMEM((2 * vectors, 6 * width), jnp.bfloat16),
            pltpu.VMEM((pair_rows, 6 * width), jnp.bfloat16),
        ]

    partial_sums = jax.ShapeDtypeStruct((pair_rows, 2 * vectors), jnp.float32)
    before = call(
        functools.partial(inner_pairs_kernel, tiles, chunk_tiles), partial_sums, "inner_pairs", 0,
        cross_links, rest, *first_outer, limit=48, flops=8e9,
        scratch=[pltpu.VMEM(plane.shape, jnp.float32)] + scratch(2 * LANES),
    )
    (sums,) = call(
        functools.partial(local_kernel, tiles, chunk_tiles, (1,)), [plane], "outer_hop", 0,
        plane_links, cross_links, first_inner, *first_outer, before, limit=48, flops=2e9,
    )
    for chunk, piece, field, own in zip(chunk_tiles[:-1], pieces, far, outer):
        before = pl.pallas_call(
            functools.partial(outer_pairs_kernel, tiles, chunk),
            out_shape=partial_sums,
            in_specs=[SMEM] + [VMEM] * 6,
            out_specs=VMEM,
            scratch_shapes=[pltpu.VMEM(piece.shape, jnp.float32)] + scratch(piece.shape[2]),
            compiler_params=params(48),
            cost_estimate=cost(4e9, 3 * plane_bytes),
            name="outer_pairs",
        )(place, top_links, low_links, field, sums, own, before)
    factor = 1.0 / math.sqrt(3.0 * sites * planes * count)
    chips = count // 2
    half = jax.ShapeDtypeStruct((chips, CAP, PB, 2 * vectors), jnp.float32)
    blocks = vectors * (vectors - 1) // 2
    keep, send = pl.pallas_call(
        functools.partial(last_pairs_kernel, tiles, chunk_tiles[-1], factor),
        out_shape=[half] * 2,
        in_specs=[SMEM] * 2 + [VMEM] * 6,
        out_specs=[VMEM] * 2,
        scratch_shapes=[
            pltpu.VMEM(partial_sums.shape, jnp.float32),
            pltpu.VMEM(pieces[-1].shape, jnp.float32),
        ]
        + scratch(pieces[-1].shape[2])
        + [
            pltpu.VMEM((vectors * vectors // 2, 2 * vectors), jnp.float32),
            pltpu.VMEM((vectors * vectors // 4, 2 * vectors), jnp.float32),
            pltpu.VMEM((blocks, 2 * vectors), jnp.float32),
        ],
        compiler_params=params(48),
        cost_estimate=cost(4e9, 3 * plane_bytes),
        name="last_pairs",
    )(block_slot, place, top_links, low_links, far[-1], sums, outer[-1], before)
    received = lax.ppermute(send, "brick", on_chip)
    bits = chips.bit_length() - 1
    cut = (slice(0, PB // 2), slice(PB // 2, PB))
    orders = [list(range(bits)), list(range(bits))]
    if bits > 1:
        orders[1][:2] = [1, 0]
    remaining = [list(range(bits)), list(range(bits))]

    def fold(halves, stage, rows_of, *pairs):
        parts, shapes = [], []
        for half_at in halves:
            bit = orders[half_at][stage]
            parts.append((rows_of[half_at], bit, remaining[half_at].index(bit)))
            remaining[half_at].remove(bit)
            shape = (2 ** len(remaining[half_at]), CAP, PB // 2, 2 * vectors)
            shapes += [jax.ShapeDtypeStruct(shape, jnp.float32)] * 2
        outs = call(
            functools.partial(fold_kernel, parts), shapes, "fold", 1, place, *pairs
        )
        found = []
        for number, half_at in enumerate(halves):
            bit = orders[half_at][stage]
            route = [(i, i ^ (2 << bit)) for i in range(count)]
            found.append((outs[2 * number], lax.ppermute(outs[2 * number + 1], "brick", route)))
        return found

    whole = (slice(None), slice(None))
    pairs = fold((0, 1), 0, cut, keep, received)
    for stage in range(1, bits):
        pairs = [fold((half_at,), stage, whole, *pairs[half_at])[0] for half_at in range(2)]
    share = jax.ShapeDtypeStruct((CAP, PB, 2 * vectors), jnp.float32)
    return call(
        functools.partial(total_kernel, cut), share, "total", 0, *(ref for pair in pairs for ref in pair)
    )


def solution(mesh):
    return jax.shard_map(
        on_device,
        mesh=mesh,
        in_specs=(
            P(None, None, None, ("cuts", "brick"), None),
            P(None, None, None, None, ("cuts", "brick"), None),
            P(),
        ),
        out_specs=P(("cuts", "brick"), None, None),
        check_vma=False,
    )
```

```python
import functools
import math

import jax
import jax.numpy as jnp
import numpy as np
from jax import lax
from jax.experimental import pallas as pl
from jax.experimental.pallas import tpu as pltpu
from jax.sharding import PartitionSpec as P

PB = 32
CAP = 4
LX = 8
LANES = 128
ROWS = 8
VMEM = pl.BlockSpec(memory_space=pltpu.VMEM)
SMEM = pl.BlockSpec(memory_space=pltpu.SMEM)


def params(limit_mib):
    return pltpu.CompilerParams(vmem_limit_bytes=limit_mib * 1024 * 1024)


def cost(flops, bytes_accessed):
    return pl.CostEstimate(
        flops=int(flops), bytes_accessed=int(bytes_accessed), transcendentals=0
    )


def tile_rows(array):
    planes, sites = array.shape[-2:]
    tiles = sites // LANES
    lead = math.prod(array.shape[:-2])
    array = array.reshape(lead, planes, tiles, LANES).transpose(0, 2, 1, 3)
    return array.reshape(lead * tiles * planes, LANES)


def times(link, field, total):
    total = list(total)
    for out_row in range(3):
        for in_row in range(3):
            real, imag = link(0, out_row, in_row), link(1, out_row, in_row)
            f_real, f_imag = field[in_row], field[3 + in_row]
            total[out_row] = total[out_row] + real * f_real - imag * f_imag
            total[3 + out_row] = total[3 + out_row] + real * f_imag + imag * f_real
    return total


def adjoint(link, field, total):
    total = list(total)
    for out_row in range(3):
        for in_row in range(3):
            real, imag = link(0, in_row, out_row), link(1, in_row, out_row)
            f_real, f_imag = field[in_row], field[3 + in_row]
            total[out_row] = total[out_row] + real * f_real + imag * f_imag
            total[3 + out_row] = total[3 + out_row] + real * f_imag - imag * f_real
    return total


def link_row(part, row, column):
    return (part * 3 + row) * 3 + column


def plane_rows(x_ref, part, tile, tiles, vectors, lower_core, inner):
    start = (part * tiles + tile) * 2
    plane_0, plane_1 = (
        x_ref[pl.ds(start + plane, vectors, stride=6 * tiles * 2), :] for plane in range(2)
    )
    if inner:
        return jnp.where(lower_core, plane_1, plane_0)
    return jnp.where(lower_core, plane_0, plane_1)


def outer_kernel(tiles, chunk_tiles, place_ref, x_ref, *outer):
    lower_core = place_ref[1] == 0
    for (first_tile, count), out in zip(chunk_tiles, outer):
        for part in range(6):
            for tile in range(count):
                at = tile * LANES
                out[part, :, at : at + LANES] = plane_rows(
                    x_ref, part, first_tile + tile, tiles, out.shape[1], lower_core, False
                )


def inner_kernel(
    tiles, vectors, place_ref, x_ref, link_ref, after, inner, plane_links, cross_links, top_links
):
    del after
    lower_core = place_ref[1] == 0
    for part in range(6):
        for tile in range(tiles):
            inner[part, :vectors, tile * LANES : (tile + 1) * LANES] = plane_rows(
                x_ref, part, tile, tiles, vectors, lower_core, True
            )
    inner[:, vectors:, :] = jnp.zeros_like(inner[:, vectors:, :])
    for index in range(36 * tiles):
        plane_0, plane_1 = (
            link_ref[index * 2 + plane : index * 2 + plane + 1, :] for plane in range(2)
        )
        plane_links[index : index + 1, :] = jnp.where(lower_core, plane_1, plane_0)
        index += 36 * tiles
        plane_links[index : index + 1, :] = jnp.where(lower_core, plane_0, plane_1)
    for part in range(2):
        for row in range(3):
            for column in range(3):
                for tile in range(tiles):
                    straight = ((36 + link_row(part, row, column)) * tiles + tile) * 2
                    turned = ((36 + link_row(part, column, row)) * tiles + tile) * 2
                    number = link_row(part, row, column)
                    index = number * tiles + tile
                    sign = -1.0 if part else 1.0
                    cross_links[index : index + 1, :] = jnp.where(
                        lower_core,
                        link_ref[straight : straight + 1, :],
                        sign * link_ref[turned : turned + 1, :],
                    )
                    top = link_ref[straight + 1 : straight + 2, :]
                    top_links[index : index + 1, :] = top
                    inner[
                        number // 3,
                        vectors + number % 3 : vectors + number % 3 + 1,
                        tile * LANES : (tile + 1) * LANES,
                    ] = top


def z_link(tiles, tile, top_links, low_link, use_low):
    found = {}
    for part in range(2):
        for row in range(3):
            for column in range(3):
                straight = link_row(part, row, column) * tiles + tile
                sign = -1.0 if part else 1.0
                value = jnp.where(
                    use_low,
                    sign * low_link(part, column, row, tile),
                    top_links[straight : straight + 1, :],
                )
                found[part, row, column] = jnp.broadcast_to(value, (ROWS, LANES))
    return lambda *index: found[index]


def low_rows(low_links, tiles):
    def low_link(part, row, column, tile):
        index = link_row(part, row, column) * tiles + tile
        return low_links[index : index + 1, :]

    return low_link


def partner_rows(partner, vectors):
    def low_link(part, row, column, tile):
        number = link_row(part, row, column)
        at = vectors + number % 3
        return partner[number // 3, at : at + 1, tile * LANES : (tile + 1) * LANES]

    return low_link


def tile_of(chunk_tiles, refs, tile):
    for (first_tile, count), ref in zip(chunk_tiles, refs):
        if first_tile <= tile < first_tile + count:
            return ref, slice((tile - first_tile) * LANES, (tile - first_tile + 1) * LANES)


def cross_of(cross_links, tiles, tile):
    def link(part, row, column):
        index = link_row(part, row, column) * tiles + tile
        return cross_links[index : index + 1, :]

    return link


def plane_hops(tiles, plane, plane_links, get, extra, put):
    lane = lax.broadcasted_iota(jnp.int32, (ROWS, LANES), 1)
    column = lane % LX
    first_column, last_column = column == 0, column == LX - 1
    below, above = lane < LX, lane >= LANES - LX
    zeros = [jnp.zeros((ROWS, LANES), jnp.float32)] * 6

    def link_of(direction, tile):
        def link(part, row, column_at):
            index = plane * 36 + direction * 18 + link_row(part, row, column_at)
            index = index * tiles + tile
            return plane_links[index : index + 1, :]

        return link

    sums = []
    rolled_in = []
    rolled_out = []
    for tile in range(tiles):
        field = get(tile)
        ahead = [
            jnp.where(last_column, pltpu.roll(f, LX - 1, 1), pltpu.roll(f, LANES - 1, 1))
            for f in field
        ]
        total = [
            jnp.where(first_column, pltpu.roll(f, LANES - LX + 1, 1), pltpu.roll(f, 1, 1))
            for f in adjoint(link_of(0, tile), field, zeros)
        ]
        sums.append(extra(tile, times(link_of(0, tile), ahead, total)))
        rolled_in.append([pltpu.roll(f, LANES - LX, 1) for f in field])
        rolled_out.append(
            [pltpu.roll(f, LX, 1) for f in adjoint(link_of(1, tile), field, zeros)]
        )
    for tile in range(tiles):
        after, before = (tile + 1) % tiles, (tile - 1) % tiles
        ahead = [jnp.where(above, b, a) for a, b in zip(rolled_in[tile], rolled_in[after])]
        total = times(link_of(1, tile), ahead, sums[tile])
        put(
            tile,
            [
                t + jnp.where(below, b, o)
                for t, b, o in zip(total, rolled_out[before], rolled_out[tile])
            ],
        )


def groups_loop(vectors, step, unroll=1):
    def body(group, carry):
        step(pl.ds(pl.multiple_of(group * ROWS, ROWS), ROWS))
        return carry

    lax.fori_loop(0, vectors // ROWS, body, 0, unroll=unroll)


def local_kernel(tiles, chunk_tiles, planes, plane_links, cross_links, inner, *refs):
    outer, outs = refs[: len(chunk_tiles)], refs[-len(planes) :]

    def step(rows):
        def get(plane, tile):
            if plane == 0:
                ref, lanes = inner, slice(tile * LANES, (tile + 1) * LANES)
            else:
                ref, lanes = tile_of(chunk_tiles, outer, tile)
            return [ref[part, rows, lanes] for part in range(6)]

        for plane, out in zip(planes, outs):
            hop = times if plane else adjoint

            def put(tile, total):
                for part in range(6):
                    out[part, rows, tile * LANES : (tile + 1) * LANES] = total[part]

            plane_hops(
                tiles,
                plane,
                plane_links,
                lambda tile: get(plane, tile),
                lambda tile, total: hop(
                    cross_of(cross_links, tiles, tile), get(1 - plane, tile), total
                ),
                put,
            )

    groups_loop(outer[0].shape[1], step)


def finish_hop(tiles, chunk, use_low, top_links, low_link, beyond, sums, out, finish):
    first_tile, count = chunk
    for tile in range(count):
        link = z_link(tiles, first_tile + tile, top_links, low_link, use_low)
        lanes = slice(tile * LANES, (tile + 1) * LANES)
        at = (first_tile + tile) * LANES

        def step(rows):
            field = [beyond[part, rows, lanes] for part in range(6)]
            total = [sums[part, rows, at : at + LANES] for part in range(6)]
            total = times(link, field, total)
            for part in range(6):
                out[part, rows, lanes] = finish(total[part], (part, rows, lanes))

        groups_loop(out.shape[1], step, 2)


def inner_step_kernel(tiles, place_ref, top_links, plane_links, partner, sums, first, out):
    finish_hop(
        tiles, (0, tiles), place_ref[1] == 1, top_links, partner_rows(partner, first.shape[1]),
        partner, sums, first, lambda total, index: total * (1.0 / 6.0),
    )

    def step(rows):
        def put(tile, total):
            for part in range(6):
                out[part, rows, tile * LANES : (tile + 1) * LANES] = total[part]

        plane_hops(
            tiles,
            0,
            plane_links,
            lambda tile: [
                first[part, rows, tile * LANES : (tile + 1) * LANES] for part in range(6)
            ],
            lambda tile, total: total,
            put,
        )

    groups_loop(out.shape[1], step)


def edge_kernel(
    tiles, chunk, place_ref, top_links, low_links, beyond, sums, token, *refs
):
    out = refs[1 if len(refs) > 1 else 0]
    del token, refs
    finish_hop(
        tiles, chunk, place_ref[1] == 0, top_links, low_rows(low_links, tiles), beyond, sums, out,
        lambda total, index: total * (1.0 / 6.0),
    )


def pair_tiles(vectors):
    half = vectors // ROWS // 2
    return [
        (base + left, base + right)
        for base in (0, half)
        for left in range(half)
        for right in range(left, half)
    ]


def add_pairs(field, low, quarks, sums):
    vectors, width = field.shape[1:]
    for colour in range(3):
        real = field[colour].astype(jnp.bfloat16)
        imag = field[3 + colour].astype(jnp.bfloat16)
        for part, (top, bottom) in enumerate(((real, imag), (-imag, real))):
            at = (part * 3 + colour) * width
            low[:vectors, at : at + width] = top
            low[vectors:, at : at + width] = bottom

    combos = pair_tiles(vectors)
    block = ROWS * ROWS
    lefts = sorted({left for left, _ in combos})
    half = len(lefts) // 2
    steps = [lefts[:1], lefts[1:half], lefts[half : half + 1], lefts[half + 1 :]]

    def form(left):
        numbers = [number for number, combo in enumerate(combos) if combo[0] == left]
        for tile in range(width // LANES):
            at = tile * LANES
            lanes = slice(at, at + LANES)
            rights = [
                [
                    field[part, right * ROWS : (right + 1) * ROWS, lanes]
                    for part in range(6)
                ]
                for right in (combos[number][1] for number in numbers)
            ]
            for row in range(0, ROWS, 2):
                pair = [
                    [field[part, index : index + 1, lanes] for part in range(6)]
                    for index in (left * ROWS + row, left * ROWS + row + 1)
                ]
                for number, b in zip(numbers, rights):
                    made = [[] for _ in range(6)]
                    for a in pair:
                        for colour in range(3):
                            x, y = (colour + 1) % 3, (colour + 2) % 3
                            made[colour].append(
                                (a[x] * b[y] - a[3 + x] * b[3 + y])
                                - (a[y] * b[x] - a[3 + y] * b[3 + x])
                            )
                            made[3 + colour].append(
                                (a[x] * b[3 + y] + a[3 + x] * b[y])
                                - (a[y] * b[3 + x] + a[3 + y] * b[x])
                            )
                    start = number * block + row * ROWS
                    for part in range(6):
                        quarks[
                            start : start + 2 * ROWS,
                            part * width + at : part * width + at + LANES,
                        ] = jnp.concatenate(made[part], 0).astype(jnp.bfloat16)

    def multiply(step):
        numbers = [number for number, combo in enumerate(combos) if combo[0] in step]
        rows = slice(numbers[0] * block, (numbers[-1] + 1) * block)
        sums[rows, :] += lax.dot_general(
            quarks[rows, :],
            low[...],
            (((1,), (1,)), ((), ())),
            preferred_element_type=jnp.float32,
        )

    for left in steps[0]:
        form(left)
    for now, later in zip(steps, steps[1:] + [[]]):
        for left in later:
            form(left)
        multiply(now)


def inner_pairs_kernel(
    tiles, chunk_tiles, place_ref, top_links, cross_links, linked, partner, partial, own, *refs
):
    outer, (sums, field, low, quarks) = refs[: len(chunk_tiles)], refs[len(chunk_tiles) :]
    vectors = field.shape[1]
    for tile in range(tiles):
        ref, from_lanes = tile_of(chunk_tiles, outer, tile)
        lanes = slice(tile * LANES, (tile + 1) * LANES)
        link = z_link(
            tiles, tile, top_links, partner_rows(linked, vectors), place_ref[1] == 1
        )
        cross = cross_of(cross_links, tiles, tile)

        def step(rows):
            total = [partial[part, rows, lanes] for part in range(6)]
            total = adjoint(cross, [ref[part, rows, from_lanes] for part in range(6)], total)
            total = times(link, [partner[part, rows, lanes] for part in range(6)], total)
            for part in range(6):
                field[part, rows, lanes] = total[part] * (2.0 / 6.0) - own[part, rows, lanes]

        groups_loop(vectors, step, 2)
    sums[...] = jnp.zeros_like(sums)
    width = low.shape[1] // 6
    for start in range(0, field.shape[2], width):
        add_pairs(field.at[:, :, start : start + width], low, quarks, sums)


def outer_pairs_kernel(
    tiles, chunk, place_ref, top_links, low_links, far, partial, own, before, sums, field, low, quarks
):
    finish_hop(
        tiles, chunk, place_ref[1] == 0, top_links, low_rows(low_links, tiles), far, partial, field,
        lambda total, index: total * (2.0 / 6.0) - own[index],
    )
    sums[...] = before[...]
    add_pairs(field, low, quarks, sums)


def arrange(sums, grid, crossed, ordered, factor):
    half = grid.shape[0] // 2
    side = math.isqrt(half)
    vectors = 2 * side
    block = ROWS * ROWS
    for number, (left, right) in enumerate(pair_tiles(vectors)):
        for row in range(ROWS):
            start = number * block + row * ROWS
            at = (left * ROWS + row) * side + right * ROWS % side
            grid[at : at + ROWS, :] = sums[start : start + ROWS, :] * factor
            if left != right:
                at = (right * ROWS + row) * side + left * ROWS % side
                grid[at : at + ROWS, :] = (
                    sums[pl.ds(number * block + row, ROWS, stride=ROWS), :] * -factor
                )
    lane = lax.broadcasted_iota(jnp.int32, (side, 2 * vectors), 1)
    own_half = lane % vectors < side
    per = 2 * vectors // side
    for start in range(0, half, 2 * vectors):
        turned = grid[half + start : half + start + 2 * vectors, :].T
        real, imag = turned[:side], turned[vectors : vectors + side]
        for index in range(per):
            second = start // side + index
            turn = (side - index * side) % (2 * vectors)
            value = jnp.where(
                lane < vectors,
                pltpu.roll(real, turn, 1) if turn else real,
                pltpu.roll(imag, (turn + vectors) % (2 * vectors), 1)
                if (turn + vectors) % (2 * vectors)
                else imag,
            )
            crossed[pl.ds(second, side, stride=side), :] = value
    for start in range(0, half, 2 * vectors):
        turned = grid[start : start + 2 * vectors, :].T
        real, imag = turned[side:vectors], turned[vectors + side :]
        for index in range(per):
            first = start // side + index
            turn = (-index * side) % (2 * vectors)
            value = jnp.where(
                lane < vectors,
                pltpu.roll(real, turn, 1) if turn else real,
                pltpu.roll(imag, (turn + vectors) % (2 * vectors), 1)
                if (turn + vectors) % (2 * vectors)
                else imag,
            )
            value = jnp.where(own_half, -value, crossed[first * side : (first + 1) * side, :])
            pair = first * vectors - first * (first + 1) // 2 + side - first - 1
            ordered[pair : pair + side, :] = value
    for first in range(vectors):
        skip = first % side + 1
        if skip < side:
            pair = first * vectors - first * (first + 1) // 2
            ordered[pair : pair + side - skip, :] = grid[
                first * side + skip : (first + 1) * side, :
            ]


def last_pairs_kernel(
    tiles, chunk, factor, slot_ref, place_ref, top_links, low_links, far, partial, own, before,
    keep, send, sums, field, low, quarks, grid, crossed, ordered,
):
    outer_pairs_kernel(
        tiles, chunk, place_ref, top_links, low_links, far, partial, own, before, sums, field, low,
        quarks,
    )
    arrange(sums, grid, crossed, ordered, factor)
    keep[...] = jnp.zeros_like(keep)
    send[...] = jnp.zeros_like(send)
    my_core = place_ref[1]

    def place(block, carry):
        slot = slot_ref[block]
        owner = slot // CAP
        away = jnp.bitwise_xor(owner // 2, place_ref[0])
        value = ordered[pl.ds(pl.multiple_of(block * PB, PB), PB), :]

        @pl.when(owner % 2 == my_core)
        def _():
            keep[away, slot % CAP] = value

        @pl.when(owner % 2 != my_core)
        def _():
            send[away, slot % CAP] = value

        return carry

    lax.fori_loop(0, slot_ref.shape[0], place, 0)


def combine_kernel(kept, received, *outs):
    for away, out in enumerate(outs):
        out[...] = kept[away] + received[away]


def total_kernel(*refs):
    total = refs[0][...]
    for ref in refs[1:-1]:
        total = total + ref[...]
    refs[-1][...] = total


def on_device(eigen_vectors, link_field, block_slot):
    count = lax.axis_size("brick")
    vectors, sites = eigen_vectors.shape[0], eigen_vectors.shape[-1]
    planes = eigen_vectors.shape[-2]
    tiles = sites // LANES
    half_tiles = tiles // 2
    chunk_tiles = ((0, half_tiles), (half_tiles, tiles - half_tiles))

    def plane_of(width):
        return jax.ShapeDtypeStruct((6, vectors, width), jnp.float32)

    plane = plane_of(sites)
    pieces = [plane_of(size * LANES) for _, size in chunk_tiles]
    plane_bytes = 6 * vectors * sites * 4
    pair_rows = len(pair_tiles(vectors)) * ROWS * ROWS
    up = [(i, (i + 1) % count) for i in range(count)]
    on_chip = [(i, i ^ 1) for i in range(count)]
    off_chip = [(i, (i + 2 * (i % 2) - 1) % count) for i in range(count)]
    me = lax.axis_index("brick")
    place = jnp.stack([me // 2, me % 2]).astype(jnp.int32)
    z_links = jax.ShapeDtypeStruct((18 * tiles, LANES), jnp.float32)

    def call(kernel, shapes, name, smem, *args, limit=32, flops=0, scratch=()):
        many = isinstance(shapes, list)
        return pl.pallas_call(
            kernel,
            out_shape=shapes,
            in_specs=[SMEM] * smem + [VMEM] * (len(args) - smem),
            out_specs=[VMEM] * len(shapes) if many else VMEM,
            scratch_shapes=list(scratch),
            compiler_params=params(limit),
            cost_estimate=cost(flops, 2 * plane_bytes) if flops else None,
            name=name,
        )(*args)

    rows = tile_rows(eigen_vectors)
    outer = call(
        functools.partial(outer_kernel, tiles, chunk_tiles), pieces, "outer", 1, place, rows
    )
    with_links = jax.ShapeDtypeStruct((6, vectors + ROWS, sites), jnp.float32)
    inner, plane_links, cross_links, top_links = call(
        functools.partial(inner_kernel, tiles, vectors),
        [with_links, jax.ShapeDtypeStruct((72 * tiles, LANES), jnp.float32), z_links, z_links],
        "inner", 1, place, rows, tile_rows(link_field), outer[-1],
    )

    def off(fields):
        return [lax.ppermute(field, "brick", off_chip) for field in fields]

    far = off(outer)
    linked = lax.ppermute(inner, "brick", on_chip)
    low_links = lax.ppermute(top_links, "brick", up)
    inner_sums, outer_sums = call(
        functools.partial(local_kernel, tiles, chunk_tiles, (0, 1)), [plane] * 2, "local", 0,
        plane_links, cross_links, inner, *outer, limit=48, flops=4e9,
    )
    first_inner, inner_sums = call(
        functools.partial(inner_step_kernel, tiles), [plane] * 2, "inner_step", 1,
        place, top_links, plane_links, linked, inner_sums,
    )
    token = sum(field[0, :ROWS, :LANES] for field in [inner_sums, *far])
    token = lax.ppermute(token, "brick", [(i, i ^ 1) for i in range(count) if i % 4 in (1, 2)])
    first_outer = []
    for chunk, piece, field in zip(chunk_tiles, pieces, far):
        args = (place, top_links, low_links, field, outer_sums, token)
        if first_outer:
            first_outer.append(
                call(functools.partial(edge_kernel, tiles, chunk), piece, "edge", 1, *args)
            )
            continue
        first, first_inner = pl.pallas_call(
            functools.partial(edge_kernel, tiles, chunk),
            out_shape=[piece, plane],
            in_specs=[SMEM] + [VMEM] * 5 + [pl.BlockSpec(memory_space=pl.ANY)],
            out_specs=[VMEM, pl.BlockSpec(memory_space=pl.ANY)],
            input_output_aliases={6: 1},
            compiler_params=params(32),
            name="edge",
        )(*args, first_inner)
        first_outer.append(first)
    partner = lax.ppermute(first_inner, "brick", on_chip)
    far = off(first_outer)
    def scratch(width):
        return [
            pltpu.VMEM((2 * vectors, 6 * width), jnp.bfloat16),
            pltpu.VMEM((pair_rows, 6 * width), jnp.bfloat16),
        ]

    partial_sums = jax.ShapeDtypeStruct((pair_rows, 2 * vectors), jnp.float32)
    before = call(
        functools.partial(inner_pairs_kernel, tiles, chunk_tiles), partial_sums, "inner_pairs", 1,
        place, top_links, cross_links, linked, partner, inner_sums, inner, *first_outer, limit=48, flops=8e9,
        scratch=[pltpu.VMEM(plane.shape, jnp.float32)] + scratch(2 * LANES),
    )
    (sums,) = call(
        functools.partial(local_kernel, tiles, chunk_tiles, (1,)), [plane], "outer_hop", 0,
        plane_links, cross_links, first_inner, *first_outer, before, limit=48, flops=2e9,
    )
    for chunk, piece, field, own in zip(chunk_tiles[:-1], pieces, far, outer):
        before = pl.pallas_call(
            functools.partial(outer_pairs_kernel, tiles, chunk),
            out_shape=partial_sums,
            in_specs=[SMEM] + [VMEM] * 6,
            out_specs=VMEM,
            scratch_shapes=[pltpu.VMEM(piece.shape, jnp.float32)] + scratch(piece.shape[2]),
            compiler_params=params(48),
            cost_estimate=cost(4e9, 3 * plane_bytes),
            name="outer_pairs",
        )(place, top_links, low_links, field, sums, own, before)
    factor = 1.0 / math.sqrt(3.0 * sites * planes * count)
    chips = count // 2
    half = jax.ShapeDtypeStruct((chips, CAP, PB, 2 * vectors), jnp.float32)
    blocks = vectors * (vectors - 1) // 2
    keep, send = pl.pallas_call(
        functools.partial(last_pairs_kernel, tiles, chunk_tiles[-1], factor),
        out_shape=[half] * 2,
        in_specs=[SMEM] * 2 + [VMEM] * 6,
        out_specs=[VMEM] * 2,
        scratch_shapes=[
            pltpu.VMEM(partial_sums.shape, jnp.float32),
            pltpu.VMEM(pieces[-1].shape, jnp.float32),
        ]
        + scratch(pieces[-1].shape[2])
        + [
            pltpu.VMEM((vectors * vectors // 2, 2 * vectors), jnp.float32),
            pltpu.VMEM((vectors * vectors // 4, 2 * vectors), jnp.float32),
            pltpu.VMEM((blocks, 2 * vectors), jnp.float32),
        ],
        compiler_params=params(48),
        cost_estimate=cost(4e9, 3 * plane_bytes),
        name="last_pairs",
    )(block_slot, place, top_links, low_links, far[-1], sums, outer[-1], before)
    received = lax.ppermute(send, "brick", on_chip)
    share = jax.ShapeDtypeStruct((CAP, PB, 2 * vectors), jnp.float32)
    shares = call(combine_kernel, [share] * chips, "combine", 0, keep, received)
    arrived = [
        lax.ppermute(shares[away], "brick", [(i, i ^ (2 * away)) for i in range(count)])
        for away in reversed(range(1, chips))
    ]
    return call(total_kernel, share, "total", 0, shares[0], *arrived)


def solution(mesh):
    return jax.shard_map(
        on_device,
        mesh=mesh,
        in_specs=(
            P(None, None, None, ("cuts", "brick"), None),
            P(None, None, None, None, ("cuts", "brick"), None),
            P(),
        ),
        out_specs=P(("cuts", "brick"), None, None),
        check_vma=False,
    )
```

```python
import functools
import math

import jax
import jax.numpy as jnp
import numpy as np
from jax import lax
from jax.experimental import pallas as pl
from jax.experimental.pallas import tpu as pltpu
from jax.sharding import PartitionSpec as P

PB = 32
CAP = 4
LX = 8
LANES = 128
ROWS = 8
VMEM = pl.BlockSpec(memory_space=pltpu.VMEM)
SMEM = pl.BlockSpec(memory_space=pltpu.SMEM)


def params(limit_mib):
    return pltpu.CompilerParams(vmem_limit_bytes=limit_mib * 1024 * 1024)


def cost(flops, bytes_accessed):
    return pl.CostEstimate(
        flops=int(flops), bytes_accessed=int(bytes_accessed), transcendentals=0
    )


def tile_rows(array):
    planes, sites = array.shape[-2:]
    tiles = sites // LANES
    lead = math.prod(array.shape[:-2])
    array = array.reshape(lead, planes, tiles, LANES).transpose(0, 2, 1, 3)
    return array.reshape(lead * tiles * planes, LANES)


def times(link, field, total):
    total = list(total)
    for out_row in range(3):
        for in_row in range(3):
            real, imag = link(0, out_row, in_row), link(1, out_row, in_row)
            f_real, f_imag = field[in_row], field[3 + in_row]
            total[out_row] = total[out_row] + real * f_real - imag * f_imag
            total[3 + out_row] = total[3 + out_row] + real * f_imag + imag * f_real
    return total


def adjoint(link, field, total):
    total = list(total)
    for out_row in range(3):
        for in_row in range(3):
            real, imag = link(0, in_row, out_row), link(1, in_row, out_row)
            f_real, f_imag = field[in_row], field[3 + in_row]
            total[out_row] = total[out_row] + real * f_real + imag * f_imag
            total[3 + out_row] = total[3 + out_row] + real * f_imag - imag * f_real
    return total


def link_row(part, row, column):
    return (part * 3 + row) * 3 + column


def plane_rows(x_ref, part, tile, tiles, vectors, lower_core, inner):
    start = (part * tiles + tile) * 2
    plane_0, plane_1 = (
        x_ref[pl.ds(start + plane, vectors, stride=6 * tiles * 2), :] for plane in range(2)
    )
    if inner:
        return jnp.where(lower_core, plane_1, plane_0)
    return jnp.where(lower_core, plane_0, plane_1)


def outer_kernel(tiles, chunk_tiles, place_ref, x_ref, *outer):
    lower_core = place_ref[1] == 0
    for (first_tile, count), out in zip(chunk_tiles, outer):
        for part in range(6):
            for tile in range(count):
                at = tile * LANES
                out[part, :, at : at + LANES] = plane_rows(
                    x_ref, part, first_tile + tile, tiles, out.shape[1], lower_core, False
                )


def inner_kernel(
    tiles, vectors, place_ref, x_ref, link_ref, after, inner, plane_links, cross_links, top_links
):
    del after
    lower_core = place_ref[1] == 0
    for part in range(6):
        for tile in range(tiles):
            inner[part, :vectors, tile * LANES : (tile + 1) * LANES] = plane_rows(
                x_ref, part, tile, tiles, vectors, lower_core, True
            )
    inner[:, vectors:, :] = jnp.zeros_like(inner[:, vectors:, :])
    for index in range(36 * tiles):
        plane_0, plane_1 = (
            link_ref[index * 2 + plane : index * 2 + plane + 1, :] for plane in range(2)
        )
        plane_links[index : index + 1, :] = jnp.where(lower_core, plane_1, plane_0)
        index += 36 * tiles
        plane_links[index : index + 1, :] = jnp.where(lower_core, plane_0, plane_1)
    for part in range(2):
        for row in range(3):
            for column in range(3):
                for tile in range(tiles):
                    straight = ((36 + link_row(part, row, column)) * tiles + tile) * 2
                    turned = ((36 + link_row(part, column, row)) * tiles + tile) * 2
                    number = link_row(part, row, column)
                    index = number * tiles + tile
                    sign = -1.0 if part else 1.0
                    cross_links[index : index + 1, :] = jnp.where(
                        lower_core,
                        link_ref[straight : straight + 1, :],
                        sign * link_ref[turned : turned + 1, :],
                    )
                    top = link_ref[straight + 1 : straight + 2, :]
                    top_links[index : index + 1, :] = top
                    inner[
                        number // 3,
                        vectors + number % 3 : vectors + number % 3 + 1,
                        tile * LANES : (tile + 1) * LANES,
                    ] = top


def z_link(tiles, tile, top_links, low_link, use_low):
    found = {}
    for part in range(2):
        for row in range(3):
            for column in range(3):
                straight = link_row(part, row, column) * tiles + tile
                sign = -1.0 if part else 1.0
                value = jnp.where(
                    use_low,
                    sign * low_link(part, column, row, tile),
                    top_links[straight : straight + 1, :],
                )
                found[part, row, column] = jnp.broadcast_to(value, (ROWS, LANES))
    return lambda *index: found[index]


def low_rows(low_links, tiles):
    def low_link(part, row, column, tile):
        index = link_row(part, row, column) * tiles + tile
        return low_links[index : index + 1, :]

    return low_link


def partner_rows(partner, vectors):
    def low_link(part, row, column, tile):
        number = link_row(part, row, column)
        at = vectors + number % 3
        return partner[number // 3, at : at + 1, tile * LANES : (tile + 1) * LANES]

    return low_link


def tile_of(chunk_tiles, refs, tile):
    for (first_tile, count), ref in zip(chunk_tiles, refs):
        if first_tile <= tile < first_tile + count:
            return ref, slice((tile - first_tile) * LANES, (tile - first_tile + 1) * LANES)


def cross_of(cross_links, tiles, tile):
    def link(part, row, column):
        index = link_row(part, row, column) * tiles + tile
        return cross_links[index : index + 1, :]

    return link


def plane_hops(tiles, plane, plane_links, get, extra, put):
    lane = lax.broadcasted_iota(jnp.int32, (ROWS, LANES), 1)
    column = lane % LX
    first_column, last_column = column == 0, column == LX - 1
    below, above = lane < LX, lane >= LANES - LX
    zeros = [jnp.zeros((ROWS, LANES), jnp.float32)] * 6

    def link_of(direction, tile):
        def link(part, row, column_at):
            index = plane * 36 + direction * 18 + link_row(part, row, column_at)
            index = index * tiles + tile
            return plane_links[index : index + 1, :]

        return link

    sums = []
    rolled_in = []
    rolled_out = []
    for tile in range(tiles):
        field = get(tile)
        ahead = [
            jnp.where(last_column, pltpu.roll(f, LX - 1, 1), pltpu.roll(f, LANES - 1, 1))
            for f in field
        ]
        total = [
            jnp.where(first_column, pltpu.roll(f, LANES - LX + 1, 1), pltpu.roll(f, 1, 1))
            for f in adjoint(link_of(0, tile), field, zeros)
        ]
        sums.append(extra(tile, times(link_of(0, tile), ahead, total)))
        rolled_in.append([pltpu.roll(f, LANES - LX, 1) for f in field])
        rolled_out.append(
            [pltpu.roll(f, LX, 1) for f in adjoint(link_of(1, tile), field, zeros)]
        )
    for tile in range(tiles):
        after, before = (tile + 1) % tiles, (tile - 1) % tiles
        ahead = [jnp.where(above, b, a) for a, b in zip(rolled_in[tile], rolled_in[after])]
        total = times(link_of(1, tile), ahead, sums[tile])
        put(
            tile,
            [
                t + jnp.where(below, b, o)
                for t, b, o in zip(total, rolled_out[before], rolled_out[tile])
            ],
        )


def groups_loop(vectors, step, unroll=1):
    def body(group, carry):
        step(pl.ds(pl.multiple_of(group * ROWS, ROWS), ROWS))
        return carry

    lax.fori_loop(0, vectors // ROWS, body, 0, unroll=unroll)


def local_kernel(tiles, chunk_tiles, planes, plane_links, cross_links, inner, *refs):
    outer, outs = refs[: len(chunk_tiles)], refs[-len(planes) :]

    def step(rows):
        def get(plane, tile):
            if plane == 0:
                ref, lanes = inner, slice(tile * LANES, (tile + 1) * LANES)
            else:
                ref, lanes = tile_of(chunk_tiles, outer, tile)
            return [ref[part, rows, lanes] for part in range(6)]

        for plane, out in zip(planes, outs):
            hop = times if plane else adjoint

            def put(tile, total):
                for part in range(6):
                    out[part, rows, tile * LANES : (tile + 1) * LANES] = total[part]

            plane_hops(
                tiles,
                plane,
                plane_links,
                lambda tile: get(plane, tile),
                lambda tile, total: hop(
                    cross_of(cross_links, tiles, tile), get(1 - plane, tile), total
                ),
                put,
            )

    groups_loop(outer[0].shape[1], step)


def finish_hop(tiles, chunk, use_low, top_links, low_link, beyond, sums, out, finish):
    first_tile, count = chunk
    for tile in range(count):
        link = z_link(tiles, first_tile + tile, top_links, low_link, use_low)
        lanes = slice(tile * LANES, (tile + 1) * LANES)
        at = (first_tile + tile) * LANES

        def step(rows):
            field = [beyond[part, rows, lanes] for part in range(6)]
            total = [sums[part, rows, at : at + LANES] for part in range(6)]
            total = times(link, field, total)
            for part in range(6):
                out[part, rows, lanes] = finish(total[part], (part, rows, lanes))

        groups_loop(out.shape[1], step, 2)


def inner_step_kernel(tiles, place_ref, top_links, plane_links, partner, sums, first, out):
    finish_hop(
        tiles, (0, tiles), place_ref[1] == 1, top_links, partner_rows(partner, first.shape[1]),
        partner, sums, first, lambda total, index: total * (1.0 / 6.0),
    )

    def step(rows):
        def put(tile, total):
            for part in range(6):
                out[part, rows, tile * LANES : (tile + 1) * LANES] = total[part]

        plane_hops(
            tiles,
            0,
            plane_links,
            lambda tile: [
                first[part, rows, tile * LANES : (tile + 1) * LANES] for part in range(6)
            ],
            lambda tile, total: total,
            put,
        )

    groups_loop(out.shape[1], step)


def edge_kernel(
    tiles, chunk, place_ref, top_links, low_links, beyond, sums, token, *refs
):
    out = refs[1 if len(refs) > 1 else 0]
    del token, refs
    finish_hop(
        tiles, chunk, place_ref[1] == 0, top_links, low_rows(low_links, tiles), beyond, sums, out,
        lambda total, index: total * (1.0 / 6.0),
    )


def pair_tiles(vectors):
    half = vectors // ROWS // 2
    return [
        (base + left, base + right)
        for base in (0, half)
        for left in range(half)
        for right in range(left, half)
    ]


def add_pairs(field, low, quarks, sums):
    vectors, width = field.shape[1:]
    for colour in range(3):
        real = field[colour].astype(jnp.bfloat16)
        imag = field[3 + colour].astype(jnp.bfloat16)
        for part, (top, bottom) in enumerate(((real, imag), (-imag, real))):
            at = (part * 3 + colour) * width
            low[:vectors, at : at + width] = top
            low[vectors:, at : at + width] = bottom

    combos = pair_tiles(vectors)
    block = ROWS * ROWS
    lefts = sorted({left for left, _ in combos})
    def form(left):
        numbers = [number for number, combo in enumerate(combos) if combo[0] == left]
        for tile in range(width // LANES):
            at = tile * LANES
            lanes = slice(at, at + LANES)
            rights = [
                [
                    field[part, right * ROWS : (right + 1) * ROWS, lanes]
                    for part in range(6)
                ]
                for right in (combos[number][1] for number in numbers)
            ]
            for row in range(0, ROWS, 2):
                pair = [
                    [field[part, index : index + 1, lanes] for part in range(6)]
                    for index in (left * ROWS + row, left * ROWS + row + 1)
                ]
                for number, b in zip(numbers, rights):
                    made = [[] for _ in range(6)]
                    for a in pair:
                        for colour in range(3):
                            x, y = (colour + 1) % 3, (colour + 2) % 3
                            made[colour].append(
                                (a[x] * b[y] - a[3 + x] * b[3 + y])
                                - (a[y] * b[x] - a[3 + y] * b[3 + x])
                            )
                            made[3 + colour].append(
                                (a[x] * b[3 + y] + a[3 + x] * b[y])
                                - (a[y] * b[3 + x] + a[3 + y] * b[x])
                            )
                    start = number * block + row * ROWS
                    for part in range(6):
                        quarks[
                            start : start + 2 * ROWS,
                            part * width + at : part * width + at + LANES,
                        ] = jnp.concatenate(made[part], 0).astype(jnp.bfloat16)

    for left in lefts:
        form(left)
    sums[...] += lax.dot_general(
        quarks[...], low[...], (((1,), (1,)), ((), ())), preferred_element_type=jnp.float32
    )


def inner_pairs_kernel(
    tiles, chunk_tiles, place_ref, top_links, cross_links, linked, partner, partial, own, *refs
):
    outer, (sums, field, low, quarks) = refs[: len(chunk_tiles)], refs[len(chunk_tiles) :]
    vectors = field.shape[1]
    for tile in range(tiles):
        ref, from_lanes = tile_of(chunk_tiles, outer, tile)
        lanes = slice(tile * LANES, (tile + 1) * LANES)
        link = z_link(
            tiles, tile, top_links, partner_rows(linked, vectors), place_ref[1] == 1
        )
        cross = cross_of(cross_links, tiles, tile)

        def step(rows):
            total = [partial[part, rows, lanes] for part in range(6)]
            total = adjoint(cross, [ref[part, rows, from_lanes] for part in range(6)], total)
            total = times(link, [partner[part, rows, lanes] for part in range(6)], total)
            for part in range(6):
                field[part, rows, lanes] = total[part] * (2.0 / 6.0) - own[part, rows, lanes]

        groups_loop(vectors, step, 2)
    sums[...] = jnp.zeros_like(sums)
    width = low.shape[1] // 6
    for start in range(0, field.shape[2], width):
        add_pairs(field.at[:, :, start : start + width], low, quarks, sums)


def outer_pairs_kernel(
    tiles, chunk, place_ref, top_links, low_links, far, partial, own, before, sums, field, low, quarks
):
    finish_hop(
        tiles, chunk, place_ref[1] == 0, top_links, low_rows(low_links, tiles), far, partial, field,
        lambda total, index: total * (2.0 / 6.0) - own[index],
    )
    sums[...] = before[...]
    add_pairs(field, low, quarks, sums)


def arrange(sums, grid, crossed, ordered, factor):
    half = grid.shape[0] // 2
    side = math.isqrt(half)
    vectors = 2 * side
    block = ROWS * ROWS
    for number, (left, right) in enumerate(pair_tiles(vectors)):
        for row in range(ROWS):
            start = number * block + row * ROWS
            at = (left * ROWS + row) * side + right * ROWS % side
            grid[at : at + ROWS, :] = sums[start : start + ROWS, :] * factor
            if left != right:
                at = (right * ROWS + row) * side + left * ROWS % side
                grid[at : at + ROWS, :] = (
                    sums[pl.ds(number * block + row, ROWS, stride=ROWS), :] * -factor
                )
    lane = lax.broadcasted_iota(jnp.int32, (side, 2 * vectors), 1)
    own_half = lane % vectors < side
    per = 2 * vectors // side
    for start in range(0, half, 2 * vectors):
        turned = grid[half + start : half + start + 2 * vectors, :].T
        real, imag = turned[:side], turned[vectors : vectors + side]
        for index in range(per):
            second = start // side + index
            turn = (side - index * side) % (2 * vectors)
            value = jnp.where(
                lane < vectors,
                pltpu.roll(real, turn, 1) if turn else real,
                pltpu.roll(imag, (turn + vectors) % (2 * vectors), 1)
                if (turn + vectors) % (2 * vectors)
                else imag,
            )
            crossed[pl.ds(second, side, stride=side), :] = value
    for start in range(0, half, 2 * vectors):
        turned = grid[start : start + 2 * vectors, :].T
        real, imag = turned[side:vectors], turned[vectors + side :]
        for index in range(per):
            first = start // side + index
            turn = (-index * side) % (2 * vectors)
            value = jnp.where(
                lane < vectors,
                pltpu.roll(real, turn, 1) if turn else real,
                pltpu.roll(imag, (turn + vectors) % (2 * vectors), 1)
                if (turn + vectors) % (2 * vectors)
                else imag,
            )
            value = jnp.where(own_half, -value, crossed[first * side : (first + 1) * side, :])
            pair = first * vectors - first * (first + 1) // 2 + side - first - 1
            ordered[pair : pair + side, :] = value
    for first in range(vectors):
        skip = first % side + 1
        if skip < side:
            pair = first * vectors - first * (first + 1) // 2
            ordered[pair : pair + side - skip, :] = grid[
                first * side + skip : (first + 1) * side, :
            ]


def last_pairs_kernel(
    tiles, chunk, factor, slot_ref, place_ref, top_links, low_links, far, partial, own, before,
    keep, send, sums, field, low, quarks, grid, crossed, ordered,
):
    outer_pairs_kernel(
        tiles, chunk, place_ref, top_links, low_links, far, partial, own, before, sums, field, low,
        quarks,
    )
    arrange(sums, grid, crossed, ordered, factor)
    keep[...] = jnp.zeros_like(keep)
    send[...] = jnp.zeros_like(send)
    my_core = place_ref[1]

    def place(block, carry):
        slot = slot_ref[block]
        owner = slot // CAP
        away = jnp.bitwise_xor(owner // 2, place_ref[0])
        value = ordered[pl.ds(pl.multiple_of(block * PB, PB), PB), :]

        @pl.when(owner % 2 == my_core)
        def _():
            keep[away, slot % CAP] = value

        @pl.when(owner % 2 != my_core)
        def _():
            send[away, slot % CAP] = value

        return carry

    lax.fori_loop(0, slot_ref.shape[0], place, 0)


def combine_kernel(kept, received, far_sent, far_kept, *near):
    for away, out in enumerate(near):
        out[...] = kept[away] + received[away]
    for index in range(far_sent.shape[0]):
        away = len(near) + 2 * index
        far_kept[index] = kept[away] + received[away]
        far_sent[index] = kept[away + 1] + received[away + 1]


def far_kernel(kept, received, *outs):
    for index, out in enumerate(outs):
        out[...] = kept[index] + received[index]


def total_kernel(*refs):
    total = refs[0][...]
    for ref in refs[1:-1]:
        total = total + ref[...]
    refs[-1][...] = total


def on_device(eigen_vectors, link_field, block_slot):
    count = lax.axis_size("brick")
    vectors, sites = eigen_vectors.shape[0], eigen_vectors.shape[-1]
    planes = eigen_vectors.shape[-2]
    tiles = sites // LANES
    half_tiles = tiles // 2
    chunk_tiles = ((0, half_tiles), (half_tiles, tiles - half_tiles))

    def plane_of(width):
        return jax.ShapeDtypeStruct((6, vectors, width), jnp.float32)

    plane = plane_of(sites)
    pieces = [plane_of(size * LANES) for _, size in chunk_tiles]
    plane_bytes = 6 * vectors * sites * 4
    pair_rows = len(pair_tiles(vectors)) * ROWS * ROWS
    up = [(i, (i + 1) % count) for i in range(count)]
    on_chip = [(i, i ^ 1) for i in range(count)]
    off_chip = [(i, (i + 2 * (i % 2) - 1) % count) for i in range(count)]
    me = lax.axis_index("brick")
    place = jnp.stack([me // 2, me % 2]).astype(jnp.int32)
    z_links = jax.ShapeDtypeStruct((18 * tiles, LANES), jnp.float32)

    def call(kernel, shapes, name, smem, *args, limit=32, flops=0, scratch=()):
        many = isinstance(shapes, list)
        return pl.pallas_call(
            kernel,
            out_shape=shapes,
            in_specs=[SMEM] * smem + [VMEM] * (len(args) - smem),
            out_specs=[VMEM] * len(shapes) if many else VMEM,
            scratch_shapes=list(scratch),
            compiler_params=params(limit),
            cost_estimate=cost(flops, 2 * plane_bytes) if flops else None,
            name=name,
        )(*args)

    rows = tile_rows(eigen_vectors)
    outer = call(
        functools.partial(outer_kernel, tiles, chunk_tiles), pieces, "outer", 1, place, rows
    )
    with_links = jax.ShapeDtypeStruct((6, vectors + ROWS, sites), jnp.float32)
    inner, plane_links, cross_links, top_links = call(
        functools.partial(inner_kernel, tiles, vectors),
        [with_links, jax.ShapeDtypeStruct((72 * tiles, LANES), jnp.float32), z_links, z_links],
        "inner", 1, place, rows, tile_rows(link_field), outer[-1],
    )

    def off(fields):
        return [lax.ppermute(field, "brick", off_chip) for field in fields]

    far = off(outer)
    linked = lax.ppermute(inner, "brick", on_chip)
    low_links = lax.ppermute(top_links, "brick", up)
    inner_sums, outer_sums = call(
        functools.partial(local_kernel, tiles, chunk_tiles, (0, 1)), [plane] * 2, "local", 0,
        plane_links, cross_links, inner, *outer, limit=48, flops=4e9,
    )
    first_inner, inner_sums = call(
        functools.partial(inner_step_kernel, tiles), [plane] * 2, "inner_step", 1,
        place, top_links, plane_links, linked, inner_sums,
    )
    token = sum(field[0, :ROWS, :LANES] for field in [inner_sums, *far])
    token = lax.ppermute(token, "brick", [(i, i ^ 1) for i in range(count) if i % 4 in (1, 2)])
    first_outer = []
    for chunk, piece, field in zip(chunk_tiles, pieces, far):
        args = (place, top_links, low_links, field, outer_sums, token)
        if first_outer:
            first_outer.append(
                call(functools.partial(edge_kernel, tiles, chunk), piece, "edge", 1, *args)
            )
            continue
        first, first_inner = pl.pallas_call(
            functools.partial(edge_kernel, tiles, chunk),
            out_shape=[piece, plane],
            in_specs=[SMEM] + [VMEM] * 5 + [pl.BlockSpec(memory_space=pl.ANY)],
            out_specs=[VMEM, pl.BlockSpec(memory_space=pl.ANY)],
            input_output_aliases={6: 1},
            compiler_params=params(32),
            name="edge",
        )(*args, first_inner)
        first_outer.append(first)
    partner = lax.ppermute(first_inner, "brick", on_chip)
    far = off(first_outer)
    def scratch(width):
        return [
            pltpu.VMEM((2 * vectors, 6 * width), jnp.bfloat16),
            pltpu.VMEM((pair_rows, 6 * width), jnp.bfloat16),
        ]

    partial_sums = jax.ShapeDtypeStruct((pair_rows, 2 * vectors), jnp.float32)
    before = call(
        functools.partial(inner_pairs_kernel, tiles, chunk_tiles), partial_sums, "inner_pairs", 1,
        place, top_links, cross_links, linked, partner, inner_sums, inner, *first_outer, limit=48, flops=8e9,
        scratch=[pltpu.VMEM(plane.shape, jnp.float32)] + scratch(2 * LANES),
    )
    (sums,) = call(
        functools.partial(local_kernel, tiles, chunk_tiles, (1,)), [plane], "outer_hop", 0,
        plane_links, cross_links, first_inner, *first_outer, before, limit=48, flops=2e9,
    )
    for chunk, piece, field, own in zip(chunk_tiles[:-1], pieces, far, outer):
        before = pl.pallas_call(
            functools.partial(outer_pairs_kernel, tiles, chunk),
            out_shape=partial_sums,
            in_specs=[SMEM] + [VMEM] * 6,
            out_specs=VMEM,
            scratch_shapes=[pltpu.VMEM(piece.shape, jnp.float32)] + scratch(piece.shape[2]),
            compiler_params=params(48),
            cost_estimate=cost(4e9, 3 * plane_bytes),
            name="outer_pairs",
        )(place, top_links, low_links, field, sums, own, before)
    factor = 1.0 / math.sqrt(3.0 * sites * planes * count)
    chips = count // 2
    half = jax.ShapeDtypeStruct((chips, CAP, PB, 2 * vectors), jnp.float32)
    blocks = vectors * (vectors - 1) // 2
    keep, send = pl.pallas_call(
        functools.partial(last_pairs_kernel, tiles, chunk_tiles[-1], factor),
        out_shape=[half] * 2,
        in_specs=[SMEM] * 2 + [VMEM] * 6,
        out_specs=[VMEM] * 2,
        scratch_shapes=[
            pltpu.VMEM(partial_sums.shape, jnp.float32),
            pltpu.VMEM(pieces[-1].shape, jnp.float32),
        ]
        + scratch(pieces[-1].shape[2])
        + [
            pltpu.VMEM((vectors * vectors // 2, 2 * vectors), jnp.float32),
            pltpu.VMEM((vectors * vectors // 4, 2 * vectors), jnp.float32),
            pltpu.VMEM((blocks, 2 * vectors), jnp.float32),
        ],
        compiler_params=params(48),
        cost_estimate=cost(4e9, 3 * plane_bytes),
        name="last_pairs",
    )(block_slot, place, top_links, low_links, far[-1], sums, outer[-1], before)
    received = lax.ppermute(send, "brick", on_chip)
    share = jax.ShapeDtypeStruct((CAP, PB, 2 * vectors), jnp.float32)
    near = chips // 2
    stack = jax.ShapeDtypeStruct((near // 2, CAP, PB, 2 * vectors), jnp.float32)
    far_sent, far_kept, *shares = call(
        combine_kernel, [stack] * 2 + [share] * near, "combine", 0, keep, received
    )

    def to_chip(array, away):
        return lax.ppermute(array, "brick", [(i, i ^ (2 * away)) for i in range(count)])

    far_received = to_chip(far_sent, 1)
    far_shares = call(far_kernel, [share] * (near // 2), "far", 0, far_kept, far_received)
    arrived = [to_chip(shares[away], away) for away in range(1, near)]
    arrived += [
        to_chip(far_shares[index], near + 2 * index) for index in reversed(range(near // 2))
    ]
    return call(total_kernel, share, "total", 0, shares[0], *arrived)


def solution(mesh):
    return jax.shard_map(
        on_device,
        mesh=mesh,
        in_specs=(
            P(None, None, None, ("cuts", "brick"), None),
            P(None, None, None, None, ("cuts", "brick"), None),
            P(),
        ),
        out_specs=P(("cuts", "brick"), None, None),
        check_vma=False,
    )
```

```python
import functools
import math

import jax
import jax.numpy as jnp
import numpy as np
from jax import lax
from jax.experimental import pallas as pl
from jax.experimental.pallas import tpu as pltpu
from jax.sharding import PartitionSpec as P

PB = 32
CAP = 4
LX = 8
LANES = 128
ROWS = 8
VMEM = pl.BlockSpec(memory_space=pltpu.VMEM)
SMEM = pl.BlockSpec(memory_space=pltpu.SMEM)


def params(limit_mib):
    return pltpu.CompilerParams(vmem_limit_bytes=limit_mib * 1024 * 1024)


def cost(flops, bytes_accessed):
    return pl.CostEstimate(
        flops=int(flops), bytes_accessed=int(bytes_accessed), transcendentals=0
    )


def tile_rows(array):
    planes, sites = array.shape[-2:]
    tiles = sites // LANES
    lead = math.prod(array.shape[:-2])
    array = array.reshape(lead, planes, tiles, LANES).transpose(0, 2, 1, 3)
    return array.reshape(lead * tiles * planes, LANES)


def times(link, field, total):
    total = list(total)
    for out_row in range(3):
        for in_row in range(3):
            real, imag = link(0, out_row, in_row), link(1, out_row, in_row)
            f_real, f_imag = field[in_row], field[3 + in_row]
            total[out_row] = total[out_row] + real * f_real - imag * f_imag
            total[3 + out_row] = total[3 + out_row] + real * f_imag + imag * f_real
    return total


def adjoint(link, field, total):
    total = list(total)
    for out_row in range(3):
        for in_row in range(3):
            real, imag = link(0, in_row, out_row), link(1, in_row, out_row)
            f_real, f_imag = field[in_row], field[3 + in_row]
            total[out_row] = total[out_row] + real * f_real + imag * f_imag
            total[3 + out_row] = total[3 + out_row] + real * f_imag - imag * f_real
    return total


def link_row(part, row, column):
    return (part * 3 + row) * 3 + column


def plane_rows(x_ref, part, tile, tiles, vectors, lower_core, inner):
    start = (part * tiles + tile) * 2
    plane_0, plane_1 = (
        x_ref[pl.ds(start + plane, vectors, stride=6 * tiles * 2), :] for plane in range(2)
    )
    if inner:
        return jnp.where(lower_core, plane_1, plane_0)
    return jnp.where(lower_core, plane_0, plane_1)


def outer_kernel(tiles, chunk_tiles, place_ref, x_ref, *outer):
    lower_core = place_ref[1] == 0
    for (first_tile, count), out in zip(chunk_tiles, outer):
        for part in range(6):
            for tile in range(count):
                at = tile * LANES
                out[part, :, at : at + LANES] = plane_rows(
                    x_ref, part, first_tile + tile, tiles, out.shape[1], lower_core, False
                )


def inner_kernel(
    tiles, vectors, place_ref, x_ref, link_ref, after, inner, plane_links, cross_links, top_links
):
    del after
    lower_core = place_ref[1] == 0
    for part in range(6):
        for tile in range(tiles):
            inner[part, :vectors, tile * LANES : (tile + 1) * LANES] = plane_rows(
                x_ref, part, tile, tiles, vectors, lower_core, True
            )
    inner[:, vectors:, :] = jnp.zeros_like(inner[:, vectors:, :])
    for index in range(36 * tiles):
        plane_0, plane_1 = (
            link_ref[index * 2 + plane : index * 2 + plane + 1, :] for plane in range(2)
        )
        plane_links[index : index + 1, :] = jnp.where(lower_core, plane_1, plane_0)
        index += 36 * tiles
        plane_links[index : index + 1, :] = jnp.where(lower_core, plane_0, plane_1)
    for part in range(2):
        for row in range(3):
            for column in range(3):
                for tile in range(tiles):
                    straight = ((36 + link_row(part, row, column)) * tiles + tile) * 2
                    turned = ((36 + link_row(part, column, row)) * tiles + tile) * 2
                    number = link_row(part, row, column)
                    index = number * tiles + tile
                    sign = -1.0 if part else 1.0
                    cross_links[index : index + 1, :] = jnp.where(
                        lower_core,
                        link_ref[straight : straight + 1, :],
                        sign * link_ref[turned : turned + 1, :],
                    )
                    top = link_ref[straight + 1 : straight + 2, :]
                    top_links[index : index + 1, :] = top
                    inner[
                        number // 3,
                        vectors + number % 3 : vectors + number % 3 + 1,
                        tile * LANES : (tile + 1) * LANES,
                    ] = top


def z_link(tiles, tile, top_links, low_link, use_low):
    found = {}
    for part in range(2):
        for row in range(3):
            for column in range(3):
                straight = link_row(part, row, column) * tiles + tile
                sign = -1.0 if part else 1.0
                value = jnp.where(
                    use_low,
                    sign * low_link(part, column, row, tile),
                    top_links[straight : straight + 1, :],
                )
                found[part, row, column] = jnp.broadcast_to(value, (ROWS, LANES))
    return lambda *index: found[index]


def low_rows(low_links, tiles):
    def low_link(part, row, column, tile):
        index = link_row(part, row, column) * tiles + tile
        return low_links[index : index + 1, :]

    return low_link


def partner_rows(partner, vectors):
    def low_link(part, row, column, tile):
        number = link_row(part, row, column)
        at = vectors + number % 3
        return partner[number // 3, at : at + 1, tile * LANES : (tile + 1) * LANES]

    return low_link


def tile_of(chunk_tiles, refs, tile):
    for (first_tile, count), ref in zip(chunk_tiles, refs):
        if first_tile <= tile < first_tile + count:
            return ref, slice((tile - first_tile) * LANES, (tile - first_tile + 1) * LANES)


def cross_of(cross_links, tiles, tile):
    def link(part, row, column):
        index = link_row(part, row, column) * tiles + tile
        return cross_links[index : index + 1, :]

    return link


def plane_hops(tiles, plane, plane_links, get, extra, put):
    lane = lax.broadcasted_iota(jnp.int32, (ROWS, LANES), 1)
    column = lane % LX
    first_column, last_column = column == 0, column == LX - 1
    below, above = lane < LX, lane >= LANES - LX
    zeros = [jnp.zeros((ROWS, LANES), jnp.float32)] * 6

    def link_of(direction, tile):
        def link(part, row, column_at):
            index = plane * 36 + direction * 18 + link_row(part, row, column_at)
            index = index * tiles + tile
            return plane_links[index : index + 1, :]

        return link

    sums = []
    rolled_in = []
    rolled_out = []
    for tile in range(tiles):
        field = get(tile)
        ahead = [
            jnp.where(last_column, pltpu.roll(f, LX - 1, 1), pltpu.roll(f, LANES - 1, 1))
            for f in field
        ]
        total = [
            jnp.where(first_column, pltpu.roll(f, LANES - LX + 1, 1), pltpu.roll(f, 1, 1))
            for f in adjoint(link_of(0, tile), field, zeros)
        ]
        sums.append(extra(tile, times(link_of(0, tile), ahead, total)))
        rolled_in.append([pltpu.roll(f, LANES - LX, 1) for f in field])
        rolled_out.append(
            [pltpu.roll(f, LX, 1) for f in adjoint(link_of(1, tile), field, zeros)]
        )
    for tile in range(tiles):
        after, before = (tile + 1) % tiles, (tile - 1) % tiles
        ahead = [jnp.where(above, b, a) for a, b in zip(rolled_in[tile], rolled_in[after])]
        total = times(link_of(1, tile), ahead, sums[tile])
        put(
            tile,
            [
                t + jnp.where(below, b, o)
                for t, b, o in zip(total, rolled_out[before], rolled_out[tile])
            ],
        )


def groups_loop(vectors, step, unroll=1):
    def body(group, carry):
        step(pl.ds(pl.multiple_of(group * ROWS, ROWS), ROWS))
        return carry

    lax.fori_loop(0, vectors // ROWS, body, 0, unroll=unroll)


def local_kernel(tiles, chunk_tiles, planes, plane_links, cross_links, inner, *refs):
    outer, outs = refs[: len(chunk_tiles)], refs[-len(planes) :]

    def step(rows):
        def get(plane, tile):
            if plane == 0:
                ref, lanes = inner, slice(tile * LANES, (tile + 1) * LANES)
            else:
                ref, lanes = tile_of(chunk_tiles, outer, tile)
            return [ref[part, rows, lanes] for part in range(6)]

        for plane, out in zip(planes, outs):
            hop = times if plane else adjoint

            def put(tile, total):
                for part in range(6):
                    out[part, rows, tile * LANES : (tile + 1) * LANES] = total[part]

            plane_hops(
                tiles,
                plane,
                plane_links,
                lambda tile: get(plane, tile),
                lambda tile, total: hop(
                    cross_of(cross_links, tiles, tile), get(1 - plane, tile), total
                ),
                put,
            )

    groups_loop(outer[0].shape[1], step)


def finish_hop(tiles, chunk, use_low, top_links, low_link, beyond, sums, out, finish):
    first_tile, count = chunk
    for tile in range(count):
        link = z_link(tiles, first_tile + tile, top_links, low_link, use_low)
        lanes = slice(tile * LANES, (tile + 1) * LANES)
        at = (first_tile + tile) * LANES

        def step(rows):
            field = [beyond[part, rows, lanes] for part in range(6)]
            total = [sums[part, rows, at : at + LANES] for part in range(6)]
            total = times(link, field, total)
            for part in range(6):
                out[part, rows, lanes] = finish(total[part], (part, rows, lanes))

        groups_loop(out.shape[1], step, 2)


def inner_step_kernel(tiles, place_ref, top_links, plane_links, partner, sums, first, out):
    finish_hop(
        tiles, (0, tiles), place_ref[1] == 1, top_links, partner_rows(partner, first.shape[1]),
        partner, sums, first, lambda total, index: total * (1.0 / 6.0),
    )

    def step(rows):
        def put(tile, total):
            for part in range(6):
                out[part, rows, tile * LANES : (tile + 1) * LANES] = total[part]

        plane_hops(
            tiles,
            0,
            plane_links,
            lambda tile: [
                first[part, rows, tile * LANES : (tile + 1) * LANES] for part in range(6)
            ],
            lambda tile, total: total,
            put,
        )

    groups_loop(out.shape[1], step)


def edge_kernel(
    tiles, chunk, place_ref, top_links, low_links, beyond, sums, token, *refs
):
    out = refs[1 if len(refs) > 1 else 0]
    del token, refs
    finish_hop(
        tiles, chunk, place_ref[1] == 0, top_links, low_rows(low_links, tiles), beyond, sums, out,
        lambda total, index: total * (1.0 / 6.0),
    )


def pair_tiles(vectors):
    half = vectors // ROWS // 2
    return [
        (base + left, base + right)
        for base in (0, half)
        for left in range(half)
        for right in range(left, half)
    ]


def add_pairs(field, low, quarks, sums):
    vectors, width = field.shape[1:]
    for colour in range(3):
        real = field[colour].astype(jnp.bfloat16)
        imag = field[3 + colour].astype(jnp.bfloat16)
        for part, (top, bottom) in enumerate(((real, imag), (-imag, real))):
            at = (part * 3 + colour) * width
            low[:vectors, at : at + width] = top
            low[vectors:, at : at + width] = bottom

    combos = pair_tiles(vectors)
    block = ROWS * ROWS
    lefts = sorted({left for left, _ in combos})
    def form(left):
        numbers = [number for number, combo in enumerate(combos) if combo[0] == left]
        for tile in range(width // LANES):
            at = tile * LANES
            lanes = slice(at, at + LANES)
            rights = [
                [
                    field[part, right * ROWS : (right + 1) * ROWS, lanes]
                    for part in range(6)
                ]
                for right in (combos[number][1] for number in numbers)
            ]
            for row in range(0, ROWS, 2):
                pair = [
                    [field[part, index : index + 1, lanes] for part in range(6)]
                    for index in (left * ROWS + row, left * ROWS + row + 1)
                ]
                for number, b in zip(numbers, rights):
                    made = [[] for _ in range(6)]
                    for a in pair:
                        for colour in range(3):
                            x, y = (colour + 1) % 3, (colour + 2) % 3
                            made[colour].append(
                                (a[x] * b[y] - a[3 + x] * b[3 + y])
                                - (a[y] * b[x] - a[3 + y] * b[3 + x])
                            )
                            made[3 + colour].append(
                                (a[x] * b[3 + y] + a[3 + x] * b[y])
                                - (a[y] * b[3 + x] + a[3 + y] * b[x])
                            )
                    start = number * block + row * ROWS
                    for part in range(6):
                        quarks[
                            start : start + 2 * ROWS,
                            part * width + at : part * width + at + LANES,
                        ] = jnp.concatenate(made[part], 0).astype(jnp.bfloat16)

    for left in lefts:
        form(left)
    sums[...] += lax.dot_general(
        quarks[...], low[...], (((1,), (1,)), ((), ())), preferred_element_type=jnp.float32
    )


def inner_pairs_kernel(
    tiles, chunk_tiles, place_ref, top_links, cross_links, linked, partner, partial, own, *refs
):
    outer, (sums, field, low, quarks) = refs[: len(chunk_tiles)], refs[len(chunk_tiles) :]
    vectors = field.shape[1]
    for tile in range(tiles):
        ref, from_lanes = tile_of(chunk_tiles, outer, tile)
        lanes = slice(tile * LANES, (tile + 1) * LANES)
        link = z_link(
            tiles, tile, top_links, partner_rows(linked, vectors), place_ref[1] == 1
        )
        cross = cross_of(cross_links, tiles, tile)

        def step(rows):
            total = [partial[part, rows, lanes] for part in range(6)]
            total = adjoint(cross, [ref[part, rows, from_lanes] for part in range(6)], total)
            total = times(link, [partner[part, rows, lanes] for part in range(6)], total)
            for part in range(6):
                field[part, rows, lanes] = total[part] * (2.0 / 6.0) - own[part, rows, lanes]

        groups_loop(vectors, step, 2)
    sums[...] = jnp.zeros_like(sums)
    width = low.shape[1] // 6
    for start in range(0, field.shape[2], width):
        add_pairs(field.at[:, :, start : start + width], low, quarks, sums)


def outer_pairs_kernel(
    tiles, chunk, place_ref, top_links, low_links, far, partial, own, before, sums, field, low, quarks
):
    finish_hop(
        tiles, chunk, place_ref[1] == 0, top_links, low_rows(low_links, tiles), far, partial, field,
        lambda total, index: total * (2.0 / 6.0) - own[index],
    )
    sums[...] = before[...]
    add_pairs(field, low, quarks, sums)


def arrange(sums, grid, crossed, ordered, factor):
    half = grid.shape[0] // 2
    side = math.isqrt(half)
    vectors = 2 * side
    block = ROWS * ROWS
    for number, (left, right) in enumerate(pair_tiles(vectors)):
        for row in range(ROWS):
            start = number * block + row * ROWS
            at = (left * ROWS + row) * side + right * ROWS % side
            grid[at : at + ROWS, :] = sums[start : start + ROWS, :] * factor
            if left != right:
                at = (right * ROWS + row) * side + left * ROWS % side
                grid[at : at + ROWS, :] = (
                    sums[pl.ds(number * block + row, ROWS, stride=ROWS), :] * -factor
                )
    lane = lax.broadcasted_iota(jnp.int32, (side, 2 * vectors), 1)
    own_half = lane % vectors < side
    per = 2 * vectors // side
    for start in range(0, half, 2 * vectors):
        turned = grid[half + start : half + start + 2 * vectors, :].T
        real, imag = turned[:side], turned[vectors : vectors + side]
        for index in range(per):
            second = start // side + index
            turn = (side - index * side) % (2 * vectors)
            value = jnp.where(
                lane < vectors,
                pltpu.roll(real, turn, 1) if turn else real,
                pltpu.roll(imag, (turn + vectors) % (2 * vectors), 1)
                if (turn + vectors) % (2 * vectors)
                else imag,
            )
            crossed[pl.ds(second, side, stride=side), :] = value
    for start in range(0, half, 2 * vectors):
        turned = grid[start : start + 2 * vectors, :].T
        real, imag = turned[side:vectors], turned[vectors + side :]
        for index in range(per):
            first = start // side + index
            turn = (-index * side) % (2 * vectors)
            value = jnp.where(
                lane < vectors,
                pltpu.roll(real, turn, 1) if turn else real,
                pltpu.roll(imag, (turn + vectors) % (2 * vectors), 1)
                if (turn + vectors) % (2 * vectors)
                else imag,
            )
            value = jnp.where(own_half, -value, crossed[first * side : (first + 1) * side, :])
            pair = first * vectors - first * (first + 1) // 2 + side - first - 1
            ordered[pair : pair + side, :] = value
    for first in range(vectors):
        skip = first % side + 1
        if skip < side:
            pair = first * vectors - first * (first + 1) // 2
            ordered[pair : pair + side - skip, :] = grid[
                first * side + skip : (first + 1) * side, :
            ]


def last_pairs_kernel(
    tiles, chunk, factor, slot_ref, place_ref, top_links, low_links, far, partial, own, before,
    keep, send, sums, field, low, quarks, grid, crossed, ordered, both,
):
    outer_pairs_kernel(
        tiles, chunk, place_ref, top_links, low_links, far, partial, own, before, sums, field, low,
        quarks,
    )
    arrange(sums, grid, crossed, ordered, factor)
    both[...] = jnp.zeros_like(both)

    def place(block, carry):
        slot = slot_ref[block]
        owner = slot // CAP
        other = jnp.bitwise_xor(owner % 2, place_ref[1])
        away = jnp.bitwise_xor(owner // 2, place_ref[0])
        both[other, away, slot % CAP] = ordered[pl.ds(pl.multiple_of(block * PB, PB), PB), :]
        return carry

    lax.fori_loop(0, slot_ref.shape[0], place, 0, unroll=7 if slot_ref.shape[0] % 7 == 0 else 1)
    keep[...] = both[0]
    send[...] = both[1]


def combine_kernel(kept, received, far_sent, far_kept, *near):
    for away, out in enumerate(near):
        out[...] = kept[away] + received[away]
    for index in range(far_sent.shape[0]):
        away = len(near) + 2 * index
        far_kept[index] = kept[away] + received[away]
        far_sent[index] = kept[away + 1] + received[away + 1]


def far_kernel(kept, received, *outs):
    for index, out in enumerate(outs):
        out[...] = kept[index] + received[index]


def total_kernel(*refs):
    total = refs[0][...]
    for ref in refs[1:-1]:
        total = total + ref[...]
    refs[-1][...] = total


def on_device(eigen_vectors, link_field, block_slot):
    count = lax.axis_size("brick")
    vectors, sites = eigen_vectors.shape[0], eigen_vectors.shape[-1]
    planes = eigen_vectors.shape[-2]
    tiles = sites // LANES
    half_tiles = tiles // 2
    chunk_tiles = ((0, half_tiles), (half_tiles, tiles - half_tiles))

    def plane_of(width):
        return jax.ShapeDtypeStruct((6, vectors, width), jnp.float32)

    plane = plane_of(sites)
    pieces = [plane_of(size * LANES) for _, size in chunk_tiles]
    plane_bytes = 6 * vectors * sites * 4
    pair_rows = len(pair_tiles(vectors)) * ROWS * ROWS
    up = [(i, (i + 1) % count) for i in range(count)]
    on_chip = [(i, i ^ 1) for i in range(count)]
    off_chip = [(i, (i + 2 * (i % 2) - 1) % count) for i in range(count)]
    me = lax.axis_index("brick")
    place = jnp.stack([me // 2, me % 2]).astype(jnp.int32)
    z_links = jax.ShapeDtypeStruct((18 * tiles, LANES), jnp.float32)

    def call(kernel, shapes, name, smem, *args, limit=32, flops=0, scratch=()):
        many = isinstance(shapes, list)
        return pl.pallas_call(
            kernel,
            out_shape=shapes,
            in_specs=[SMEM] * smem + [VMEM] * (len(args) - smem),
            out_specs=[VMEM] * len(shapes) if many else VMEM,
            scratch_shapes=list(scratch),
            compiler_params=params(limit),
            cost_estimate=cost(flops, 2 * plane_bytes) if flops else None,
            name=name,
        )(*args)

    rows = tile_rows(eigen_vectors)
    outer = call(
        functools.partial(outer_kernel, tiles, chunk_tiles), pieces, "outer", 1, place, rows
    )
    with_links = jax.ShapeDtypeStruct((6, vectors + ROWS, sites), jnp.float32)
    inner, plane_links, cross_links, top_links = call(
        functools.partial(inner_kernel, tiles, vectors),
        [with_links, jax.ShapeDtypeStruct((72 * tiles, LANES), jnp.float32), z_links, z_links],
        "inner", 1, place, rows, tile_rows(link_field), outer[-1],
    )

    def off(fields):
        return [lax.ppermute(field, "brick", off_chip) for field in fields]

    far = off(outer)
    linked = lax.ppermute(inner, "brick", on_chip)
    low_links = lax.ppermute(top_links, "brick", up)
    inner_sums, outer_sums = call(
        functools.partial(local_kernel, tiles, chunk_tiles, (0, 1)), [plane] * 2, "local", 0,
        plane_links, cross_links, inner, *outer, limit=48, flops=4e9,
    )
    first_inner, inner_sums = call(
        functools.partial(inner_step_kernel, tiles), [plane] * 2, "inner_step", 1,
        place, top_links, plane_links, linked, inner_sums,
    )
    token = sum(field[0, :ROWS, :LANES] for field in [inner_sums, *far])
    token = lax.ppermute(token, "brick", [(i, i ^ 1) for i in range(count) if i % 4 in (1, 2)])
    first_outer = []
    for chunk, piece, field in zip(chunk_tiles, pieces, far):
        args = (place, top_links, low_links, field, outer_sums, token)
        if first_outer:
            first_outer.append(
                call(functools.partial(edge_kernel, tiles, chunk), piece, "edge", 1, *args)
            )
            continue
        first, first_inner = pl.pallas_call(
            functools.partial(edge_kernel, tiles, chunk),
            out_shape=[piece, plane],
            in_specs=[SMEM] + [VMEM] * 5 + [pl.BlockSpec(memory_space=pl.ANY)],
            out_specs=[VMEM, pl.BlockSpec(memory_space=pl.ANY)],
            input_output_aliases={6: 1},
            compiler_params=params(32),
            name="edge",
        )(*args, first_inner)
        first_outer.append(first)
    partner = lax.ppermute(first_inner, "brick", on_chip)
    far = off(first_outer)
    def scratch(width):
        return [
            pltpu.VMEM((2 * vectors, 6 * width), jnp.bfloat16),
            pltpu.VMEM((pair_rows, 6 * width), jnp.bfloat16),
        ]

    partial_sums = jax.ShapeDtypeStruct((pair_rows, 2 * vectors), jnp.float32)
    before = call(
        functools.partial(inner_pairs_kernel, tiles, chunk_tiles), partial_sums, "inner_pairs", 1,
        place, top_links, cross_links, linked, partner, inner_sums, inner, *first_outer, limit=48, flops=8e9,
        scratch=[pltpu.VMEM(plane.shape, jnp.float32)] + scratch(2 * LANES),
    )
    (sums,) = call(
        functools.partial(local_kernel, tiles, chunk_tiles, (1,)), [plane], "outer_hop", 0,
        plane_links, cross_links, first_inner, *first_outer, before, limit=48, flops=2e9,
    )
    for chunk, piece, field, own in zip(chunk_tiles[:-1], pieces, far, outer):
        before = pl.pallas_call(
            functools.partial(outer_pairs_kernel, tiles, chunk),
            out_shape=partial_sums,
            in_specs=[SMEM] + [VMEM] * 6,
            out_specs=VMEM,
            scratch_shapes=[pltpu.VMEM(piece.shape, jnp.float32)] + scratch(piece.shape[2]),
            compiler_params=params(48),
            cost_estimate=cost(4e9, 3 * plane_bytes),
            name="outer_pairs",
        )(place, top_links, low_links, field, sums, own, before)
    factor = 1.0 / math.sqrt(3.0 * sites * planes * count)
    chips = count // 2
    half = jax.ShapeDtypeStruct((chips, CAP, PB, 2 * vectors), jnp.float32)
    blocks = vectors * (vectors - 1) // 2
    keep, send = pl.pallas_call(
        functools.partial(last_pairs_kernel, tiles, chunk_tiles[-1], factor),
        out_shape=[half] * 2,
        in_specs=[SMEM] * 2 + [VMEM] * 6,
        out_specs=[VMEM] * 2,
        scratch_shapes=[
            pltpu.VMEM(partial_sums.shape, jnp.float32),
            pltpu.VMEM(pieces[-1].shape, jnp.float32),
        ]
        + scratch(pieces[-1].shape[2])
        + [
            pltpu.VMEM((vectors * vectors // 2, 2 * vectors), jnp.float32),
            pltpu.VMEM((vectors * vectors // 4, 2 * vectors), jnp.float32),
            pltpu.VMEM((blocks, 2 * vectors), jnp.float32),
            pltpu.VMEM((2,) + half.shape, jnp.float32),
        ],
        compiler_params=params(48),
        cost_estimate=cost(4e9, 3 * plane_bytes),
        name="last_pairs",
    )(block_slot, place, top_links, low_links, far[-1], sums, outer[-1], before)
    received = lax.ppermute(send, "brick", on_chip)
    share = jax.ShapeDtypeStruct((CAP, PB, 2 * vectors), jnp.float32)
    near = chips // 2
    stack = jax.ShapeDtypeStruct((near // 2, CAP, PB, 2 * vectors), jnp.float32)
    far_sent, far_kept, *shares = call(
        combine_kernel, [stack] * 2 + [share] * near, "combine", 0, keep, received
    )

    def to_chip(array, away):
        return lax.ppermute(array, "brick", [(i, i ^ (2 * away)) for i in range(count)])

    far_received = to_chip(far_sent, 1)
    far_shares = call(far_kernel, [share] * (near // 2), "far", 0, far_kept, far_received)
    arrived = [to_chip(shares[away], away) for away in range(1, near)]
    arrived += [
        to_chip(far_shares[index], near + 2 * index) for index in range(near // 2)
    ]
    return call(total_kernel, share, "total", 0, shares[0], *arrived)


def solution(mesh):
    return jax.shard_map(
        on_device,
        mesh=mesh,
        in_specs=(
            P(None, None, None, ("cuts", "brick"), None),
            P(None, None, None, None, ("cuts", "brick"), None),
            P(),
        ),
        out_specs=P(("cuts", "brick"), None, None),
        check_vma=False,
    )
```

```python
import functools
import math

import jax
import jax.numpy as jnp
import numpy as np
from jax import lax
from jax.experimental import pallas as pl
from jax.experimental.pallas import tpu as pltpu
from jax.sharding import PartitionSpec as P

PB = 32
CAP = 4
LX = 8
LANES = 128
ROWS = 8
VMEM = pl.BlockSpec(memory_space=pltpu.VMEM)
SMEM = pl.BlockSpec(memory_space=pltpu.SMEM)


def params(limit_mib):
    return pltpu.CompilerParams(vmem_limit_bytes=limit_mib * 1024 * 1024)


def cost(flops, bytes_accessed):
    return pl.CostEstimate(
        flops=int(flops), bytes_accessed=int(bytes_accessed), transcendentals=0
    )


def tile_rows(array):
    planes, sites = array.shape[-2:]
    tiles = sites // LANES
    lead = math.prod(array.shape[:-2])
    array = array.reshape(lead, planes, tiles, LANES).transpose(0, 2, 1, 3)
    return array.reshape(lead * tiles * planes, LANES)


def times(link, field, total):
    total = list(total)
    for out_row in range(3):
        for in_row in range(3):
            real, imag = link(0, out_row, in_row), link(1, out_row, in_row)
            f_real, f_imag = field[in_row], field[3 + in_row]
            total[out_row] = total[out_row] + real * f_real - imag * f_imag
            total[3 + out_row] = total[3 + out_row] + real * f_imag + imag * f_real
    return total


def adjoint(link, field, total):
    total = list(total)
    for out_row in range(3):
        for in_row in range(3):
            real, imag = link(0, in_row, out_row), link(1, in_row, out_row)
            f_real, f_imag = field[in_row], field[3 + in_row]
            total[out_row] = total[out_row] + real * f_real + imag * f_imag
            total[3 + out_row] = total[3 + out_row] + real * f_imag - imag * f_real
    return total


def link_row(part, row, column):
    return (part * 3 + row) * 3 + column


def plane_rows(x_ref, part, tile, tiles, vectors, lower_core, inner):
    start = (part * tiles + tile) * 2
    plane_0, plane_1 = (
        x_ref[pl.ds(start + plane, vectors, stride=6 * tiles * 2), :] for plane in range(2)
    )
    if inner:
        return jnp.where(lower_core, plane_1, plane_0)
    return jnp.where(lower_core, plane_0, plane_1)


def outer_kernel(tiles, chunk_tiles, place_ref, x_ref, *outer):
    lower_core = place_ref[1] == 0
    for (first_tile, count), out in zip(chunk_tiles, outer):
        for part in range(6):
            for tile in range(count):
                at = tile * LANES
                out[part, :, at : at + LANES] = plane_rows(
                    x_ref, part, first_tile + tile, tiles, out.shape[1], lower_core, False
                )


def inner_kernel(
    tiles, vectors, place_ref, x_ref, link_ref, after, inner, plane_links, cross_links, top_links
):
    del after
    lower_core = place_ref[1] == 0
    for part in range(6):
        for tile in range(tiles):
            inner[part, :vectors, tile * LANES : (tile + 1) * LANES] = plane_rows(
                x_ref, part, tile, tiles, vectors, lower_core, True
            )
    inner[:, vectors:, :] = jnp.zeros_like(inner[:, vectors:, :])
    for index in range(36 * tiles):
        plane_0, plane_1 = (
            link_ref[index * 2 + plane : index * 2 + plane + 1, :] for plane in range(2)
        )
        plane_links[index : index + 1, :] = jnp.where(lower_core, plane_1, plane_0)
        index += 36 * tiles
        plane_links[index : index + 1, :] = jnp.where(lower_core, plane_0, plane_1)
    for part in range(2):
        for row in range(3):
            for column in range(3):
                for tile in range(tiles):
                    straight = ((36 + link_row(part, row, column)) * tiles + tile) * 2
                    turned = ((36 + link_row(part, column, row)) * tiles + tile) * 2
                    number = link_row(part, row, column)
                    index = number * tiles + tile
                    sign = -1.0 if part else 1.0
                    cross_links[index : index + 1, :] = jnp.where(
                        lower_core,
                        link_ref[straight : straight + 1, :],
                        sign * link_ref[turned : turned + 1, :],
                    )
                    top = link_ref[straight + 1 : straight + 2, :]
                    top_links[index : index + 1, :] = top
                    inner[
                        number // 3,
                        vectors + number % 3 : vectors + number % 3 + 1,
                        tile * LANES : (tile + 1) * LANES,
                    ] = top


def z_link(tiles, tile, top_links, low_link, use_low):
    found = {}
    for part in range(2):
        for row in range(3):
            for column in range(3):
                straight = link_row(part, row, column) * tiles + tile
                sign = -1.0 if part else 1.0
                value = jnp.where(
                    use_low,
                    sign * low_link(part, column, row, tile),
                    top_links[straight : straight + 1, :],
                )
                found[part, row, column] = jnp.broadcast_to(value, (ROWS, LANES))
    return lambda *index: found[index]


def low_rows(low_links, tiles):
    def low_link(part, row, column, tile):
        index = link_row(part, row, column) * tiles + tile
        return low_links[index : index + 1, :]

    return low_link


def partner_rows(partner, vectors):
    def low_link(part, row, column, tile):
        number = link_row(part, row, column)
        at = vectors + number % 3
        return partner[number // 3, at : at + 1, tile * LANES : (tile + 1) * LANES]

    return low_link


def tile_of(chunk_tiles, refs, tile):
    for (first_tile, count), ref in zip(chunk_tiles, refs):
        if first_tile <= tile < first_tile + count:
            return ref, slice((tile - first_tile) * LANES, (tile - first_tile + 1) * LANES)


def cross_of(cross_links, tiles, tile):
    def link(part, row, column):
        index = link_row(part, row, column) * tiles + tile
        return cross_links[index : index + 1, :]

    return link


def plane_hops(tiles, plane, plane_links, get, extra, put):
    lane = lax.broadcasted_iota(jnp.int32, (ROWS, LANES), 1)
    column = lane % LX
    first_column, last_column = column == 0, column == LX - 1
    below, above = lane < LX, lane >= LANES - LX
    zeros = [jnp.zeros((ROWS, LANES), jnp.float32)] * 6

    def link_of(direction, tile):
        def link(part, row, column_at):
            index = plane * 36 + direction * 18 + link_row(part, row, column_at)
            index = index * tiles + tile
            return plane_links[index : index + 1, :]

        return link

    sums = []
    rolled_in = []
    rolled_out = []
    for tile in range(tiles):
        field = get(tile)
        ahead = [
            jnp.where(last_column, pltpu.roll(f, LX - 1, 1), pltpu.roll(f, LANES - 1, 1))
            for f in field
        ]
        total = [
            jnp.where(first_column, pltpu.roll(f, LANES - LX + 1, 1), pltpu.roll(f, 1, 1))
            for f in adjoint(link_of(0, tile), field, zeros)
        ]
        sums.append(extra(tile, times(link_of(0, tile), ahead, total)))
        rolled_in.append([pltpu.roll(f, LANES - LX, 1) for f in field])
        rolled_out.append(
            [pltpu.roll(f, LX, 1) for f in adjoint(link_of(1, tile), field, zeros)]
        )
    for tile in range(tiles):
        after, before = (tile + 1) % tiles, (tile - 1) % tiles
        ahead = [jnp.where(above, b, a) for a, b in zip(rolled_in[tile], rolled_in[after])]
        total = times(link_of(1, tile), ahead, sums[tile])
        put(
            tile,
            [
                t + jnp.where(below, b, o)
                for t, b, o in zip(total, rolled_out[before], rolled_out[tile])
            ],
        )


def groups_loop(vectors, step, unroll=1):
    def body(group, carry):
        step(pl.ds(pl.multiple_of(group * ROWS, ROWS), ROWS))
        return carry

    lax.fori_loop(0, vectors // ROWS, body, 0, unroll=unroll)


def local_kernel(tiles, chunk_tiles, planes, plane_links, cross_links, inner, *refs):
    outer, outs = refs[: len(chunk_tiles)], refs[-len(planes) :]

    def step(rows):
        def get(plane, tile):
            if plane == 0:
                ref, lanes = inner, slice(tile * LANES, (tile + 1) * LANES)
            else:
                ref, lanes = tile_of(chunk_tiles, outer, tile)
            return [ref[part, rows, lanes] for part in range(6)]

        for plane, out in zip(planes, outs):
            hop = times if plane else adjoint

            def put(tile, total):
                for part in range(6):
                    out[part, rows, tile * LANES : (tile + 1) * LANES] = total[part]

            plane_hops(
                tiles,
                plane,
                plane_links,
                lambda tile: get(plane, tile),
                lambda tile, total: hop(
                    cross_of(cross_links, tiles, tile), get(1 - plane, tile), total
                ),
                put,
            )

    groups_loop(outer[0].shape[1], step)


def finish_hop(tiles, chunk, use_low, top_links, low_link, beyond, sums, out, finish):
    first_tile, count = chunk
    for tile in range(count):
        link = z_link(tiles, first_tile + tile, top_links, low_link, use_low)
        lanes = slice(tile * LANES, (tile + 1) * LANES)
        at = (first_tile + tile) * LANES

        def step(rows):
            field = [beyond[part, rows, lanes] for part in range(6)]
            total = [sums[part, rows, at : at + LANES] for part in range(6)]
            total = times(link, field, total)
            for part in range(6):
                out[part, rows, lanes] = finish(total[part], (part, rows, lanes))

        groups_loop(out.shape[1], step, 4)


def inner_step_kernel(tiles, place_ref, top_links, plane_links, partner, sums, first, out):
    finish_hop(
        tiles, (0, tiles), place_ref[1] == 1, top_links, partner_rows(partner, first.shape[1]),
        partner, sums, first, lambda total, index: total * (1.0 / 6.0),
    )

    def step(rows):
        def put(tile, total):
            for part in range(6):
                out[part, rows, tile * LANES : (tile + 1) * LANES] = total[part]

        plane_hops(
            tiles,
            0,
            plane_links,
            lambda tile: [
                first[part, rows, tile * LANES : (tile + 1) * LANES] for part in range(6)
            ],
            lambda tile, total: total,
            put,
        )

    groups_loop(out.shape[1], step)


def edge_kernel(
    tiles, chunk, place_ref, top_links, low_links, beyond, sums, token, *refs
):
    out = refs[1 if len(refs) > 1 else 0]
    del token, refs
    finish_hop(
        tiles, chunk, place_ref[1] == 0, top_links, low_rows(low_links, tiles), beyond, sums, out,
        lambda total, index: total * (1.0 / 6.0),
    )


def pair_tiles(vectors):
    half = vectors // ROWS // 2
    return [
        (base + left, base + right)
        for base in (0, half)
        for left in range(half)
        for right in range(left, half)
    ]


def add_pairs(field, low, quarks, sums):
    vectors, width = field.shape[1:]
    for colour in range(3):
        real = field[colour].astype(jnp.bfloat16)
        imag = field[3 + colour].astype(jnp.bfloat16)
        for part, (top, bottom) in enumerate(((real, imag), (-imag, real))):
            at = (part * 3 + colour) * width
            low[:vectors, at : at + width] = top
            low[vectors:, at : at + width] = bottom

    combos = pair_tiles(vectors)
    block = ROWS * ROWS
    lefts = sorted({left for left, _ in combos})
    def form(left):
        numbers = [number for number, combo in enumerate(combos) if combo[0] == left]
        for tile in range(width // LANES):
            at = tile * LANES
            lanes = slice(at, at + LANES)
            rights = [
                [
                    field[part, right * ROWS : (right + 1) * ROWS, lanes]
                    for part in range(6)
                ]
                for right in (combos[number][1] for number in numbers)
            ]
            for row in range(0, ROWS, 2):
                pair = [
                    [field[part, index : index + 1, lanes] for part in range(6)]
                    for index in (left * ROWS + row, left * ROWS + row + 1)
                ]
                for number, b in zip(numbers, rights):
                    made = [[] for _ in range(6)]
                    for a in pair:
                        for colour in range(3):
                            x, y = (colour + 1) % 3, (colour + 2) % 3
                            made[colour].append(
                                (a[x] * b[y] - a[3 + x] * b[3 + y])
                                - (a[y] * b[x] - a[3 + y] * b[3 + x])
                            )
                            made[3 + colour].append(
                                (a[x] * b[3 + y] + a[3 + x] * b[y])
                                - (a[y] * b[3 + x] + a[3 + y] * b[x])
                            )
                    start = number * block + row * ROWS
                    for part in range(6):
                        quarks[
                            start : start + 2 * ROWS,
                            part * width + at : part * width + at + LANES,
                        ] = jnp.concatenate(made[part], 0).astype(jnp.bfloat16)

    for left in lefts:
        form(left)
    sums[...] += lax.dot_general(
        quarks[...], low[...], (((1,), (1,)), ((), ())), preferred_element_type=jnp.float32
    )


def inner_pairs_kernel(
    tiles, chunk_tiles, place_ref, top_links, cross_links, linked, partner, partial, own, *refs
):
    outer, (sums, field, low, quarks) = refs[: len(chunk_tiles)], refs[len(chunk_tiles) :]
    vectors = field.shape[1]
    for tile in range(tiles):
        ref, from_lanes = tile_of(chunk_tiles, outer, tile)
        lanes = slice(tile * LANES, (tile + 1) * LANES)
        link = z_link(
            tiles, tile, top_links, partner_rows(linked, vectors), place_ref[1] == 1
        )
        cross = cross_of(cross_links, tiles, tile)

        def step(rows):
            total = [partial[part, rows, lanes] for part in range(6)]
            total = adjoint(cross, [ref[part, rows, from_lanes] for part in range(6)], total)
            total = times(link, [partner[part, rows, lanes] for part in range(6)], total)
            for part in range(6):
                field[part, rows, lanes] = total[part] * (2.0 / 6.0) - own[part, rows, lanes]

        groups_loop(vectors, step, 4)
    sums[...] = jnp.zeros_like(sums)
    width = low.shape[1] // 6
    for start in range(0, field.shape[2], width):
        add_pairs(field.at[:, :, start : start + width], low, quarks, sums)


def outer_pairs_kernel(
    tiles, chunk, place_ref, top_links, low_links, far, partial, own, before, sums, field, low, quarks
):
    finish_hop(
        tiles, chunk, place_ref[1] == 0, top_links, low_rows(low_links, tiles), far, partial, field,
        lambda total, index: total * (2.0 / 6.0) - own[index],
    )
    sums[...] = before[...]
    add_pairs(field, low, quarks, sums)


def arrange(sums, grid, crossed, ordered, factor):
    half = grid.shape[0] // 2
    side = math.isqrt(half)
    vectors = 2 * side
    block = ROWS * ROWS
    for number, (left, right) in enumerate(pair_tiles(vectors)):
        for row in range(ROWS):
            start = number * block + row * ROWS
            at = (left * ROWS + row) * side + right * ROWS % side
            grid[at : at + ROWS, :] = sums[start : start + ROWS, :] * factor
            if left != right:
                at = (right * ROWS + row) * side + left * ROWS % side
                grid[at : at + ROWS, :] = (
                    sums[pl.ds(number * block + row, ROWS, stride=ROWS), :] * -factor
                )
    lane = lax.broadcasted_iota(jnp.int32, (side, 2 * vectors), 1)
    own_half = lane % vectors < side
    per = 2 * vectors // side
    for start in range(0, half, 2 * vectors):
        turned = grid[half + start : half + start + 2 * vectors, :].T
        real, imag = turned[:side], turned[vectors : vectors + side]
        for index in range(per):
            second = start // side + index
            turn = (side - index * side) % (2 * vectors)
            value = jnp.where(
                lane < vectors,
                pltpu.roll(real, turn, 1) if turn else real,
                pltpu.roll(imag, (turn + vectors) % (2 * vectors), 1)
                if (turn + vectors) % (2 * vectors)
                else imag,
            )
            crossed[pl.ds(second, side, stride=side), :] = value
    for start in range(0, half, 2 * vectors):
        turned = grid[start : start + 2 * vectors, :].T
        real, imag = turned[side:vectors], turned[vectors + side :]
        for index in range(per):
            first = start // side + index
            turn = (-index * side) % (2 * vectors)
            value = jnp.where(
                lane < vectors,
                pltpu.roll(real, turn, 1) if turn else real,
                pltpu.roll(imag, (turn + vectors) % (2 * vectors), 1)
                if (turn + vectors) % (2 * vectors)
                else imag,
            )
            value = jnp.where(own_half, -value, crossed[first * side : (first + 1) * side, :])
            pair = first * vectors - first * (first + 1) // 2 + side - first - 1
            ordered[pair : pair + side, :] = value
    for first in range(vectors):
        skip = first % side + 1
        if skip < side:
            pair = first * vectors - first * (first + 1) // 2
            ordered[pair : pair + side - skip, :] = grid[
                first * side + skip : (first + 1) * side, :
            ]


def last_pairs_kernel(
    tiles, chunk, factor, slot_ref, place_ref, top_links, low_links, far, partial, own, before,
    keep, send, sums, field, low, quarks, grid, crossed, ordered, both,
):
    outer_pairs_kernel(
        tiles, chunk, place_ref, top_links, low_links, far, partial, own, before, sums, field, low,
        quarks,
    )
    arrange(sums, grid, crossed, ordered, factor)
    both[...] = jnp.zeros_like(both)

    def place(block, carry):
        slot = slot_ref[block]
        owner = slot // CAP
        other = jnp.bitwise_xor(owner % 2, place_ref[1])
        away = jnp.bitwise_xor(owner // 2, place_ref[0])
        both[other, away, slot % CAP] = ordered[pl.ds(pl.multiple_of(block * PB, PB), PB), :]
        return carry

    lax.fori_loop(0, slot_ref.shape[0], place, 0, unroll=7 if slot_ref.shape[0] % 7 == 0 else 1)
    keep[...] = both[0]
    send[...] = both[1]


def combine_kernel(kept, received, far_sent, far_kept, *near):
    for away, out in enumerate(near):
        out[...] = kept[away] + received[away]
    for index in range(far_sent.shape[0]):
        away = len(near) + 2 * index
        far_kept[index] = kept[away] + received[away]
        far_sent[index] = kept[away + 1] + received[away + 1]


def far_kernel(kept, received, *outs):
    for index, out in enumerate(outs):
        out[...] = kept[index] + received[index]


def total_kernel(*refs):
    total = refs[0][...]
    for ref in refs[1:-1]:
        total = total + ref[...]
    refs[-1][...] = total


def on_device(eigen_vectors, link_field, block_slot):
    count = lax.axis_size("brick")
    vectors, sites = eigen_vectors.shape[0], eigen_vectors.shape[-1]
    planes = eigen_vectors.shape[-2]
    tiles = sites // LANES
    half_tiles = tiles // 2
    chunk_tiles = ((0, half_tiles), (half_tiles, tiles - half_tiles))

    def plane_of(width):
        return jax.ShapeDtypeStruct((6, vectors, width), jnp.float32)

    plane = plane_of(sites)
    pieces = [plane_of(size * LANES) for _, size in chunk_tiles]
    plane_bytes = 6 * vectors * sites * 4
    pair_rows = len(pair_tiles(vectors)) * ROWS * ROWS
    up = [(i, (i + 1) % count) for i in range(count)]
    on_chip = [(i, i ^ 1) for i in range(count)]
    off_chip = [(i, (i + 2 * (i % 2) - 1) % count) for i in range(count)]
    me = lax.axis_index("brick")
    place = jnp.stack([me // 2, me % 2]).astype(jnp.int32)
    z_links = jax.ShapeDtypeStruct((18 * tiles, LANES), jnp.float32)

    def call(kernel, shapes, name, smem, *args, limit=32, flops=0, scratch=()):
        many = isinstance(shapes, list)
        return pl.pallas_call(
            kernel,
            out_shape=shapes,
            in_specs=[SMEM] * smem + [VMEM] * (len(args) - smem),
            out_specs=[VMEM] * len(shapes) if many else VMEM,
            scratch_shapes=list(scratch),
            compiler_params=params(limit),
            cost_estimate=cost(flops, 2 * plane_bytes) if flops else None,
            name=name,
        )(*args)

    rows = tile_rows(eigen_vectors)
    outer = call(
        functools.partial(outer_kernel, tiles, chunk_tiles), pieces, "outer", 1, place, rows
    )
    with_links = jax.ShapeDtypeStruct((6, vectors + ROWS, sites), jnp.float32)
    inner, plane_links, cross_links, top_links = call(
        functools.partial(inner_kernel, tiles, vectors),
        [with_links, jax.ShapeDtypeStruct((72 * tiles, LANES), jnp.float32), z_links, z_links],
        "inner", 1, place, rows, tile_rows(link_field), outer[-1],
    )

    def off(fields):
        return [lax.ppermute(field, "brick", off_chip) for field in fields]

    far = off(outer)
    linked = lax.ppermute(inner, "brick", on_chip)
    low_links = lax.ppermute(top_links, "brick", up)
    inner_sums, outer_sums = call(
        functools.partial(local_kernel, tiles, chunk_tiles, (0, 1)), [plane] * 2, "local", 0,
        plane_links, cross_links, inner, *outer, limit=48, flops=4e9,
    )
    first_inner, inner_sums = call(
        functools.partial(inner_step_kernel, tiles), [plane] * 2, "inner_step", 1,
        place, top_links, plane_links, linked, inner_sums,
    )
    token = sum(field[0, :ROWS, :LANES] for field in [inner_sums, *far])
    token = lax.ppermute(token, "brick", [(i, i ^ 1) for i in range(count) if i % 4 in (1, 2)])
    first_outer = []
    for chunk, piece, field in zip(chunk_tiles, pieces, far):
        args = (place, top_links, low_links, field, outer_sums, token)
        if first_outer:
            first_outer.append(
                call(functools.partial(edge_kernel, tiles, chunk), piece, "edge", 1, *args)
            )
            continue
        first, first_inner = pl.pallas_call(
            functools.partial(edge_kernel, tiles, chunk),
            out_shape=[piece, plane],
            in_specs=[SMEM] + [VMEM] * 5 + [pl.BlockSpec(memory_space=pl.ANY)],
            out_specs=[VMEM, pl.BlockSpec(memory_space=pl.ANY)],
            input_output_aliases={6: 1},
            compiler_params=params(32),
            name="edge",
        )(*args, first_inner)
        first_outer.append(first)
    partner = lax.ppermute(first_inner, "brick", on_chip)
    far = off(first_outer)
    def scratch(width):
        return [
            pltpu.VMEM((2 * vectors, 6 * width), jnp.bfloat16),
            pltpu.VMEM((pair_rows, 6 * width), jnp.bfloat16),
        ]

    partial_sums = jax.ShapeDtypeStruct((pair_rows, 2 * vectors), jnp.float32)
    before = call(
        functools.partial(inner_pairs_kernel, tiles, chunk_tiles), partial_sums, "inner_pairs", 1,
        place, top_links, cross_links, linked, partner, inner_sums, inner, *first_outer, limit=48, flops=8e9,
        scratch=[pltpu.VMEM(plane.shape, jnp.float32)] + scratch(2 * LANES),
    )
    (sums,) = call(
        functools.partial(local_kernel, tiles, chunk_tiles, (1,)), [plane], "outer_hop", 0,
        plane_links, cross_links, first_inner, *first_outer, before, limit=48, flops=2e9,
    )
    for chunk, piece, field, own in zip(chunk_tiles[:-1], pieces, far, outer):
        before = pl.pallas_call(
            functools.partial(outer_pairs_kernel, tiles, chunk),
            out_shape=partial_sums,
            in_specs=[SMEM] + [VMEM] * 6,
            out_specs=VMEM,
            scratch_shapes=[pltpu.VMEM(piece.shape, jnp.float32)] + scratch(piece.shape[2]),
            compiler_params=params(48),
            cost_estimate=cost(4e9, 3 * plane_bytes),
            name="outer_pairs",
        )(place, top_links, low_links, field, sums, own, before)
    factor = 1.0 / math.sqrt(3.0 * sites * planes * count)
    chips = count // 2
    half = jax.ShapeDtypeStruct((chips, CAP, PB, 2 * vectors), jnp.float32)
    blocks = vectors * (vectors - 1) // 2
    keep, send = pl.pallas_call(
        functools.partial(last_pairs_kernel, tiles, chunk_tiles[-1], factor),
        out_shape=[half] * 2,
        in_specs=[SMEM] * 2 + [VMEM] * 6,
        out_specs=[VMEM] * 2,
        scratch_shapes=[
            pltpu.VMEM(partial_sums.shape, jnp.float32),
            pltpu.VMEM(pieces[-1].shape, jnp.float32),
        ]
        + scratch(pieces[-1].shape[2])
        + [
            pltpu.VMEM((vectors * vectors // 2, 2 * vectors), jnp.float32),
            pltpu.VMEM((vectors * vectors // 4, 2 * vectors), jnp.float32),
            pltpu.VMEM((blocks, 2 * vectors), jnp.float32),
            pltpu.VMEM((2,) + half.shape, jnp.float32),
        ],
        compiler_params=params(48),
        cost_estimate=cost(4e9, 3 * plane_bytes),
        name="last_pairs",
    )(block_slot, place, top_links, low_links, far[-1], sums, outer[-1], before)
    received = lax.ppermute(send, "brick", on_chip)
    share = jax.ShapeDtypeStruct((CAP, PB, 2 * vectors), jnp.float32)
    near = chips // 2
    stack = jax.ShapeDtypeStruct((near // 2, CAP, PB, 2 * vectors), jnp.float32)
    far_sent, far_kept, *shares = call(
        combine_kernel, [stack] * 2 + [share] * near, "combine", 0, keep, received
    )

    def to_chip(array, away):
        return lax.ppermute(array, "brick", [(i, i ^ (2 * away)) for i in range(count)])

    far_received = to_chip(far_sent, 1)
    far_shares = call(far_kernel, [share] * (near // 2), "far", 0, far_kept, far_received)
    arrived = [to_chip(shares[away], away) for away in range(1, near)]
    arrived += [
        to_chip(far_shares[index], near + 2 * index) for index in range(near // 2)
    ]
    return call(total_kernel, share, "total", 0, shares[0], *arrived)


def solution(mesh):
    return jax.shard_map(
        on_device,
        mesh=mesh,
        in_specs=(
            P(None, None, None, ("cuts", "brick"), None),
            P(None, None, None, None, ("cuts", "brick"), None),
            P(),
        ),
        out_specs=P(("cuts", "brick"), None, None),
        check_vma=False,
    )
```
